32 devices in a mesh: dp: 8 (over z, y), tensor: 4 (over x, core).
Axes of the slice: x: 2, y: 2, z: 4, core: 2. Of those that a mesh axis runs over, the one named last changes fastest.
Arguments:
- inputs: bfloat16 [16384, 1024], P('dp'), may hold values from -6 to 6
- cotangent: bfloat16 [16384, 1024], P('dp', 'tensor'), may hold values from -12 to 12
- doc_lengths: int32 [8, 3], P('dp'), may hold values from 200 to 2000, as said below
- weight_qk: float32 [2, 1024, 512], P(None, 'dp', 'tensor'), may hold values from -0.1875 to 0.1875
- weight_vg: float32 [2, 1024, 1024], P(None, 'dp', 'tensor'), may hold values from -0.1875 to 0.1875
- weight_lowin: float32 [1024, 16], P('dp'), may hold values from -0.1875 to 0.1875
- weight_lowout: float32 [16, 4, 128], P(None, 'tensor', 'dp'), may hold values from -1.5 to 1.5
- weight_mixout: float32 [1024, 1024], P('tensor', 'dp'), may hold values from -0.1875 to 0.1875
- weight_gateup: float32 [2, 1024, 2816], P(None, 'dp', 'tensor'), may hold values from -0.1875 to 0.1875
- weight_down: float32 [2816, 1024], P('tensor', 'dp'), may hold values from -0.109375 to 0.109375
- weight_small: float32 [2816], replicated, may hold values from 0 to 6
- first_qk: float32 [2, 1024, 512], P(None, 'dp', 'tensor'), may hold values from -0.00048828125 to 0.00048828125
- first_vg: float32 [2, 1024, 1024], P(None, 'dp', 'tensor'), may hold values from -0.00048828125 to 0.00048828125
- first_lowin: float32 [1024, 16], P('dp'), may hold values from -0.00048828125 to 0.00048828125
- first_lowout: float32 [16, 4, 128], P(None, 'tensor', 'dp'), may hold values from -0.00048828125 to 0.00048828125
- first_mixout: float32 [1024, 1024], P('tensor', 'dp'), may hold values from -0.00048828125 to 0.00048828125
- first_gateup: float32 [2, 1024, 2816], P(None, 'dp', 'tensor'), may hold values from -0.00048828125 to 0.00048828125
- first_down: float32 [2816, 1024], P('tensor', 'dp'), may hold values from -0.00048828125 to 0.00048828125
- first_small: float32 [2816], replicated, may hold values from -0.00048828125 to 0.00048828125
- second_qk: float32 [2, 1024, 512], P(None, 'dp', 'tensor'), may hold values from 4.086247e-09 to 1.6313914e-08
- second_vg: float32 [2, 1024, 1024], P(None, 'dp', 'tensor'), may hold values from 4.086247e-09 to 1.6313914e-08
- second_lowin: float32 [1024, 16], P('dp'), may hold values from 4.086247e-09 to 1.6313914e-08
- second_lowout: float32 [16, 4, 128], P(None, 'tensor', 'dp'), may hold values from 4.086247e-09 to 1.6313914e-08
- second_mixout: float32 [1024, 1024], P('tensor', 'dp'), may hold values from 4.086247e-09 to 1.6313914e-08
- second_gateup: float32 [2, 1024, 2816], P(None, 'dp', 'tensor'), may hold values from 4.086247e-09 to 1.6313914e-08
- second_down: float32 [2816, 1024], P('tensor', 'dp'), may hold values from 4.086247e-09 to 1.6313914e-08
- second_small: float32 [2816], replicated, may hold values from 4.086247e-09 to 1.6313914e-08
Outputs:
- output: bfloat16 [16384, 1024], P('dp', 'tensor')
- input_grad: float32 [16384, 1024], P('dp', 'tensor')
- grad_norm: float32 [1], replicated
- momentum_qk: float32 [2, 1024, 512], P(None, 'dp', 'tensor')
- momentum_vg: float32 [2, 1024, 1024], P(None, 'dp', 'tensor')
- momentum_lowin: float32 [1024, 16], P('dp')
- momentum_lowout: float32 [16, 4, 128], P(None, 'tensor', 'dp')
- momentum_mixout: float32 [1024, 1024], P('tensor', 'dp')
- momentum_gateup: float32 [2, 1024, 2816], P(None, 'dp', 'tensor')
- momentum_down: float32 [2816, 1024], P('tensor', 'dp')
- momentum_small: float32 [2816], replicated
- variance_qk: float32 [2, 1024, 512], P(None, 'dp', 'tensor')
- variance_vg: float32 [2, 1024, 1024], P(None, 'dp', 'tensor')
- variance_lowin: float32 [1024, 16], P('dp')
- variance_lowout: float32 [16, 4, 128], P(None, 'tensor', 'dp')
- variance_mixout: float32 [1024, 1024], P('tensor', 'dp')
- variance_gateup: float32 [2, 1024, 2816], P(None, 'dp', 'tensor')
- variance_down: float32 [2816, 1024], P('tensor', 'dp')
- variance_small: float32 [2816], replicated
- updated_qk: float32 [2, 1024, 512], P(None, 'dp', 'tensor')
- updated_vg: float32 [2, 1024, 1024], P(None, 'dp', 'tensor')
- updated_lowin: float32 [1024, 16], P('dp')
- updated_lowout: float32 [16, 4, 128], P(None, 'tensor', 'dp')
- updated_mixout: float32 [1024, 1024], P('tensor', 'dp')
- updated_gateup: float32 [2, 1024, 2816], P(None, 'dp', 'tensor')
- updated_down: float32 [2816, 1024], P('tensor', 'dp')
- updated_small: float32 [2816], replicated
The draws below stay inside these ranges and needn't reach their ends.
Inputs may be any that keep to these rules, and one draw needn't show every extreme that they name: `doc_lengths`: documents of a sequence are packed in order from its first token; tokens after them are padding, and a document that runs past 2048 tokens is cut there. Some sequence holds a document of 2000 tokens and one of 200.
All inputs are finite; a program needn't handle non-finite values.
Results may differ from the reference program's by a relative error of at most 0.029.
Values may be sent and summed in bfloat16 or wider, within the bound.
No kernel may reach another device: no remote copies, remote signals or barrier semaphores. Data moves between devices by JAX's collectives and lax.ppermute only.
A program may use at most 192 MiB of HBM per device.

```python
import math
import jax
import jax.numpy as jnp
from jax import lax

D = 1024
HEADS = 4
DK = 128
DV = 256
RANK = 16
FF = 2816
SPAN = 64
SEQ_LEN = 2048
DOCS = 3
DOC_MIN = 200
DOC_MAX = 2000
STEP = 10
TOK_DEV = 2048
SEQS = 8
TOKENS = 16384
SMALL = 2816
PARAMS = 12872448
N_DP = 8
N_TENSOR = 4


def draw_cotangent(key, part):
    columns = lax.broadcasted_iota(jnp.float32, (TOKENS, D), 1) / D
    base_draw = jnp.clip(jax.random.normal(key, (TOKENS, D), jnp.float32), -4.0, 4.0)
    return (base_draw * (1.0 + 2.0 * columns)).astype(jnp.bfloat16)


def draw_doc_lengths(key, part):
    key_first = jax.random.fold_in(key, 11)
    key_second = jax.random.fold_in(key, 12)
    key_chosen = jax.random.fold_in(key, 13)
    pick_top = 16
    first_pick = jax.random.randint(key_first, (SEQS, DOCS), 0, pick_top + 1)
    second_pick = jax.random.randint(key_second, (SEQS, DOCS), 0, pick_top + 1)
    spread = DOC_MAX - DOC_MIN
    lengths = DOC_MIN + spread * first_pick * second_pick // (pick_top * pick_top)
    chosen = jax.random.randint(key_chosen, (), 0, SEQS)
    row_index = lax.broadcasted_iota(jnp.int32, (SEQS, DOCS), 0)
    col_index = lax.broadcasted_iota(jnp.int32, (SEQS, DOCS), 1)
    lengths = jnp.where((row_index == chosen) & (col_index == 0), DOC_MAX, lengths)
    lengths = jnp.where((row_index == chosen) & (col_index == 1), DOC_MIN, lengths)
    return lengths.astype(jnp.int32)


def draw_weight_small(key, part):
    key_gain = jax.random.fold_in(key, 21)
    key_head = jax.random.fold_in(key, 22)
    key_bias = jax.random.fold_in(key, 23)
    position = lax.broadcasted_iota(jnp.float32, (2, D), 1) / D
    rise_factor = 1.0 + 2.0 * position
    jitter = jax.random.uniform(key_gain, (2, D), jnp.float32, 0.85, 1.15)
    head_gain = jax.random.uniform(key_head, (DV,), jnp.float32, 0.5, 1.5)
    bias_draw = jax.random.uniform(key_bias, (HEADS * DK,), jnp.float32, 0.0, 5.0)
    return jnp.concatenate([(rise_factor * jitter).reshape(-1), head_gain, bias_draw])


def shard_levels(own_key, dims, cuts, smallest, high):
    factor_of = 1.0
    for dim, parts in cuts:
        steps = jax.random.uniform(jax.random.fold_in(jax.random.fold_in(own_key, 6), dim), (parts,), jnp.float32, smallest / len(cuts), high / len(cuts))
        factor_of = factor_of * jnp.repeat(jnp.exp(steps), dims[dim] // parts).reshape((-1,) + (1,) * (len(dims) - 1 - dim))
    return factor_of


def scatter_about(own_key, dims, width, most, shards=(), held_as=jnp.bfloat16):
    values = width * jax.random.normal(own_key, dims, jnp.float32)
    if shards:
        values = values * shard_levels(own_key, dims, shards, -0.22, 0.18)
    return jnp.clip(values, -most, most).astype(held_as)


def setup_inputs(seed: int = 0) -> dict:
    streams_of = jax.random.split(jax.random.key(seed), 28)
    inputs = scatter_about(streams_of[0], (TOKENS, D), 1.0, 6.0, ((0, 8),))
    cotangent = draw_cotangent(jax.random.fold_in(streams_of[27], 71), 0)
    doc_lengths = draw_doc_lengths(jax.random.fold_in(streams_of[27], 71), 0)
    weight_qk = scatter_about(streams_of[3], (2, D, HEADS * DK), D ** -0.5, 0.1875, ((1, 8), (2, 4)), jnp.float32)
    weight_vg = scatter_about(streams_of[4], (2, D, HEADS * DV), D ** -0.5, 0.1875, ((1, 8), (2, 4)), jnp.float32)
    weight_lowin = scatter_about(streams_of[5], (D, RANK), D ** -0.5, 0.1875, ((0, 8),), jnp.float32)
    weight_lowout = scatter_about(streams_of[6], (RANK, HEADS, DK), RANK ** -0.5, 1.5, ((1, 4), (2, 8)), jnp.float32)
    weight_mixout = scatter_about(streams_of[7], (HEADS * DV, D), (HEADS * DV) ** -0.5, 0.1875, ((0, 4), (1, 8)), jnp.float32)
    weight_gateup = scatter_about(streams_of[8], (2, D, FF), D ** -0.5, 0.1875, ((1, 8), (2, 4)), jnp.float32)
    weight_down = scatter_about(streams_of[9], (FF, D), FF ** -0.5, 0.109375, ((0, 4), (1, 8)), jnp.float32)
    weight_small = draw_weight_small(jax.random.fold_in(streams_of[27], 71), 0)
    first_qk = scatter_about(streams_of[11], (2, D, HEADS * DK), (0.111 / PARAMS ** 0.5), 0.00048828125, ((1, 8), (2, 4)), jnp.float32)
    first_vg = scatter_about(streams_of[12], (2, D, HEADS * DV), (0.111 / PARAMS ** 0.5), 0.00048828125, ((1, 8), (2, 4)), jnp.float32)
    first_lowin = scatter_about(streams_of[13], (D, RANK), (0.111 / PARAMS ** 0.5), 0.00048828125, ((0, 8),), jnp.float32)
    first_lowout = scatter_about(streams_of[14], (RANK, HEADS, DK), (0.111 / PARAMS ** 0.5), 0.00048828125, ((1, 4), (2, 8)), jnp.float32)
    first_mixout = scatter_about(streams_of[15], (HEADS * DV, D), (0.111 / PARAMS ** 0.5), 0.00048828125, ((0, 4), (1, 8)), jnp.float32)
    first_gateup = scatter_about(streams_of[16], (2, D, FF), (0.111 / PARAMS ** 0.5), 0.00048828125, ((1, 8), (2, 4)), jnp.float32)
    first_down = scatter_about(streams_of[17], (FF, D), (0.111 / PARAMS ** 0.5), 0.00048828125, ((0, 4), (1, 8)), jnp.float32)
    first_small = scatter_about(streams_of[18], (SMALL,), (0.111 / PARAMS ** 0.5), 0.00048828125, (), jnp.float32)
    second_qk = jnp.clip(jnp.exp(math.log(1.631391377543423e-08) - 1.3843914 * jax.random.uniform(streams_of[19], (2, D, HEADS * DK), jnp.float32) ** shard_levels(streams_of[19], (2, D, HEADS * DK), ((1, 8), (2, 4)), -0.2, 0.2)), 4.086246896406465e-09, 1.631391377543423e-08)
    second_vg = jnp.clip(jnp.exp(math.log(1.631391377543423e-08) - 1.3843914 * jax.random.uniform(streams_of[20], (2, D, HEADS * DV), jnp.float32) ** shard_levels(streams_of[20], (2, D, HEADS * DV), ((1, 8), (2, 4)), -0.2, 0.2)), 4.086246896406465e-09, 1.631391377543423e-08)
    second_lowin = jnp.clip(jnp.exp(math.log(1.631391377543423e-08) - 1.3843914 * jax.random.uniform(streams_of[21], (D, RANK), jnp.float32) ** shard_levels(streams_of[21], (D, RANK), ((0, 8),), -0.2, 0.2)), 4.086246896406465e-09, 1.631391377543423e-08)
    second_lowout = jnp.clip(jnp.exp(math.log(1.631391377543423e-08) - 1.3843914 * jax.random.uniform(streams_of[22], (RANK, HEADS, DK), jnp.float32) ** shard_levels(streams_of[22], (RANK, HEADS, DK), ((1, 4), (2, 8)), -0.2, 0.2)), 4.086246896406465e-09, 1.631391377543423e-08)
    second_mixout = jnp.clip(jnp.exp(math.log(1.631391377543423e-08) - 1.3843914 * jax.random.uniform(streams_of[23], (HEADS * DV, D), jnp.float32) ** shard_levels(streams_of[23], (HEADS * DV, D), ((0, 4), (1, 8)), -0.2, 0.2)), 4.086246896406465e-09, 1.631391377543423e-08)
    second_gateup = jnp.clip(jnp.exp(math.log(1.631391377543423e-08) - 1.3843914 * jax.random.uniform(streams_of[24], (2, D, FF), jnp.float32) ** shard_levels(streams_of[24], (2, D, FF), ((1, 8), (2, 4)), -0.2, 0.2)), 4.086246896406465e-09, 1.631391377543423e-08)
    second_down = jnp.clip(jnp.exp(math.log(1.631391377543423e-08) - 1.3843914 * jax.random.uniform(streams_of[25], (FF, D), jnp.float32) ** shard_levels(streams_of[25], (FF, D), ((0, 4), (1, 8)), -0.2, 0.2)), 4.086246896406465e-09, 1.631391377543423e-08)
    second_small = jnp.clip(jnp.exp(jax.random.uniform(streams_of[26], (SMALL,), jnp.float32, math.log(4.086246896406465e-09), math.log(1.631391377543423e-08))), 4.086246896406465e-09, 1.631391377543423e-08)
    return {"inputs": inputs, "cotangent": cotangent, "doc_lengths": doc_lengths, "weight_qk": weight_qk, "weight_vg": weight_vg, "weight_lowin": weight_lowin, "weight_lowout": weight_lowout, "weight_mixout": weight_mixout, "weight_gateup": weight_gateup, "weight_down": weight_down, "weight_small": weight_small, "first_qk": first_qk, "first_vg": first_vg, "first_lowin": first_lowin, "first_lowout": first_lowout, "first_mixout": first_mixout, "first_gateup": first_gateup, "first_down": first_down, "first_small": first_small, "second_qk": second_qk, "second_vg": second_vg, "second_lowin": second_lowin, "second_lowout": second_lowout, "second_mixout": second_mixout, "second_gateup": second_gateup, "second_down": second_down, "second_small": second_small}


@jax.custom_vjp
def low(v):
    return lax.optimization_barrier(v.astype(jnp.bfloat16)).astype(jnp.float32)

@jax.custom_vjp
def low_back(v):
    return v

def low_keep(v):
    return (low(v), None)

def low_pass(kept, grad):
    return (grad,)

def back_keep(v):
    return (v, None)

def back_low(kept, grad):
    return (low(grad),)
low.defvjp(low_keep, low_pass)
low_back.defvjp(back_keep, back_low)
NORM_EPS = 1e-06
GATE_NORM = 16.0
BETA_FIRST = 0.9
BETA_SECOND = 0.95
ADAM_EPS = 1e-08
WEIGHT_DECAY = 0.1
CLIP_NORM = 1.0
GAIN_RATE = 2.5
BIAS_RATE = 4.0

def rms_scale(values):
    return lax.rsqrt(lax.optimization_barrier(jnp.mean(values * values, axis=-1, keepdims=True)) + NORM_EPS)

def layout(doc_lengths, seq_len):
    seq_count = doc_lengths.shape[0]
    doc_count = doc_lengths.shape[1]
    doc_ends = jnp.cumsum(doc_lengths, axis=1).astype(jnp.int32)
    where_at = lax.broadcasted_iota(jnp.int32, (seq_count, seq_len, doc_count), 1)
    doc_number = lax.optimization_barrier(jnp.sum((where_at >= doc_ends[:, None, :]).astype(jnp.int32), axis=2)).astype(jnp.int32)
    valid_mask = (doc_number < doc_count).astype(jnp.float32)
    offset = lax.broadcasted_iota(jnp.int32, (seq_count, seq_len), 0) * (doc_count + 1)
    return ((doc_number + offset).reshape(-1), valid_mask.reshape(-1))

def mixer_block(carry, pieces):
    running_state, last_segment = carry
    query_tile_rows, key_block, value_tile_rows, forget_block, segment_block = pieces
    largest_exponent = lax.Precision.HIGHEST
    block_len = query_tile_rows.shape[0]
    decay_prefix_sum = jnp.cumsum(forget_block, axis=0)
    mid_point = decay_prefix_sum[block_len // 2]
    alive_mask = (segment_block == last_segment).astype(jnp.float32)
    state_contribution = jnp.einsum('dqi,qis->dqs', query_tile_rows * jnp.exp(decay_prefix_sum), running_state, precision=largest_exponent)
    state_contribution = state_contribution * alive_mask[:, None, None]
    query_rel = query_tile_rows * jnp.exp(decay_prefix_sum - mid_point[None])
    key_rel = key_block * jnp.exp(mid_point[None] - decay_prefix_sum)
    scores = jnp.einsum('ihk,jhk->hij', query_rel, key_rel, precision=largest_exponent)
    row_index = lax.broadcasted_iota(jnp.int32, (block_len, block_len), 0)
    col_index = lax.broadcasted_iota(jnp.int32, (block_len, block_len), 1)
    allowed = (col_index <= row_index) & (segment_block[:, None] == segment_block[None, :])
    scores = jnp.where(allowed[None, :, :], scores, jnp.zeros_like(scores))
    in_block = jnp.einsum('hij,jhv->ihv', scores, value_tile_rows, precision=largest_exponent)
    block_out = (state_contribution + in_block) * query_tile_rows.shape[2] ** (-0.5)
    last_decay = decay_prefix_sum[block_len - 1]
    end_segment = segment_block[block_len - 1]
    keep_mask = (segment_block == end_segment).astype(jnp.float32)
    damped_key_rows = key_block * jnp.exp(last_decay[None] - decay_prefix_sum) * keep_mask[:, None, None]
    state_passed_forward = running_state * jnp.exp(last_decay)[:, :, None] * (end_segment == last_segment).astype(jnp.float32)
    next_state = state_passed_forward + jnp.einsum('yrm,yrd->rmd', damped_key_rows, value_tile_rows, precision=largest_exponent)
    return ((next_state, end_segment), block_out)

def gated_mixer(queries, key_rows, value_rows, forget, segment):
    tokens_here = queries.shape[0]
    heads_here = queries.shape[1]
    blocks = tokens_here // SPAN

    def to_blocks(array):
        return array.reshape((blocks, SPAN) + array.shape[1:])
    initial = (jnp.zeros((heads_here, queries.shape[2], value_rows.shape[2]), jnp.float32), jnp.full((), -1, jnp.int32))
    pieces = (to_blocks(queries), to_blocks(key_rows), to_blocks(value_rows), to_blocks(forget), to_blocks(segment))
    finished, outputs = lax.scan(jax.checkpoint(mixer_block), initial, pieces)
    return outputs.reshape(tokens_here, heads_here, value_rows.shape[2])

def block_forward(weights, small_params, inputs, segment, valid_mask):
    largest_exponent = lax.Precision.HIGHEST
    rounded = tuple((low(weight) for weight in weights))
    proj_qk, proj_vg, rank_in, rank_out, mix_out, gate_up, down_proj = rounded
    tokens_here = inputs.shape[0]
    feature_width = inputs.shape[1]
    gain_in = small_params[:feature_width]
    gain_mid = small_params[feature_width:2 * feature_width]
    gain_head = small_params[2 * feature_width:2 * feature_width + DV]
    gate_bias = small_params[2 * feature_width + DV:]
    normed = low(inputs * rms_scale(inputs) * gain_in)
    queries = low(low_back(jnp.dot(normed, proj_qk[0], precision=largest_exponent)))
    key_rows = low(low_back(jnp.dot(normed, proj_qk[1], precision=largest_exponent)))
    value_rows = low(low_back(jnp.dot(normed, proj_vg[0], precision=largest_exponent)))
    out_gate = low_back(jnp.dot(normed, proj_vg[1], precision=largest_exponent))
    lowrank = low(low_back(jnp.dot(normed, rank_in, precision=largest_exponent)))
    logits = low_back(jnp.dot(lowrank, rank_out.reshape(RANK, HEADS * DK), precision=largest_exponent) + gate_bias)
    forget = jax.nn.log_sigmoid(logits) / GATE_NORM
    mixer_out = gated_mixer(queries.reshape(tokens_here, HEADS, DK), key_rows.reshape(tokens_here, HEADS, DK), value_rows.reshape(tokens_here, HEADS, DV), forget.reshape(tokens_here, HEADS, DK), segment)
    gate_act = jax.nn.silu(out_gate.reshape(tokens_here, HEADS, DV))
    headed = mixer_out * rms_scale(mixer_out) * gain_head * gate_act * valid_mask[:, None, None]
    headed = low(headed.reshape(tokens_here, HEADS * DV))
    group_width = HEADS * DV // N_TENSOR
    attended = jnp.zeros((tokens_here, feature_width), jnp.float32)
    for block_index in range(N_TENSOR):
        lower = block_index * group_width
        upper = lower + group_width
        attended = attended + low(jnp.dot(headed[:, lower:upper], mix_out[lower:upper], precision=largest_exponent))
    attended = low_back(attended)
    residual = inputs + attended
    normed_mid = low(residual * rms_scale(residual) * gain_mid)
    unit_width = FF // N_TENSOR
    feed_out = jnp.zeros((tokens_here, feature_width), jnp.float32)
    for block_index in range(N_TENSOR):
        lower = block_index * unit_width
        upper = lower + unit_width
        local_in = low_back(normed_mid)
        gate_pre = low_back(jnp.dot(local_in, gate_up[0][:, lower:upper], precision=largest_exponent))
        up_pre = low_back(jnp.dot(local_in, gate_up[1][:, lower:upper], precision=largest_exponent))
        hidden = low(jax.nn.silu(gate_pre) * up_pre)
        feed_out = feed_out + jnp.dot(hidden, down_proj[lower:upper], precision=largest_exponent)
    return low(residual + feed_out)

def adam_step(weight, gradient, first_moment, second_moment, clip_factor, learn_rate, weight_decay):
    clipped = gradient * clip_factor
    momentum = BETA_FIRST * first_moment + (1.0 - BETA_FIRST) * clipped
    variance = BETA_SECOND * second_moment + (1.0 - BETA_SECOND) * clipped * clipped
    step_size = momentum / (1.0 - BETA_FIRST ** STEP) / (jnp.sqrt(variance / (1.0 - BETA_SECOND ** STEP)) + ADAM_EPS)
    updated = weight * (1.0 - learn_rate * weight_decay) - learn_rate * step_size
    return (momentum, variance, updated)

def reference(inputs, cotangent, doc_lengths, weight_qk, weight_vg, weight_lowin, weight_lowout, weight_mixout, weight_gateup, weight_down, weight_small, first_qk, first_vg, first_lowin, first_lowout, first_mixout, first_gateup, first_down, first_small, second_qk, second_vg, second_lowin, second_lowout, second_mixout, second_gateup, second_down, second_small):
    segment, valid_mask = layout(doc_lengths, SEQ_LEN)
    weights = (weight_qk, weight_vg, weight_lowin, weight_lowout, weight_mixout, weight_gateup, weight_down)
    stacked_in = inputs.astype(jnp.float32).reshape(N_DP, TOK_DEV, D)
    stacked_cot = cotangent.astype(jnp.float32).reshape(N_DP, TOK_DEV, D)

    def one_block(totals, pieces):
        block_in, block_cot, block_segment, block_valid = pieces

        def run_block(weights_now, small_now, inputs_now):
            return block_forward(weights_now, small_now, inputs_now, block_segment, block_valid)
        result, back_fn = jax.vjp(run_block, weights, weight_small, block_in)
        grad_weights, grad_small, grad_in = back_fn(block_cot)
        totals = jax.tree.map(lambda held, added: held + added, totals, (grad_weights, grad_small))
        return (totals, (result, grad_in))
    initial = (tuple((jnp.zeros_like(weight) for weight in weights)), jnp.zeros_like(weight_small))
    sums, stacked_out = lax.scan(one_block, initial, (stacked_in, stacked_cot, segment.reshape(N_DP, TOK_DEV), valid_mask.reshape(N_DP, TOK_DEV)))
    grad_weights, grad_small = sums
    results, grads_in = stacked_out
    squares = jnp.sum(grad_small * grad_small)
    for gradient in grad_weights:
        squares = squares + jnp.sum(gradient * gradient)
    grad_norm = jnp.sqrt(squares)
    clip_factor = jnp.minimum(1.0, CLIP_NORM / (grad_norm + 1e-06))
    rates = (2.0 * D ** (-0.5), 2.0 * D ** (-0.5), 2.0 * D ** (-0.5), 2.0 * RANK ** (-0.5), 2.0 * (HEADS * DV) ** (-0.5), 2.0 * D ** (-0.5), 2.0 * FF ** (-0.5))
    firsts = (first_qk, first_vg, first_lowin, first_lowout, first_mixout, first_gateup, first_down)
    seconds = (second_qk, second_vg, second_lowin, second_lowout, second_mixout, second_gateup, second_down)
    momenta = []
    variances = []
    renewed = []
    for index_now in range(7):
        momentum, variance, updated = adam_step(weights[index_now], grad_weights[index_now], firsts[index_now], seconds[index_now], clip_factor, rates[index_now], WEIGHT_DECAY)
        momenta.append(momentum)
        variances.append(variance)
        renewed.append(updated)
    small_rate = jnp.where(lax.broadcasted_iota(jnp.int32, weight_small.shape, 0) < 2 * D + DV, GAIN_RATE, BIAS_RATE)
    momentum, variance, updated = adam_step(weight_small, grad_small, first_small, second_small, clip_factor, small_rate, 0.0)
    momenta.append(momentum)
    variances.append(variance)
    renewed.append(updated)
    return (results.reshape(TOKENS, D).astype(jnp.bfloat16), grads_in.reshape(TOKENS, D), grad_norm.reshape(1), momenta[0], momenta[1], momenta[2], momenta[3], momenta[4], momenta[5], momenta[6], momenta[7], variances[0], variances[1], variances[2], variances[3], variances[4], variances[5], variances[6], variances[7], renewed[0], renewed[1], renewed[2], renewed[3], renewed[4], renewed[5], renewed[6], renewed[7])
```

```python
import functools

import jax
import jax.numpy as jnp
from jax import lax
from jax.experimental import pallas as pl
from jax.experimental.pallas import tpu as pltpu
from jax.sharding import PartitionSpec as P

D = 1024
HEADS = 4
DK = 128
DV = 256
RANK = 16
FF = 2816
SPAN = 64
SEQ_LEN = 2048
STEP = 10

NORM_EPS = 1e-06
GATE_NORM = 16.0
BETA_FIRST = 0.9
BETA_SECOND = 0.95
ADAM_EPS = 1e-08
WEIGHT_DECAY = 0.1
CLIP_NORM = 1.0
GAIN_RATE = 2.5
BIAS_RATE = 4.0

F32 = jnp.float32
BF16 = jnp.bfloat16
LANES = 128
SLAB = 256
SLABS = 4
CHUNK = 2 * SPAN
BLOCK = 256
PIECES = 2
ORDER = (0, 2, 1, 3)
MAIN = 768
ATTN = 896
OUT_SCALE = DK**-0.5
VMEM_LIMIT = 48 * 1024 * 1024


def nn(a, b):
    return lax.dot_general(a, b, (((1,), (0,)), ((), ())), preferred_element_type=F32)


def nt(a, b):
    return lax.dot_general(a, b, (((1,), (1,)), ((), ())), preferred_element_type=F32)


def tn(a, b):
    return lax.dot_general(a, b, (((0,), (0,)), ((), ())), preferred_element_type=F32)


def doc_at(position, ends):
    number = jnp.zeros_like(position)
    for end in ends:
        number = number + jnp.where(position >= end, 1, 0)
    return number


def log_sigmoid(values):
    return jnp.minimum(values, 0.0) - jnp.log1p(jnp.exp(-jnp.abs(values)))


def prefix_sums(values, triangle):
    high = values.astype(BF16)
    low = (values - high.astype(F32)).astype(BF16)
    width = values.shape[1]
    both = nn(triangle, jnp.concatenate([high, low], axis=1))
    return both[:, :width] + both[:, width:]


def chunk_terms(queries, keys, forget, base, ends):
    row = lax.broadcasted_iota(jnp.int32, (CHUNK, CHUNK), 0)
    col = lax.broadcasted_iota(jnp.int32, (CHUNK, CHUNK), 1)
    decay = prefix_sums(forget, jnp.where(col <= row, 1.0, 0.0).astype(BF16))
    seg_row = doc_at(row + base, ends)
    same = seg_row == doc_at(col + base, ends)
    upper = row >= SPAN
    near = same & (col <= row) & (upper == (col >= SPAN))
    far = same & upper & (col < SPAN)
    before = jnp.where(base > 0, doc_at(base - 1, ends), -1)
    final = doc_at(base + CHUNK - 1, ends)
    alive = jnp.where(seg_row == before, 1.0, 0.0)
    keep = jnp.where(seg_row == final, 1.0, 0.0)
    carry = jnp.where(before == final, 1.0, 0.0)
    mid = jnp.where(upper, decay[SPAN + SPAN // 2 :][:1], decay[SPAN // 2 :][:1])
    grow = jnp.exp(decay - mid)
    shrink = jnp.exp(mid - decay)
    edge = jnp.exp(-jnp.abs(decay - decay[SPAN - 1 : SPAN]))
    from_start = jnp.exp(decay) * alive
    last = decay[CHUNK - 1 : CHUNK]
    to_end = jnp.exp(last - decay) * keep
    step = jnp.exp(last) * carry
    q_near = (queries * grow).astype(BF16)
    k_near = (keys * shrink).astype(BF16)
    q_far = (queries * edge).astype(BF16)
    k_far = (keys * edge).astype(BF16)
    q_state = (queries * from_start).astype(BF16)
    k_state = (keys * to_end).astype(BF16)
    scores = jnp.where(near, nt(q_near, k_near), jnp.where(far, nt(q_far, k_far), 0.0)).astype(BF16)
    return (
        (row, col, near, far),
        (grow, shrink, edge, from_start, to_end, step),
        (q_near, k_near, q_far, k_far, q_state, k_state),
        scores,
    )


def slab_at(meta, j):
    return pl.ds(pl.multiple_of(meta[j] * SLAB, SLAB), SLAB)


def lanes_at(start):
    return pl.ds(pl.multiple_of(start, LANES), LANES)


def one_hot(rows, shift):
    row = lax.broadcasted_iota(jnp.int32, (rows, LANES), 0)
    col = lax.broadcasted_iota(jnp.int32, (rows, LANES), 1)
    return jnp.where(col - row == shift, 1.0, 0.0).astype(BF16)


def pack_kernel(qk_ref, vg_ref, lowin_ref, lowout_ref, mixout_ref, gateup_ref, down_ref, attn_ref, feed_ref):
    units = gateup_ref.shape[2]
    width = feed_ref.shape[1] // 3
    attn_ref[:, :DK] = qk_ref[0].astype(BF16)
    attn_ref[:, DK : 2 * DK] = qk_ref[1].astype(BF16)
    attn_ref[:, 2 * DK : 2 * DK + DV] = vg_ref[0].astype(BF16)
    attn_ref[:, 2 * DK + DV : MAIN] = vg_ref[1].astype(BF16)
    attn_ref[:, MAIN:ATTN] = nn(lowin_ref[...].astype(BF16), one_hot(RANK, 0)).astype(BF16)
    lowout = lowout_ref[...].astype(BF16)
    attn_ref[:RANK, MAIN:ATTN] += nn(lowout, one_hot(lowout.shape[1], RANK)).astype(BF16)
    attn_ref[:, ATTN:] = mixout_ref[...].T.astype(BF16)
    rows = feed_ref.shape[0]
    pad = jnp.zeros((rows, width - units), BF16)
    feed_ref[:, :units] = gateup_ref[0].astype(BF16)
    feed_ref[:, units:width] = pad
    feed_ref[:, width : width + units] = gateup_ref[1].astype(BF16)
    feed_ref[:, width + units : 2 * width] = pad
    feed_ref[:, 2 * width : 2 * width + units] = down_ref[...].T.astype(BF16)
    feed_ref[:, 2 * width + units :] = pad


def assemble_kernel(place, *refs):
    pieces = refs[: 2 * SLABS]
    w_ref, wo_ref, wb_ref = refs[2 * SLABS :]
    rows = pieces[0].shape[0]
    keys = DK // (2 * SLABS)
    wb_ref[...] = jnp.zeros_like(wb_ref)
    for i, piece in enumerate(pieces):
        block = place[i]
        at = pl.ds(pl.multiple_of(block * rows, rows), rows)
        w_ref[at, :] = piece[:, :ATTN]
        wo_ref[at, :] = piece[:, ATTN:]
        row = lax.broadcasted_iota(jnp.int32, (LANES, DK), 0)
        col = lax.broadcasted_iota(jnp.int32, (LANES, DK), 1)
        inside = (row >= RANK) & (row < RANK + keys)
        move = jnp.where(inside & (col - row == block * keys - RANK), 1.0, 0.0).astype(BF16)
        wb_ref[:RANK, :] += nn(piece[:RANK, MAIN:ATTN], move).astype(BF16)


def attend_kernel(first_block, n_saved, meta, *refs):
    x_ref, w_ref, wo_ref, wb_ref, g1_ref, go_ref, c_ref, state_ref = refs[:8]
    refs = refs[8 + n_saved :]
    part_ref, state_out_ref = refs[:2]
    xn_ref, qkv_ref, gout_ref, lowr_ref, zeta_ref, mixed_ref, z_ref, states_ref = refs[2:]
    step = pl.program_id(0)

    @pl.when(step == 0)
    def _():
        state_out_ref[...] = state_ref[...]

    ends = [meta[SLABS + i] for i in range(meta.shape[0] - SLABS)]
    x = x_ref[...].astype(F32)
    scale = lax.rsqrt(jnp.mean(x * x, axis=-1, keepdims=True) + NORM_EPS)
    normed = (x * scale * g1_ref[...]).astype(BF16)
    xn_ref[...] = normed
    proj = nn(normed, w_ref[...])
    qkv = proj[:, : 2 * DK + DV].astype(BF16)
    qkv_ref[...] = qkv
    gout = proj[:, 2 * DK + DV : MAIN]
    gout_ref[...] = gout
    lowr = proj[:, MAIN:].astype(BF16)
    lowr_ref[...] = lowr
    zeta = nn(lowr, wb_ref[...]) + c_ref[...]
    zeta_ref[...] = zeta
    forget = log_sigmoid(zeta) * (1.0 / GATE_NORM)
    base = (first_block + step) * BLOCK
    state = state_out_ref[...]
    for i in range(BLOCK // CHUNK):
        rows = slice(i * CHUNK, (i + 1) * CHUNK)
        queries = qkv[rows, :DK].astype(F32)
        keys = qkv[rows, DK : 2 * DK].astype(F32)
        values = qkv[rows, 2 * DK :]
        start = base + i * CHUNK
        _, factors, terms, scores = chunk_terms(queries, keys, forget[rows], start, ends)
        q_state, k_state = terms[4:]
        state_low = state.astype(BF16)
        states_ref[i * DV : (i + 1) * DV, :] = state_low
        mixed = (nn(scores, values) + nt(q_state, state_low)) * OUT_SCALE
        mixed_ref[rows, :] = mixed
        state = state * factors[5] + tn(values, k_state)
        where = lax.broadcasted_iota(jnp.int32, (CHUNK, DV), 0) + start
        valid = jnp.where(where < ends[-1], 1.0, 0.0)
        head_scale = lax.rsqrt(jnp.mean(mixed * mixed, axis=-1, keepdims=True) + NORM_EPS)
        gate = gout[rows]
        z = mixed * head_scale * go_ref[...] * (gate * jax.nn.sigmoid(gate)) * valid
        z_ref[rows, :] = z.astype(BF16)
    state_out_ref[...] = state
    z = z_ref[...]
    for j in range(SLABS):
        part_ref[:, j * SLAB : (j + 1) * SLAB] = nt(z, wo_ref[slab_at(meta, j), :]).astype(BF16)


def summed(mine, core, far, far_core, j):
    other = (j + 2) % SLABS
    total = mine[:, j * SLAB : (j + 1) * SLAB].astype(F32)
    total = total + core[:, other * SLAB : (other + 1) * SLAB].astype(F32)
    beyond = far if j < 2 else far_core
    k = 1 - j % 2
    return total + beyond[:, k * SLAB : (k + 1) * SLAB].astype(F32)


def feed_kernel(n_saved, meta, *refs):
    x_ref, terms, dys = refs[0], refs[1:5], refs[5:9]
    wf_ref, g2_ref = refs[9:11]
    refs = refs[11 + n_saved :]
    part_ref = refs[0]
    feed_keep_ref, feed_send_ref, hn_ref, dy_ref, hidden_ref, dgu_ref, rhat_ref, rs_ref, resid_ref = refs[1:]
    width = hidden_ref.shape[1]
    resid = []
    total = 0.0
    for j in range(SLABS):
        part = x_ref[:, slab_at(meta, j)].astype(F32) + summed(*terms, j)
        resid.append(part)
        total = total + jnp.sum(part * part, axis=-1, keepdims=True)
    resid_ref[...] = resid[0]
    scale = lax.rsqrt(total / D + NORM_EPS)
    rs_ref[...] = jnp.broadcast_to(scale, rs_ref.shape)
    units = 0.0
    dhid = 0.0
    for j in range(SLABS):
        at = slab_at(meta, j)
        rhat = resid[j] * scale
        rhat_ref[:, j * SLAB : (j + 1) * SLAB] = rhat.astype(BF16)
        hn = (rhat * g2_ref[:, at]).astype(BF16)
        hn_ref[:, at] = hn
        dy = dys[j][...]
        dy_ref[:, at] = dy
        units = units + nn(hn, wf_ref[at, : 2 * width])
        dhid = dhid + nn(dy, wf_ref[at, 2 * width :])
    gate = units[:, :width]
    up = units[:, width:]
    sig = jax.nn.sigmoid(gate)
    act = gate * sig
    hidden = (act * up).astype(BF16)
    hidden_ref[...] = hidden
    dgate = (dhid * up * (sig * (1.0 + gate * (1.0 - sig)))).astype(BF16)
    dup = (dhid * act).astype(BF16)
    dgu_ref[:, :width] = dgate
    dgu_ref[:, width:] = dup
    for j in range(SLABS):
        at = slab_at(meta, j)
        part = nt(dgate, wf_ref[at, :width]) + nt(dup, wf_ref[at, width : 2 * width])
        part_ref[:, j * SLAB : (j + 1) * SLAB] = part.astype(BF16)
        fed = nt(hidden, wf_ref[at, 2 * width :]).astype(BF16)
        target = feed_keep_ref if j < 2 else feed_send_ref
        target[:, (j % 2) * SLAB : (j % 2 + 1) * SLAB] = fed


LOWIN_ROW = 0
IN_ROW = 16
MID_ROW = 17
HEAD_ROW = 18
LOWOUT_ROW = 24
SUM_ROWS = 32


def back_kernel(last_block, n_saved, meta, *refs):
    terms = refs[:4]
    dy_ref, rhat_ref, rs_ref, x_ref, xn_ref = refs[4:9]
    qkv_ref, gout_ref, lowr_ref, zeta_ref, mixed_ref, states_ref = refs[9:15]
    w_ref, wo_ref, wb_ref, g2_ref, go_ref = refs[15:20]
    dstate_ref, next_ref, sums_ref = refs[20:23]
    refs = refs[23 + n_saved :]
    keep_ref, send_ref, dstate_out_ref, next_out_ref, sums_out_ref = refs[:5]
    dres16_ref, dres_ref, dall_ref = refs[5:]
    step = pl.program_id(0)

    @pl.when(step == 0)
    def _():
        dstate_out_ref[...] = dstate_ref[...]
        next_out_ref[...] = next_ref[...]
        sums_out_ref[...] = sums_ref[...]

    ends = [meta[SLABS + i] for i in range(meta.shape[0] - SLABS)]
    base = (last_block - step) * BLOCK
    scaled = []
    dot = 0.0
    for j in range(SLABS):
        dhn = summed(*terms, j)
        rhat = rhat_ref[:, j * SLAB : (j + 1) * SLAB].astype(F32)
        if j == 0:
            sums_out_ref[MID_ROW : MID_ROW + 1, slab_at(meta, 0)] += jnp.sum(
                dhn * rhat, axis=0, keepdims=True
            )
        part = dhn * g2_ref[:, slab_at(meta, j)]
        scaled.append(part)
        dot = dot + jnp.sum(part * rhat, axis=-1, keepdims=True)
    scale = rs_ref[:, :1]
    mean = dot / D
    dz = 0.0
    for j in range(SLABS):
        at = slab_at(meta, j)
        rhat = rhat_ref[:, j * SLAB : (j + 1) * SLAB].astype(F32)
        dres = dy_ref[:, at].astype(F32) + scale * (scaled[j] - rhat * mean)
        if j == 0:
            dres_ref[...] = dres
        low = dres.astype(BF16)
        dres16_ref[:, at] = low
        dz = dz + nn(low, wo_ref[at, :])
    where = lax.broadcasted_iota(jnp.int32, (BLOCK, DV), 0) + base
    u = jnp.where(where < ends[-1], dz, 0.0)
    mixed = mixed_ref[...]
    head_scale = lax.rsqrt(jnp.mean(mixed * mixed, axis=-1, keepdims=True) + NORM_EPS)
    hat = mixed * head_scale
    gate = gout_ref[...]
    sig = jax.nn.sigmoid(gate)
    act = gate * sig
    uhat = u * hat
    go = go_ref[...]
    sums_out_ref[HEAD_ROW : HEAD_ROW + 1, :DV] += jnp.sum(uhat * act, axis=0, keepdims=True)
    dall_ref[:, 2 * DK + DV : MAIN] = (uhat * go * (sig * (1.0 + gate * (1.0 - sig)))).astype(BF16)
    dhat = u * go * act
    dmix = head_scale * (dhat - hat * jnp.mean(dhat * hat, axis=-1, keepdims=True))
    dmix = (dmix * OUT_SCALE).astype(BF16)
    zeta = zeta_ref[...]
    forget = log_sigmoid(zeta) * (1.0 / GATE_NORM)
    slope = jax.nn.sigmoid(-zeta) * (1.0 / GATE_NORM)
    dstate = dstate_out_ref[...]
    after = next_out_ref[...]
    head_at = meta[0] * DK
    for i in reversed(range(BLOCK // CHUNK)):
        rows = slice(i * CHUNK, (i + 1) * CHUNK)
        queries = qkv_ref[rows, :DK].astype(F32)
        keys = qkv_ref[rows, DK : 2 * DK].astype(F32)
        values = qkv_ref[rows, 2 * DK :]
        masks, factors, parts, scores = chunk_terms(
            queries, keys, forget[rows], base + i * CHUNK, ends
        )
        row, col, near, far = masks
        grow, shrink, edge, from_start, to_end, decay_step = factors
        q_near, k_near, q_far, k_far, q_state, k_state = parts
        state = states_ref[i * DV : (i + 1) * DV, :]
        do = dmix[rows]
        dstate_low = dstate.astype(BF16)
        dscores = nt(do, values)
        dnear = jnp.where(near, dscores, 0.0).astype(BF16)
        dfar = jnp.where(far, dscores, 0.0).astype(BF16)
        dv = tn(scores, do) + nt(k_state, dstate_low)
        dq = nn(do, state) * from_start + nn(dnear, k_near) * grow
        dq = dq + jnp.where(row >= SPAN, nn(dfar, k_far) * edge, 0.0)
        dk = nn(values, dstate_low) * to_end + tn(dnear, q_near) * shrink
        dk = dk + jnp.where(row < SPAN, tn(dfar, q_far) * edge, 0.0)
        dall_ref[rows, :DK] = dq.astype(BF16)
        dall_ref[rows, DK : 2 * DK] = dk.astype(BF16)
        dall_ref[rows, 2 * DK : 2 * DK + DV] = dv.astype(BF16)
        at_end = jnp.sum(dstate * after.astype(F32), axis=0, keepdims=True)
        ddecay = queries * dq - keys * dk
        dforget = prefix_sums(ddecay, jnp.where(col >= row, 1.0, 0.0).astype(BF16)) + at_end
        dzeta = (dforget * slope[rows]).astype(BF16)
        sums_out_ref[HEAD_ROW : HEAD_ROW + 1, lanes_at(DV + head_at)] += jnp.sum(
            dzeta.astype(F32), axis=0, keepdims=True
        )
        dlowout = tn(lowr_ref[rows, :], dzeta)
        for k in range(2):
            sums_out_ref[LOWOUT_ROW:, lanes_at(k * (D // 2) + head_at)] += dlowout[k * 8 : (k + 1) * 8]
        dall_ref[rows, MAIN:] = nt(dzeta, wb_ref[...]).astype(BF16)
        dstate = dstate * decay_step + tn(do, q_state)
        after = state
    dstate_out_ref[...] = dstate
    next_out_ref[...] = after
    dall = dall_ref[...]
    sums_out_ref[LOWIN_ROW : LOWIN_ROW + RANK, :] += tn(dall[:, MAIN:], xn_ref[...])[:RANK]
    x = x_ref[...].astype(F32)
    in_scale = lax.rsqrt(jnp.mean(x * x, axis=-1, keepdims=True) + NORM_EPS)
    for j in range(SLABS):
        at = slab_at(meta, j)
        part = nt(dall, w_ref[at, :])
        sums_out_ref[IN_ROW : IN_ROW + 1, at] += jnp.sum(
            part * (x_ref[:, at].astype(F32) * in_scale), axis=0, keepdims=True
        )
        target = keep_ref if j < 2 else send_ref
        target[:, (j % 2) * SLAB : (j % 2 + 1) * SLAB] = part.astype(BF16)


def update_kernel(*refs):
    clip_ref, attn_ref, units_ref, down_ref = refs[:4]
    masters, firsts, seconds = refs[4:9], refs[9:14], refs[14:19]
    outs = refs[19:]
    clip = clip_ref[0]
    units = masters[3].shape[2]
    width = down_ref.shape[1]
    attn = attn_ref[...]
    grads = (
        (attn[:, :DK], attn[:, DK : 2 * DK]),
        (attn[:, 2 * DK : 2 * DK + DV], attn[:, 2 * DK + DV : MAIN]),
        (attn[:, MAIN:].T,),
        (units_ref[:, :units].astype(F32), units_ref[:, width : width + units].astype(F32)),
        (down_ref[...].astype(F32).T[:units],),
    )
    rates = (D, D, HEADS * DV, D, FF)
    for i in range(5):
        for k, grad in enumerate(grads[i]):
            at = k if len(grads[i]) > 1 else Ellipsis
            results = adam_step(
                masters[i][at], grad, firsts[i][at], seconds[i][at], clip, 2.0 * rates[i] ** (-0.5), WEIGHT_DECAY
            )
            for n in range(3):
                outs[n * 5 + i][at] = results[n]


def whole(array):
    zeros = (0,) * array.ndim
    return pl.BlockSpec(array.shape, lambda i, meta: zeros, pipeline_mode=pl.Buffered(1))


def fixed(shape):
    return pl.BlockSpec(shape, lambda i, meta: (0,) * len(shape))


def rows_at(rows, width, place):
    return pl.BlockSpec((rows, width), lambda i, meta: (place(i), 0))


def like(shape, dtype):
    return jax.ShapeDtypeStruct(shape, dtype)


def params():
    return pltpu.CompilerParams(vmem_limit_bytes=VMEM_LIMIT)


def run_kernel(body, meta, steps, ins, in_specs, saved, outs, out_specs, saved_like, saved_specs, name, flops):
    given = [] if saved is None else list(saved)
    aliases = {1 + len(ins) + i: len(outs) + i for i in range(len(given))}
    result = pl.pallas_call(
        functools.partial(body, len(given)),
        grid_spec=pltpu.PrefetchScalarGridSpec(
            num_scalar_prefetch=1,
            grid=(steps,),
            in_specs=list(in_specs) + [pl.BlockSpec(memory_space=pl.ANY)] * len(given),
            out_specs=list(out_specs) + list(saved_specs),
        ),
        out_shape=list(outs) + list(saved_like),
        input_output_aliases=aliases,
        compiler_params=params(),
        cost_estimate=pl.CostEstimate(flops=flops, bytes_accessed=16 * 1024 * 1024, transcendentals=0),
        name=name,
    )(meta, *ins, *given)
    return list(result[: len(outs)]), list(result[len(outs) :])


def attend(piece, meta, x, w, wo, wb, g1, go, c, state, saved):
    tokens = x.shape[0]
    size = tokens // PIECES
    steps = size // BLOCK
    first = piece * steps
    here = lambda i: first + i
    ins = [x, w, wo, wb, g1, go, c, state]
    in_specs = [rows_at(BLOCK, D, here)] + [whole(a) for a in ins[1:]]
    outs = [like((size, D), BF16), like(state.shape, F32)]
    out_specs = [rows_at(BLOCK, D, lambda i: i), fixed(state.shape)]
    widths = [
        (D, BF16),
        (2 * DK + DV, BF16),
        (DV, F32),
        (LANES, BF16),
        (DK, F32),
        (DV, F32),
        (DV, BF16),
    ]
    saved_like = [like((tokens, n), d) for n, d in widths]
    saved_specs = [rows_at(BLOCK, n, here) for n, _ in widths]
    saved_like.append(like((tokens // CHUNK * DV, DK), BF16))
    saved_specs.append(rows_at(BLOCK // CHUNK * DV, DK, here))
    return run_kernel(
        functools.partial(attend_kernel, first),
        meta, steps, ins, in_specs, saved, outs, out_specs, saved_like, saved_specs,
        "attend", size * 8 * D * 1024,
    )


def feed(piece, meta, x, terms, dys, wf, g2, saved):
    tokens = x.shape[0]
    size = tokens // PIECES
    steps = size // BLOCK
    first = piece * steps
    here = lambda i: first + i
    width = wf.shape[1] // 3
    ins = [x, *terms, *dys, wf, g2]
    in_specs = (
        [rows_at(BLOCK, D, here)]
        + [rows_at(BLOCK, a.shape[1], lambda i: i) for a in terms]
        + [rows_at(BLOCK, SLAB, here)] * SLABS
        + [whole(wf), whole(g2)]
    )
    outs = [like((size, D), BF16)]
    out_specs = [rows_at(BLOCK, D, lambda i: i)]
    widths = [
        (2 * SLAB, BF16),
        (2 * SLAB, BF16),
        (D, BF16),
        (D, BF16),
        (width, BF16),
        (2 * width, BF16),
        (D, BF16),
        (LANES, F32),
        (SLAB, F32),
    ]
    saved_like = [like((tokens, n), d) for n, d in widths]
    saved_specs = [rows_at(BLOCK, n, here) for n, _ in widths]
    return run_kernel(
        feed_kernel,
        meta, steps, ins, in_specs, saved, outs, out_specs, saved_like, saved_specs,
        "feed", size * 2 * D * width * 6,
    )


def back(piece, meta, terms, dy, rhat, rs, x, xn, kept, w, wo, wb, g2, go, carried, saved):
    tokens = x.shape[0]
    size = tokens // PIECES
    steps = size // BLOCK
    last = (piece + 1) * steps - 1
    here = lambda i: last - i
    local = lambda i: steps - 1 - i
    ins = [*terms, dy, rhat, rs, x, xn, *kept, w, wo, wb, g2, go, *carried]
    in_specs = (
        [rows_at(BLOCK, a.shape[1], local) for a in terms]
        + [rows_at(BLOCK, a.shape[1], here) for a in (dy, rhat, rs, x, xn)]
        + [rows_at(BLOCK, a.shape[1], here) for a in kept[:-1]]
        + [rows_at(BLOCK // CHUNK * DV, DK, here)]
        + [whole(a) for a in (w, wo, wb, g2, go, *carried)]
    )
    outs = [like((size, 2 * SLAB), BF16)] * 2 + [like(a.shape, a.dtype) for a in carried]
    out_specs = [rows_at(BLOCK, 2 * SLAB, local)] * 2 + [fixed(a.shape) for a in carried]
    widths = [(D, BF16), (SLAB, F32), (ATTN, BF16)]
    saved_like = [like((tokens, n), d) for n, d in widths]
    saved_specs = [rows_at(BLOCK, n, here) for n, _ in widths]
    return run_kernel(
        functools.partial(back_kernel, last),
        meta, steps, ins, in_specs, saved, outs, out_specs, saved_like, saved_specs,
        "back", size * 12 * D * 1024,
    )


def swap(array, axis, bit):
    return lax.ppermute(array, axis, [(i, i ^ bit) for i in range(lax.axis_size(axis))])


def swap_core(array):
    return swap(array, "tensor", 1)


def swap_far(array):
    return swap(array, "tensor", 2)


def swap_row(array):
    return swap(array, "dp", 1)


def shift_layer(array, by):
    count = lax.axis_size("dp")
    return lax.ppermute(array, "dp", [(i, (i + 2 * by) % count) for i in range(count)])


def gather_attn(own):
    dp_at = lax.axis_index("dp")
    pieces, places = [], []
    received = [own] + [shift_layer(own, k) for k in (1, 3, 2)]
    for k, here in zip((0, 1, 3, 2), received):
        block = (dp_at - 2 * k) % (2 * SLABS)
        pieces += [here, swap_row(here)]
        places += [block, block ^ 1]
    rows = D
    return pl.pallas_call(
        assemble_kernel,
        in_specs=[pl.BlockSpec(memory_space=pltpu.SMEM)]
        + [pl.BlockSpec(memory_space=pltpu.VMEM)] * (2 * SLABS),
        out_shape=(like((rows, ATTN), BF16), like((rows, DV), BF16), like((LANES, DK), BF16)),
        compiler_params=params(),
        name="assemble",
    )(jnp.stack(places).astype(jnp.int32), *pieces)


def gather_plain(own):
    count, rows = lax.axis_size("dp"), own.shape[0]
    full = lax.all_gather(own, "dp", axis=0, tiled=True)
    keys = DK // count
    blocks = full.reshape(count, rows, -1)[:, :RANK, MAIN + RANK : MAIN + RANK + keys]
    wb = jnp.pad(blocks.transpose(1, 0, 2).reshape(RANK, DK), ((0, LANES - RANK), (0, 0)))
    return full[:, :ATTN], full[:, ATTN:], wb


def scatter_attn(grads):
    dp_at = lax.axis_index("dp")
    high, low, row = dp_at // 4, (dp_at // 2) % 2, dp_at % 2
    rows = D // (2 * SLABS)

    def pick(array, axis, index):
        return lax.dynamic_index_in_dim(array, index, axis, keepdims=False)

    def halves(axis, index):
        def cut(at):
            parts = [pick(g.reshape(2, 2, 2, rows, -1), axis, at) for g in grads]
            return jnp.concatenate(parts, axis=-1)

        return cut(index), cut(1 - index)

    here, away = halves(2, row)
    here = here.astype(F32) + swap_row(away).astype(F32)
    away = pick(here, 1, 1 - low).astype(BF16)
    here = pick(here, 1, low) + swap(away, "dp", 2).astype(F32)
    away = pick(here, 0, 1 - high).astype(BF16)
    return pick(here, 0, high) + swap(away, "dp", 4).astype(F32)


def sum_terms(part):
    core = swap_core(part)
    own = (part[:, : 2 * SLAB].astype(F32) + core[:, 2 * SLAB :].astype(F32)).astype(BF16)
    far = swap_far(own)
    return part, core, far, swap_core(far)


def slab_sum(keep, send):
    own = keep.astype(F32) + swap_core(send).astype(F32)
    return own[:, :SLAB] + swap_far(own[:, SLAB:].astype(BF16)).astype(F32)


def sum_everywhere(array, axes=("tensor", "dp")):
    for axis in axes:
        size = lax.axis_size(axis)
        bit = 1
        while bit < size:
            array = array + swap(array, axis, bit)
            bit *= 2
    return array


def adam_step(weight, gradient, first_moment, second_moment, clip_factor, learn_rate, weight_decay):
    clipped = gradient * clip_factor
    momentum = BETA_FIRST * first_moment + (1.0 - BETA_FIRST) * clipped
    variance = BETA_SECOND * second_moment + (1.0 - BETA_SECOND) * clipped * clipped
    step_size = (
        momentum
        / (1.0 - BETA_FIRST**STEP)
        / (jnp.sqrt(variance / (1.0 - BETA_SECOND**STEP)) + ADAM_EPS)
    )
    updated = weight * (1.0 - learn_rate * weight_decay) - learn_rate * step_size
    return (momentum, variance, updated)


LARGE = (0, 1, 4, 5, 6)


def body(*args):
    inputs, cotangent, doc_lengths = args[:3]
    masters, firsts, seconds = args[3:11], args[11:19], args[19:27]
    weight_qk, weight_vg, weight_lowin, weight_lowout, weight_mixout, weight_gateup, weight_down = masters[:7]
    weight_small = masters[7]
    tensor_at = lax.axis_index("tensor")
    dp_at = lax.axis_index("dp")
    layered = lax.axis_size("dp") == 2 * SLABS
    rows_here = weight_qk.shape[1]
    ranks, _, keys_here = weight_lowout.shape
    units = weight_gateup.shape[2]
    width = units + -units % LANES

    attn_pack, feed_pack = pl.pallas_call(
        pack_kernel,
        out_shape=(like((rows_here, ATTN + DV), BF16), like((rows_here, 3 * width), BF16)),
        compiler_params=params(),
        name="pack",
    )(weight_qk, weight_vg, weight_lowin, weight_lowout[:, 0, :], weight_mixout, weight_gateup, weight_down)
    w, wo, wb = (gather_attn if layered else gather_plain)(attn_pack)
    wf = lax.all_gather(feed_pack, "dp", axis=0, tiled=True)
    doc_ends = jnp.cumsum(doc_lengths[0])
    slots = jnp.stack([tensor_at ^ o for o in ORDER])
    meta = jnp.concatenate([slots.astype(jnp.int32), doc_ends.astype(jnp.int32)])

    g1, g2 = weight_small[:D].reshape(1, D), weight_small[D : 2 * D].reshape(1, D)
    go = weight_small[2 * D : 2 * D + DV].reshape(1, DV)
    gate_bias = lax.dynamic_slice_in_dim(weight_small, 2 * D + DV + tensor_at * DK, DK).reshape(1, DK)
    x = inputs
    far_cot = swap_far(cotangent)
    dys = [cotangent, far_cot, swap_core(cotangent), swap_core(far_cot)]

    state = jnp.zeros((DV, DK), F32)
    saved = None
    terms = []
    for piece in range(PIECES):
        (part, state), saved = attend(piece, meta, x, w, wo, wb, g1, go, gate_bias, state, saved)
        terms.append(sum_terms(part))
    xn, *kept = saved
    z = kept.pop(5)

    fed = None
    back_terms = {}
    for piece in reversed(range(PIECES)):
        (part,), fed = feed(piece, meta, x, terms[piece], dys, wf, g2, fed)
        back_terms[piece] = sum_terms(part)
    feed_keep, feed_send, hn, dy, hidden, dgu, rhat, rs, resid = fed
    grad_units = tn(hn, dgu).astype(BF16)
    grad_down = tn(dy, hidden).astype(BF16)
    shard_units = lax.psum_scatter(grad_units, "dp", scatter_dimension=0, tiled=True)
    shard_down = lax.psum_scatter(grad_down, "dp", scatter_dimension=0, tiled=True)
    output = (resid + slab_sum(feed_keep, feed_send)).astype(BF16)

    carried = [jnp.zeros((DV, DK), F32), jnp.zeros((DV, DK), BF16), jnp.zeros((SUM_ROWS, D), F32)]
    backed = None
    dxn = []
    for piece in reversed(range(PIECES)):
        (keep, send, *carried), backed = back(
            piece, meta, back_terms[piece], dy, rhat, rs, x, xn, kept, w, wo, wb, g2, go, carried, backed
        )
        dxn.insert(0, slab_sum(keep, send))
    dres16, dres, dall = backed
    grads = [tn(xn, dall[:, :MAIN]).astype(BF16), tn(dres16, z).astype(BF16)]
    if layered:
        shard_attn = scatter_attn(grads)
    else:
        shard_attn = lax.psum_scatter(
            jnp.concatenate(grads, axis=1), "dp", scatter_dimension=0, tiled=True
        ).astype(F32)

    dxn = jnp.concatenate(dxn, axis=0)
    x_wide = x.astype(F32)
    in_scale = lax.rsqrt(jnp.mean(x_wide * x_wide, axis=-1, keepdims=True) + NORM_EPS)
    hat_here = lax.dynamic_slice_in_dim(x, tensor_at * SLAB, SLAB, 1).astype(F32) * in_scale
    scaled = dxn * lax.dynamic_slice_in_dim(g1, tensor_at * SLAB, SLAB, 1)
    row_sums = jnp.sum(scaled * hat_here, axis=-1).reshape(-1, LANES)
    row_mean = sum_everywhere(row_sums, ("tensor",)).reshape(-1, 1) / D
    input_grad = dres + in_scale * (scaled - hat_here * row_mean)

    wide = sum_everywhere(carried[2])
    small_grad = jnp.concatenate([wide[IN_ROW], wide[MID_ROW], wide[HEAD_ROW, : DV + HEADS * DK]])
    grad_lowin = lax.dynamic_slice(wide, (LOWIN_ROW, dp_at * rows_here), (RANK, rows_here)).T
    lowout = jnp.concatenate([wide[LOWOUT_ROW:, : D // 2], wide[LOWOUT_ROW:, D // 2 :]], axis=0)
    grad_lowout = lax.dynamic_slice(
        lowout, (0, tensor_at * DK + dp_at * keys_here), (RANK, keys_here)
    ).reshape(weight_lowout.shape)

    squares = sum(jnp.sum(jnp.square(s.astype(F32))) for s in (shard_units, shard_down, shard_attn))
    square_total = sum_everywhere(jnp.broadcast_to(squares, (8, LANES)))[0, 0]
    grad_norm = jnp.sqrt(square_total + jnp.sum(wide * wide))
    clip_factor = jnp.minimum(1.0, CLIP_NORM / (grad_norm + 1e-06))
    pick = lambda arrays: [arrays[i] for i in LARGE]
    large = pl.pallas_call(
        update_kernel,
        in_specs=[pl.BlockSpec(memory_space=pltpu.SMEM)] + [pl.BlockSpec(memory_space=pltpu.VMEM)] * 18,
        out_shape=[like(a.shape, F32) for a in pick(masters)] * 3,
        compiler_params=params(),
        name="update",
    )(
        clip_factor.reshape(1), shard_attn, shard_units, shard_down,
        *pick(masters), *pick(firsts), *pick(seconds),
    )
    small_rate = jnp.where(
        lax.broadcasted_iota(jnp.int32, weight_small.shape, 0) < 2 * D + DV, GAIN_RATE, BIAS_RATE
    )
    steps = {}
    for k, i in enumerate(LARGE):
        steps[i] = large[k::5]
    for i, grad, rate, decay in (
        (2, grad_lowin, 2.0 * D ** (-0.5), WEIGHT_DECAY),
        (3, grad_lowout, 2.0 * RANK ** (-0.5), WEIGHT_DECAY),
        (7, small_grad, small_rate, 0.0),
    ):
        steps[i] = adam_step(masters[i], grad, firsts[i], seconds[i], clip_factor, rate, decay)
    return (output, input_grad, grad_norm.reshape(1), *(steps[i][k] for k in range(3) for i in range(8)))


def solution(mesh):
    weights = (
        P(None, "dp", "tensor"),
        P(None, "dp", "tensor"),
        P("dp", None),
        P(None, "tensor", "dp"),
        P("tensor", "dp"),
        P(None, "dp", "tensor"),
        P("tensor", "dp"),
        P(),
    )
    return jax.shard_map(
        body,
        mesh=mesh,
        in_specs=(P("dp", None), P("dp", "tensor"), P("dp", None), *weights, *weights, *weights),
        out_specs=(P("dp", "tensor"), P("dp", "tensor"), P(), *weights, *weights, *weights),
        check_vma=False,
    )
```

```python
import functools

import jax
import jax.numpy as jnp
from jax import lax
from jax.experimental import pallas as pl
from jax.experimental.pallas import tpu as pltpu
from jax.sharding import PartitionSpec as P

D = 1024
HEADS = 4
DK = 128
DV = 256
RANK = 16
FF = 2816
SPAN = 64
SEQ_LEN = 2048
STEP = 10

NORM_EPS = 1e-06
GATE_NORM = 16.0
BETA_FIRST = 0.9
BETA_SECOND = 0.95
ADAM_EPS = 1e-08
WEIGHT_DECAY = 0.1
CLIP_NORM = 1.0
GAIN_RATE = 2.5
BIAS_RATE = 4.0

F32 = jnp.float32
BF16 = jnp.bfloat16
LANES = 128
SLAB = 256
SLABS = 4
CHUNK = 2 * SPAN
BLOCK = 256
PIECES = 2
ORDER = (0, 2, 1, 3)
MAIN = 768
ATTN = 896
FEED_COLS = 3 * 768
OUT_SCALE = DK**-0.5
VMEM_LIMIT = 60 * 1024 * 1024


def nn(a, b):
    return lax.dot_general(a, b, (((1,), (0,)), ((), ())), preferred_element_type=F32)


def nt(a, b):
    return lax.dot_general(a, b, (((1,), (1,)), ((), ())), preferred_element_type=F32)


def tn(a, b):
    return lax.dot_general(a, b, (((0,), (0,)), ((), ())), preferred_element_type=F32)


def doc_at(position, ends):
    number = jnp.zeros_like(position)
    for end in ends:
        number = number + jnp.where(position >= end, 1, 0)
    return number


def log_sigmoid(values):
    return jnp.minimum(values, 0.0) - jnp.log1p(jnp.exp(-jnp.abs(values)))


def prefix_sums(values, triangle):
    high = values.astype(BF16)
    low = (values - high.astype(F32)).astype(BF16)
    width = values.shape[1]
    both = nn(triangle, jnp.concatenate([high, low], axis=1))
    return both[:, :width] + both[:, width:]


def chunk_terms(queries, keys, forget, base, ends):
    row = lax.broadcasted_iota(jnp.int32, (CHUNK, CHUNK), 0)
    col = lax.broadcasted_iota(jnp.int32, (CHUNK, CHUNK), 1)
    decay = prefix_sums(forget, jnp.where(col <= row, 1.0, 0.0).astype(BF16))
    seg_row = doc_at(row + base, ends)
    same = seg_row == doc_at(col + base, ends)
    upper = row >= SPAN
    near = same & (col <= row) & (upper == (col >= SPAN))
    far = same & upper & (col < SPAN)
    before = jnp.where(base > 0, doc_at(base - 1, ends), -1)
    final = doc_at(base + CHUNK - 1, ends)
    alive = jnp.where(seg_row == before, 1.0, 0.0)
    keep = jnp.where(seg_row == final, 1.0, 0.0)
    carry = jnp.where(before == final, 1.0, 0.0)
    mid = jnp.where(upper, decay[SPAN + SPAN // 2 :][:1], decay[SPAN // 2 :][:1])
    grow = jnp.exp(decay - mid)
    shrink = jnp.exp(mid - decay)
    edge = jnp.exp(-jnp.abs(decay - decay[SPAN - 1 : SPAN]))
    from_start = jnp.exp(decay) * alive
    last = decay[CHUNK - 1 : CHUNK]
    to_end = jnp.exp(last - decay) * keep
    step = jnp.exp(last) * carry
    q_near = (queries * grow).astype(BF16)
    k_near = (keys * shrink).astype(BF16)
    q_far = (queries * edge).astype(BF16)
    k_far = (keys * edge).astype(BF16)
    q_state = (queries * from_start).astype(BF16)
    k_state = (keys * to_end).astype(BF16)
    scores = jnp.where(near, nt(q_near, k_near), jnp.where(far, nt(q_far, k_far), 0.0)).astype(BF16)
    return (
        (row, col, near, far),
        (grow, shrink, edge, from_start, to_end, step),
        (q_near, k_near, q_far, k_far, q_state, k_state),
        scores,
    )


def slab_at(meta, j):
    return pl.ds(pl.multiple_of(meta[j] * SLAB, SLAB), SLAB)


def lanes_at(start):
    return pl.ds(pl.multiple_of(start, LANES), LANES)


def one_hot(rows, shift):
    row = lax.broadcasted_iota(jnp.int32, (rows, LANES), 0)
    col = lax.broadcasted_iota(jnp.int32, (rows, LANES), 1)
    return jnp.where(col - row == shift, 1.0, 0.0).astype(BF16)


def pack_kernel(qk_ref, vg_ref, lowin_ref, lowout_ref, mixout_ref, gateup_ref, down_ref, attn_ref, feed_ref):
    units = gateup_ref.shape[1]
    width = feed_ref.shape[1] // 3
    attn_ref[:, :DK] = qk_ref[0].astype(BF16)
    attn_ref[:, DK : 2 * DK] = qk_ref[1].astype(BF16)
    attn_ref[:, 2 * DK : 2 * DK + DV] = vg_ref[0].astype(BF16)
    attn_ref[:, 2 * DK + DV : MAIN] = vg_ref[1].astype(BF16)
    attn_ref[:, MAIN:ATTN] = tn(lowin_ref[...].astype(BF16), one_hot(RANK, 0)).astype(BF16)
    lowout = lowout_ref[...].astype(BF16)
    attn_ref[:RANK, MAIN:ATTN] += nn(lowout, one_hot(lowout.shape[1], RANK)).astype(BF16)
    attn_ref[:, ATTN:] = mixout_ref[...].T.astype(BF16)
    rows = feed_ref.shape[0]
    pad = jnp.zeros((rows, width - units), BF16)
    feed_ref[:, :units] = gateup_ref[0].T.astype(BF16)
    feed_ref[:, units:width] = pad
    feed_ref[:, width : width + units] = gateup_ref[1].T.astype(BF16)
    feed_ref[:, width + units : 2 * width] = pad
    feed_ref[:, 2 * width : 2 * width + units] = down_ref[...].T.astype(BF16)
    feed_ref[:, 2 * width + units :] = pad


def assemble_kernel(place, *refs):
    pieces = refs[: 2 * SLABS]
    w_ref, wo_ref, wb_ref = refs[2 * SLABS :]
    rows = pieces[0].shape[0]
    keys = DK // (2 * SLABS)
    wb_ref[...] = jnp.zeros_like(wb_ref)
    for i, piece in enumerate(pieces):
        block = place[i]
        at = pl.ds(pl.multiple_of(block * rows, rows), rows)
        w_ref[at, :] = piece[:, :ATTN]
        wo_ref[at, :] = piece[:, ATTN:]
        row = lax.broadcasted_iota(jnp.int32, (LANES, DK), 0)
        col = lax.broadcasted_iota(jnp.int32, (LANES, DK), 1)
        inside = (row >= RANK) & (row < RANK + keys)
        move = jnp.where(inside & (col - row == block * keys - RANK), 1.0, 0.0).astype(BF16)
        wb_ref[:RANK, :] += nn(piece[:RANK, MAIN:ATTN], move).astype(BF16)


def attend_kernel(first_block, n_saved, meta, *refs):
    x_ref, w_ref, wo_ref, wb_ref, g1_ref, go_ref, c_ref, state_ref = refs[:8]
    refs = refs[8 + n_saved :]
    part_ref, state_out_ref = refs[:2]
    xn_ref, qkv_ref, gout_ref, lowr_ref, zeta_ref, mixed_ref, z_ref, states_ref = refs[2:]
    step = pl.program_id(0)

    @pl.when(step == 0)
    def _():
        state_out_ref[...] = state_ref[...]

    ends = [meta[SLABS + i] for i in range(meta.shape[0] - SLABS)]
    x = x_ref[...].astype(F32)
    scale = lax.rsqrt(jnp.mean(x * x, axis=-1, keepdims=True) + NORM_EPS)
    normed = (x * scale * g1_ref[...]).astype(BF16)
    xn_ref[...] = normed
    proj = nn(normed, w_ref[...])
    qkv = proj[:, : 2 * DK + DV].astype(BF16)
    qkv_ref[...] = qkv
    gout = proj[:, 2 * DK + DV : MAIN]
    gout_ref[...] = gout
    lowr = proj[:, MAIN:].astype(BF16)
    lowr_ref[...] = lowr
    zeta = nn(lowr, wb_ref[...]) + c_ref[...]
    zeta_ref[...] = zeta
    forget = log_sigmoid(zeta) * (1.0 / GATE_NORM)
    base = (first_block + step) * BLOCK
    state = state_out_ref[...]
    for i in range(BLOCK // CHUNK):
        rows = slice(i * CHUNK, (i + 1) * CHUNK)
        queries = qkv[rows, :DK].astype(F32)
        keys = qkv[rows, DK : 2 * DK].astype(F32)
        values = qkv[rows, 2 * DK :]
        start = base + i * CHUNK
        _, factors, terms, scores = chunk_terms(queries, keys, forget[rows], start, ends)
        q_state, k_state = terms[4:]
        state_low = state.astype(BF16)
        states_ref[i * DV : (i + 1) * DV, :] = state_low
        mixed = (nn(scores, values) + nt(q_state, state_low)) * OUT_SCALE
        mixed_ref[rows, :] = mixed
        state = state * factors[5] + tn(values, k_state)
        where = lax.broadcasted_iota(jnp.int32, (CHUNK, DV), 0) + start
        valid = jnp.where(where < ends[-1], 1.0, 0.0)
        head_scale = lax.rsqrt(jnp.mean(mixed * mixed, axis=-1, keepdims=True) + NORM_EPS)
        gate = gout[rows]
        z = mixed * head_scale * go_ref[...] * (gate * jax.nn.sigmoid(gate)) * valid
        z_ref[rows, :] = z.astype(BF16)
    state_out_ref[...] = state
    z = z_ref[...]
    for j in range(SLABS):
        part_ref[:, j * SLAB : (j + 1) * SLAB] = nt(z, wo_ref[slab_at(meta, j), :]).astype(BF16)


def summed(mine, core, far, far_core, j):
    other = (j + 2) % SLABS
    total = mine[:, j * SLAB : (j + 1) * SLAB].astype(F32)
    total = total + core[:, other * SLAB : (other + 1) * SLAB].astype(F32)
    beyond = far if j < 2 else far_core
    k = 1 - j % 2
    return total + beyond[:, k * SLAB : (k + 1) * SLAB].astype(F32)


def feed_kernel(n_saved, meta, *refs):
    x_ref, terms, dys = refs[0], refs[1:5], refs[5:9]
    wf_ref, g2_ref = refs[9:11]
    refs = refs[11 + n_saved :]
    part_ref = refs[0]
    feed_keep_ref, feed_send_ref, hn_ref, dy_ref, hidden_ref, dgu_ref, rhat_ref, rs_ref, resid_ref = refs[1:]
    width = hidden_ref.shape[1]
    resid = []
    total = 0.0
    for j in range(SLABS):
        part = x_ref[:, slab_at(meta, j)].astype(F32) + summed(*terms, j)
        resid.append(part)
        total = total + jnp.sum(part * part, axis=-1, keepdims=True)
    resid_ref[...] = resid[0]
    scale = lax.rsqrt(total / D + NORM_EPS)
    rs_ref[...] = jnp.broadcast_to(scale, rs_ref.shape)
    units = 0.0
    dhid = 0.0
    for j in range(SLABS):
        at = slab_at(meta, j)
        rhat = resid[j] * scale
        rhat_ref[:, j * SLAB : (j + 1) * SLAB] = rhat.astype(BF16)
        hn = (rhat * g2_ref[:, at]).astype(BF16)
        hn_ref[:, at] = hn
        dy = dys[j][...]
        dy_ref[:, at] = dy
        units = units + nn(hn, wf_ref[at, : 2 * width])
        dhid = dhid + nn(dy, wf_ref[at, 2 * width :])
    gate = units[:, :width]
    up = units[:, width:]
    sig = jax.nn.sigmoid(gate)
    act = gate * sig
    hidden = (act * up).astype(BF16)
    hidden_ref[...] = hidden
    dgate = (dhid * up * (sig * (1.0 + gate * (1.0 - sig)))).astype(BF16)
    dup = (dhid * act).astype(BF16)
    dgu_ref[:, :width] = dgate
    dgu_ref[:, width:] = dup
    for j in range(SLABS):
        at = slab_at(meta, j)
        part = nt(dgate, wf_ref[at, :width]) + nt(dup, wf_ref[at, width : 2 * width])
        part_ref[:, j * SLAB : (j + 1) * SLAB] = part.astype(BF16)
        fed = nt(hidden, wf_ref[at, 2 * width :]).astype(BF16)
        target = feed_keep_ref if j < 2 else feed_send_ref
        target[:, (j % 2) * SLAB : (j % 2 + 1) * SLAB] = fed


LOWIN_ROW = 0
IN_ROW = 16
MID_ROW = 17
HEAD_ROW = 18
LOWOUT_ROW = 24
SUM_ROWS = 32


def back_kernel(last_block, n_saved, meta, *refs):
    terms = refs[:4]
    dy_ref, rhat_ref, rs_ref, x_ref, xn_ref = refs[4:9]
    qkv_ref, gout_ref, lowr_ref, zeta_ref, mixed_ref, states_ref = refs[9:15]
    w_ref, wo_ref, wb_ref, g2_ref, go_ref = refs[15:20]
    dstate_ref, next_ref, sums_ref = refs[20:23]
    refs = refs[23 + n_saved :]
    keep_ref, send_ref, dstate_out_ref, next_out_ref, sums_out_ref = refs[:5]
    dres16_ref, dres_ref, dall_ref = refs[5:]
    step = pl.program_id(0)

    @pl.when(step == 0)
    def _():
        dstate_out_ref[...] = dstate_ref[...]
        next_out_ref[...] = next_ref[...]
        sums_out_ref[...] = sums_ref[...]

    ends = [meta[SLABS + i] for i in range(meta.shape[0] - SLABS)]
    base = (last_block - step) * BLOCK
    scaled = []
    dot = 0.0
    for j in range(SLABS):
        dhn = summed(*terms, j)
        rhat = rhat_ref[:, j * SLAB : (j + 1) * SLAB].astype(F32)
        if j == 0:
            sums_out_ref[MID_ROW : MID_ROW + 1, slab_at(meta, 0)] += jnp.sum(
                dhn * rhat, axis=0, keepdims=True
            )
        part = dhn * g2_ref[:, slab_at(meta, j)]
        scaled.append(part)
        dot = dot + jnp.sum(part * rhat, axis=-1, keepdims=True)
    scale = rs_ref[:, :1]
    mean = dot / D
    dz = 0.0
    for j in range(SLABS):
        at = slab_at(meta, j)
        rhat = rhat_ref[:, j * SLAB : (j + 1) * SLAB].astype(F32)
        dres = dy_ref[:, at].astype(F32) + scale * (scaled[j] - rhat * mean)
        if j == 0:
            dres_ref[...] = dres
        low = dres.astype(BF16)
        dres16_ref[:, at] = low
        dz = dz + nn(low, wo_ref[at, :])
    where = lax.broadcasted_iota(jnp.int32, (BLOCK, DV), 0) + base
    u = jnp.where(where < ends[-1], dz, 0.0)
    mixed = mixed_ref[...]
    head_scale = lax.rsqrt(jnp.mean(mixed * mixed, axis=-1, keepdims=True) + NORM_EPS)
    hat = mixed * head_scale
    gate = gout_ref[...]
    sig = jax.nn.sigmoid(gate)
    act = gate * sig
    uhat = u * hat
    go = go_ref[...]
    sums_out_ref[HEAD_ROW : HEAD_ROW + 1, :DV] += jnp.sum(uhat * act, axis=0, keepdims=True)
    dall_ref[:, 2 * DK + DV : MAIN] = (uhat * go * (sig * (1.0 + gate * (1.0 - sig)))).astype(BF16)
    dhat = u * go * act
    dmix = head_scale * (dhat - hat * jnp.mean(dhat * hat, axis=-1, keepdims=True))
    dmix = (dmix * OUT_SCALE).astype(BF16)
    zeta = zeta_ref[...]
    forget = log_sigmoid(zeta) * (1.0 / GATE_NORM)
    slope = jax.nn.sigmoid(-zeta) * (1.0 / GATE_NORM)
    dstate = dstate_out_ref[...]
    after = next_out_ref[...]
    head_at = meta[0] * DK
    for i in reversed(range(BLOCK // CHUNK)):
        rows = slice(i * CHUNK, (i + 1) * CHUNK)
        queries = qkv_ref[rows, :DK].astype(F32)
        keys = qkv_ref[rows, DK : 2 * DK].astype(F32)
        values = qkv_ref[rows, 2 * DK :]
        masks, factors, parts, scores = chunk_terms(
            queries, keys, forget[rows], base + i * CHUNK, ends
        )
        row, col, near, far = masks
        grow, shrink, edge, from_start, to_end, decay_step = factors
        q_near, k_near, q_far, k_far, q_state, k_state = parts
        state = states_ref[i * DV : (i + 1) * DV, :]
        do = dmix[rows]
        dstate_low = dstate.astype(BF16)
        dscores = nt(do, values)
        dnear = jnp.where(near, dscores, 0.0).astype(BF16)
        dfar = jnp.where(far, dscores, 0.0).astype(BF16)
        dv = tn(scores, do) + nt(k_state, dstate_low)
        dq = nn(do, state) * from_start + nn(dnear, k_near) * grow
        dq = dq + jnp.where(row >= SPAN, nn(dfar, k_far) * edge, 0.0)
        dk = nn(values, dstate_low) * to_end + tn(dnear, q_near) * shrink
        dk = dk + jnp.where(row < SPAN, tn(dfar, q_far) * edge, 0.0)
        dall_ref[rows, :DK] = dq.astype(BF16)
        dall_ref[rows, DK : 2 * DK] = dk.astype(BF16)
        dall_ref[rows, 2 * DK : 2 * DK + DV] = dv.astype(BF16)
        at_end = jnp.sum(dstate * after.astype(F32), axis=0, keepdims=True)
        ddecay = queries * dq - keys * dk
        dforget = prefix_sums(ddecay, jnp.where(col >= row, 1.0, 0.0).astype(BF16)) + at_end
        dzeta = (dforget * slope[rows]).astype(BF16)
        sums_out_ref[HEAD_ROW : HEAD_ROW + 1, lanes_at(DV + head_at)] += jnp.sum(
            dzeta.astype(F32), axis=0, keepdims=True
        )
        dlowout = tn(lowr_ref[rows, :], dzeta)
        for k in range(2):
            sums_out_ref[LOWOUT_ROW:, lanes_at(k * (D // 2) + head_at)] += dlowout[k * 8 : (k + 1) * 8]
        dall_ref[rows, MAIN:] = nt(dzeta, wb_ref[...]).astype(BF16)
        dstate = dstate * decay_step + tn(do, q_state)
        after = state
    dstate_out_ref[...] = dstate
    next_out_ref[...] = after
    dall = dall_ref[...]
    sums_out_ref[LOWIN_ROW : LOWIN_ROW + RANK, :] += tn(dall[:, MAIN:], xn_ref[...])[:RANK]
    x = x_ref[...].astype(F32)
    in_scale = lax.rsqrt(jnp.mean(x * x, axis=-1, keepdims=True) + NORM_EPS)
    for j in range(SLABS):
        at = slab_at(meta, j)
        part = nt(dall, w_ref[at, :])
        sums_out_ref[IN_ROW : IN_ROW + 1, at] += jnp.sum(
            part * (x_ref[:, at].astype(F32) * in_scale), axis=0, keepdims=True
        )
        target = keep_ref if j < 2 else send_ref
        target[:, (j % 2) * SLAB : (j % 2 + 1) * SLAB] = part.astype(BF16)


def feed_grad_kernel(first_ref, second_ref, *refs):
    refs[-1][...] = tn(first_ref[...], second_ref[...]).astype(BF16)


def attn_grad_kernel(row_ref, xn_ref, dres_ref, dall_ref, z_ref, here_ref, away_ref, both_ref):
    both_ref[:, :MAIN] = tn(xn_ref[...], dall_ref[:, :MAIN])
    both_ref[:, MAIN:] = tn(dres_ref[...], z_ref[...])
    rows = here_ref.shape[1]
    row = row_ref[0]
    here_ref[0] = both_ref[pl.ds(pl.multiple_of(row * rows, rows), rows), :].astype(BF16)
    away_ref[0] = both_ref[pl.ds(pl.multiple_of((1 - row) * rows, rows), rows), :].astype(BF16)


def update_kernel(clip_ref, attn_ref, feed_ref, *refs):
    masters, firsts, seconds = refs[:5], refs[5:10], refs[10:15]
    outs, turned, turned_attn = refs[15:30], refs[30], refs[31]
    step = pl.program_id(0)

    @pl.when(step == 0)
    def _():
        turned[...] = feed_ref[...].astype(F32).T
        turned_attn[...] = attn_ref[:, MAIN:].T

    clip = clip_ref[0]
    width = feed_ref.shape[1] // 3

    def rows(count):
        if count == attn_ref.shape[0]:
            return slice(None)
        return pl.ds(pl.multiple_of(step * count, 8), count)

    def units(k):
        count = masters[4].shape[0]
        return turned[pl.ds(pl.multiple_of(k * width + step * count, 8), count), :]

    attn = attn_ref[rows(masters[0].shape[1]), :]
    across = masters[2].shape[0]
    grads = (
        (attn[:, :DK], attn[:, DK : 2 * DK]),
        (attn[:, 2 * DK : 2 * DK + DV], attn[:, 2 * DK + DV : MAIN]),
        (turned_attn[pl.ds(pl.multiple_of(step * across, 8), across), :],),
        (units(0), units(1)),
        (units(2),),
    )
    rates = (D, D, HEADS * DV, D, FF)
    for i in range(5):
        for k, grad in enumerate(grads[i]):
            at = k if len(grads[i]) > 1 else Ellipsis
            results = adam_step(
                masters[i][at], grad, firsts[i][at], seconds[i][at], clip, 2.0 * rates[i] ** (-0.5), WEIGHT_DECAY
            )
            for n in range(3):
                outs[n * 5 + i][at] = results[n]


def whole(array):
    zeros = (0,) * array.ndim
    return pl.BlockSpec(array.shape, lambda i, meta: zeros, pipeline_mode=pl.Buffered(1))


def fixed(shape):
    return pl.BlockSpec(shape, lambda i, meta: (0,) * len(shape))


def rows_at(rows, width, place):
    return pl.BlockSpec((rows, width), lambda i, meta: (place(i), 0))


def like(shape, dtype):
    return jax.ShapeDtypeStruct(shape, dtype)


def params():
    return pltpu.CompilerParams(vmem_limit_bytes=VMEM_LIMIT)


def run_kernel(body, meta, steps, ins, in_specs, saved, outs, out_specs, saved_like, saved_specs, name, flops):
    given = [] if saved is None else list(saved)
    aliases = {1 + len(ins) + i: len(outs) + i for i in range(len(given))}
    result = pl.pallas_call(
        functools.partial(body, len(given)),
        grid_spec=pltpu.PrefetchScalarGridSpec(
            num_scalar_prefetch=1,
            grid=(steps,),
            in_specs=list(in_specs) + [pl.BlockSpec(memory_space=pl.ANY)] * len(given),
            out_specs=list(out_specs) + list(saved_specs),
        ),
        out_shape=list(outs) + list(saved_like),
        input_output_aliases=aliases,
        compiler_params=params(),
        cost_estimate=pl.CostEstimate(flops=flops, bytes_accessed=16 * 1024 * 1024, transcendentals=0),
        name=name,
    )(meta, *ins, *given)
    return list(result[: len(outs)]), list(result[len(outs) :])


def attend(piece, meta, x, w, wo, wb, g1, go, c, state, saved):
    tokens = x.shape[0]
    size = tokens // PIECES
    steps = size // BLOCK
    first = piece * steps
    here = lambda i: first + i
    ins = [x, w, wo, wb, g1, go, c, state]
    in_specs = [rows_at(BLOCK, D, here)] + [whole(a) for a in ins[1:]]
    outs = [like((size, D), BF16), like(state.shape, F32)]
    out_specs = [rows_at(BLOCK, D, lambda i: i), fixed(state.shape)]
    widths = [
        (D, BF16),
        (2 * DK + DV, BF16),
        (DV, F32),
        (LANES, BF16),
        (DK, F32),
        (DV, F32),
        (DV, BF16),
    ]
    saved_like = [like((tokens, n), d) for n, d in widths]
    saved_specs = [rows_at(BLOCK, n, here) for n, _ in widths]
    saved_like.append(like((tokens // CHUNK * DV, DK), BF16))
    saved_specs.append(rows_at(BLOCK // CHUNK * DV, DK, here))
    return run_kernel(
        functools.partial(attend_kernel, first),
        meta, steps, ins, in_specs, saved, outs, out_specs, saved_like, saved_specs,
        "attend", size * 8 * D * 1024,
    )


def feed(piece, meta, x, terms, dys, wf, g2, saved):
    tokens = x.shape[0]
    size = tokens // PIECES
    steps = size // BLOCK
    first = piece * steps
    here = lambda i: first + i
    width = wf.shape[1] // 3
    ins = [x, *terms, *dys, wf, g2]
    in_specs = (
        [rows_at(BLOCK, D, here)]
        + [rows_at(BLOCK, a.shape[1], lambda i: i) for a in terms]
        + [rows_at(BLOCK, SLAB, here)] * SLABS
        + [whole(wf), whole(g2)]
    )
    outs = [like((size, D), BF16)]
    out_specs = [rows_at(BLOCK, D, lambda i: i)]
    widths = [
        (2 * SLAB, BF16),
        (2 * SLAB, BF16),
        (D, BF16),
        (D, BF16),
        (width, BF16),
        (2 * width, BF16),
        (D, BF16),
        (LANES, F32),
        (SLAB, F32),
    ]
    saved_like = [like((tokens, n), d) for n, d in widths]
    saved_specs = [rows_at(BLOCK, n, here) for n, _ in widths]
    return run_kernel(
        feed_kernel,
        meta, steps, ins, in_specs, saved, outs, out_specs, saved_like, saved_specs,
        "feed", size * 2 * D * width * 6,
    )


def back(piece, meta, terms, dy, rhat, rs, x, xn, kept, w, wo, wb, g2, go, carried, saved):
    tokens = x.shape[0]
    size = tokens // PIECES
    steps = size // BLOCK
    last = (piece + 1) * steps - 1
    here = lambda i: last - i
    local = lambda i: steps - 1 - i
    ins = [*terms, dy, rhat, rs, x, xn, *kept, w, wo, wb, g2, go, *carried]
    in_specs = (
        [rows_at(BLOCK, a.shape[1], local) for a in terms]
        + [rows_at(BLOCK, a.shape[1], here) for a in (dy, rhat, rs, x, xn)]
        + [rows_at(BLOCK, a.shape[1], here) for a in kept[:-1]]
        + [rows_at(BLOCK // CHUNK * DV, DK, here)]
        + [whole(a) for a in (w, wo, wb, g2, go, *carried)]
    )
    outs = [like((size, 2 * SLAB), BF16)] * 2 + [like(a.shape, a.dtype) for a in carried]
    out_specs = [rows_at(BLOCK, 2 * SLAB, local)] * 2 + [fixed(a.shape) for a in carried]
    widths = [(D, BF16), (SLAB, F32), (ATTN, BF16)]
    saved_like = [like((tokens, n), d) for n, d in widths]
    saved_specs = [rows_at(BLOCK, n, here) for n, _ in widths]
    return run_kernel(
        functools.partial(back_kernel, last),
        meta, steps, ins, in_specs, saved, outs, out_specs, saved_like, saved_specs,
        "back", size * 12 * D * 1024,
    )


def feed_grad(first, second, column, full):
    tokens, width = second.shape
    ins = [first, second] + ([] if full is None else [full])
    return pl.pallas_call(
        feed_grad_kernel,
        grid=(D // SLAB,),
        in_specs=[
            pl.BlockSpec((tokens, SLAB), lambda i: (0, i)),
            pl.BlockSpec((tokens, width), lambda i: (0, 0), pipeline_mode=pl.Buffered(1)),
        ]
        + [pl.BlockSpec(memory_space=pl.ANY)] * (len(ins) - 2),
        out_specs=pl.BlockSpec((SLAB, width), lambda i: (i, column)),
        out_shape=like((D, FEED_COLS), BF16),
        input_output_aliases={2: 0} if len(ins) > 2 else {},
        compiler_params=params(),
        cost_estimate=pl.CostEstimate(
            flops=4 * D * tokens * width, bytes_accessed=8 * 1024 * 1024, transcendentals=0
        ),
        name="feed_grad",
    )(*ins)


def attn_grad(row, xn, dres16, dall, z):
    tokens = xn.shape[0]
    half = SLAB // 2
    column = lambda i, row: (0, i)
    return pl.pallas_call(
        attn_grad_kernel,
        grid_spec=pltpu.PrefetchScalarGridSpec(
            num_scalar_prefetch=1,
            grid=(SLABS,),
            in_specs=[pl.BlockSpec((tokens, SLAB), column)] * 2 + [whole(dall), whole(z)],
            out_specs=[pl.BlockSpec((1, half, D), lambda i, row: (i, 0, 0))] * 2,
            scratch_shapes=[pltpu.VMEM((SLAB, D), F32)],
        ),
        out_shape=[like((SLABS, half, D), BF16)] * 2,
        compiler_params=params(),
        cost_estimate=pl.CostEstimate(
            flops=4 * D * tokens * D, bytes_accessed=8 * 1024 * 1024, transcendentals=0
        ),
        name="attn_grad",
    )(row, xn, dres16, dall, z)


def update(clip, attn, feed, arrays):
    rows = attn.shape[0]
    steps = 4 if rows % 32 == 0 else 1
    masters = arrays[:5]

    def cut(array):
        shape = list(array.shape)
        shape[-2] //= steps
        zeros = (0,) * (len(shape) - 2)
        return pl.BlockSpec(tuple(shape), lambda i: (*zeros, i, 0))

    return pl.pallas_call(
        update_kernel,
        grid=(steps,),
        in_specs=[pl.BlockSpec(memory_space=pltpu.SMEM)]
        + [pl.BlockSpec(a.shape, lambda i: (0, 0), pipeline_mode=pl.Buffered(1)) for a in (attn, feed)]
        + [cut(a) for a in arrays],
        out_specs=[cut(a) for a in masters] * 3,
        out_shape=[like(a.shape, F32) for a in masters] * 3,
        scratch_shapes=[pltpu.VMEM((feed.shape[1], rows), F32), pltpu.VMEM((DV, rows), F32)],
        compiler_params=params(),
        name="update",
    )(clip, attn, feed, *arrays)


def after(array, *others):
    return lax.optimization_barrier((array, *others))[0]


def swap(array, axis, bit):
    return lax.ppermute(array, axis, [(i, i ^ bit) for i in range(lax.axis_size(axis))])


def swap_core(array):
    return swap(array, "tensor", 1)


def swap_far(array):
    return swap(array, "tensor", 2)


def swap_row(array):
    return swap(array, "dp", 1)


def shift_layer(array, by):
    count = lax.axis_size("dp")
    return lax.ppermute(array, "dp", [(i, (i + 2 * by) % count) for i in range(count)])


def gather_attn(own):
    dp_at = lax.axis_index("dp")
    found = {(0, 0): own, (1, 0): shift_layer(own, 1), (3, 0): shift_layer(own, 3), (0, 1): swap_row(own)}
    first = list(found.values())[1:]
    found[2, 0] = shift_layer(after(own, *first), 2)
    for k in (1, 3):
        found[k, 1] = swap_row(after(found[k, 0], *first))
    second = [found[2, 0], found[1, 1], found[3, 1]]
    found[2, 1] = swap_row(after(*second))
    places = [((dp_at - 2 * k) % (2 * SLABS)) ^ h for k, h in found]
    pieces = list(found.values())
    rows = D
    return second, pl.pallas_call(
        assemble_kernel,
        in_specs=[pl.BlockSpec(memory_space=pltpu.SMEM)]
        + [pl.BlockSpec(memory_space=pltpu.VMEM)] * (2 * SLABS),
        out_shape=(like((rows, ATTN), BF16), like((rows, DV), BF16), like((LANES, DK), BF16)),
        compiler_params=params(),
        name="assemble",
    )(jnp.stack(places).astype(jnp.int32), *pieces)


def gather_plain(own):
    count, rows = lax.axis_size("dp"), own.shape[0]
    full = lax.all_gather(own, "dp", axis=0, tiled=True)
    keys = DK // count
    blocks = full.reshape(count, rows, -1)[:, :RANK, MAIN + RANK : MAIN + RANK + keys]
    wb = jnp.pad(blocks.transpose(1, 0, 2).reshape(RANK, DK), ((0, LANES - RANK), (0, 0)))
    return [own], (full[:, :ATTN], full[:, ATTN:], wb)


def scatter_attn(here, away):
    dp_at = lax.axis_index("dp")
    high, low = dp_at // 4, (dp_at // 2) % 2
    rows, width = here.shape[1:]

    def pick(array, axis, index):
        return lax.dynamic_index_in_dim(array, index, axis, keepdims=False)

    first = here.astype(F32) + swap_row(away).astype(F32)
    here = first.reshape(2, 2, rows, width)
    away = pick(here, 1, 1 - low).astype(BF16)
    here = pick(here, 1, low) + swap(away, "dp", 2).astype(F32)
    away = pick(here, 0, 1 - high).astype(BF16)
    return first, pick(here, 0, high) + swap(away, "dp", 4).astype(F32)


def sum_terms(part, earlier):
    core = swap_core(after(part, *earlier))
    own = (part[:, : 2 * SLAB].astype(F32) + core[:, 2 * SLAB :].astype(F32)).astype(BF16)
    return own, part, core, swap_far(own)


def slab_sum(keep, send, earlier):
    own = keep.astype(F32) + swap_core(send).astype(F32)
    far = swap_far(after(own[:, SLAB:].astype(BF16), earlier))
    return own[:, :SLAB] + far.astype(F32), far


def sum_everywhere(array, axes=("tensor", "dp")):
    for axis in axes:
        size = lax.axis_size(axis)
        bit = 1
        while bit < size:
            array = array + swap(array, axis, bit)
            bit *= 2
    return array


def adam_step(weight, gradient, first_moment, second_moment, clip_factor, learn_rate, weight_decay):
    clipped = gradient * clip_factor
    momentum = BETA_FIRST * first_moment + (1.0 - BETA_FIRST) * clipped
    variance = BETA_SECOND * second_moment + (1.0 - BETA_SECOND) * clipped * clipped
    step_size = (
        momentum
        / (1.0 - BETA_FIRST**STEP)
        / (jnp.sqrt(variance / (1.0 - BETA_SECOND**STEP)) + ADAM_EPS)
    )
    updated = weight * (1.0 - learn_rate * weight_decay) - learn_rate * step_size
    return (momentum, variance, updated)


LARGE = (0, 1, 4, 5, 6)


def body(*args):
    inputs, cotangent, doc_lengths = args[:3]
    masters, firsts, seconds = args[3:11], args[11:19], args[19:27]
    weight_qk, weight_vg, weight_lowin, weight_lowout, weight_mixout, weight_gateup, weight_down = masters[:7]
    weight_small = masters[7]
    tensor_at = lax.axis_index("tensor")
    dp_at = lax.axis_index("dp")
    layered = lax.axis_size("dp") == 2 * SLABS
    rows_here = weight_qk.shape[1]
    ranks, _, keys_here = weight_lowout.shape
    turn = lambda i, a: jnp.swapaxes(a, 1, 2) if i == 5 else a
    far_cot = swap_far(cotangent)

    attn_pack, feed_pack = pl.pallas_call(
        pack_kernel,
        out_shape=(like((rows_here, ATTN + DV), BF16), like((rows_here, FEED_COLS), BF16)),
        compiler_params=params(),
        name="pack",
    )(
        weight_qk, weight_vg, weight_lowin.T, weight_lowout[:, 0, :], weight_mixout,
        turn(5, weight_gateup), weight_down,
    )
    arrived, (w, wo, wb) = (gather_attn if layered else gather_plain)(attn_pack)
    wf = lax.all_gather(after(feed_pack, *arrived), "dp", axis=0, tiled=True)
    doc_ends = jnp.cumsum(doc_lengths[0])
    slots = jnp.stack([tensor_at ^ o for o in ORDER])
    meta = jnp.concatenate([slots.astype(jnp.int32), doc_ends.astype(jnp.int32)])

    g1, g2 = weight_small[:D].reshape(1, D), weight_small[D : 2 * D].reshape(1, D)
    go = weight_small[2 * D : 2 * D + DV].reshape(1, DV)
    gate_bias = lax.dynamic_slice_in_dim(weight_small, 2 * D + DV + tensor_at * DK, DK).reshape(1, DK)
    x = inputs
    meta = after(meta, far_cot)
    dys = [cotangent, far_cot, swap_core(after(cotangent, w)), swap_core(after(far_cot, w))]

    state = jnp.zeros((DV, DK), F32)
    saved = None
    terms = []
    earlier = []
    for piece in range(PIECES):
        (part, state), saved = attend(piece, meta, x, w, wo, wb, g1, go, gate_bias, state, saved)
        own, part, core, far = sum_terms(part, earlier)
        terms.append((part, core, far, swap_core(far)))
        earlier = [far]
        state = after(state, own)
    xn, *kept = saved
    z = kept.pop(5)

    fed = None
    back_terms = []
    order = after(meta, own)
    for piece in range(PIECES):
        (part,), fed = feed(piece, order, x, terms[piece], dys, wf, g2, fed)
        own, part, core, far = sum_terms(part, earlier)
        earlier = [far]
        order = after(meta, own)
        if piece < PIECES - 1:
            back_terms.append((part, core, far, swap_core(far)))
    feed_keep, feed_send, hn, dy, hidden, dgu, rhat, rs, resid = fed
    fed_own = (feed_keep.astype(F32) + swap_core(feed_send).astype(F32)).astype(BF16)
    grad_feed = feed_grad(dy, hidden, 2, None)
    grad_feed = feed_grad(after(hn, own, fed_own), dgu, 0, grad_feed)
    back_terms.append((part, core, far, swap_core(after(far, grad_feed))))
    shard_feed = lax.psum_scatter(grad_feed, "dp", scatter_dimension=0, tiled=True)
    fed_far = swap_far(after(fed_own[:, SLAB:], far))
    output = (resid + (fed_own[:, :SLAB].astype(F32) + fed_far.astype(F32))).astype(BF16)

    carried = [jnp.zeros((DV, DK), F32), jnp.zeros((DV, DK), BF16), jnp.zeros((SUM_ROWS, D), F32)]
    backed = None
    dxn = []
    order = after(meta, grad_feed)
    for piece in reversed(range(PIECES)):
        (keep, send, *carried), backed = back(
            piece, order, back_terms[piece], dy, rhat, rs, x, xn, kept, w, wo, wb, g2, go, carried, backed
        )
        if piece == PIECES - 1:
            order = meta
        dxn.insert(0, (keep, send))
    dres16, dres, dall = backed
    row_at = (dp_at % 2 if layered else jnp.zeros_like(dp_at)).astype(jnp.int32).reshape(1)
    here, away = attn_grad(row_at, xn, dres16, dall, z)
    earlier = fed_far
    for piece in reversed(range(PIECES)):
        keep, send = dxn[piece]
        dxn[piece], earlier = slab_sum(keep, after(send, here), earlier)
    if layered:
        half_summed, shard_attn = scatter_attn(here, away)
    else:
        half_summed = here
        shard_attn = lax.psum_scatter(
            jnp.stack([here, away], axis=1).reshape(D, D), "dp", scatter_dimension=0, tiled=True
        ).astype(F32)

    dxn = jnp.concatenate(dxn, axis=0)
    x_wide = x.astype(F32)
    in_scale = lax.rsqrt(jnp.mean(x_wide * x_wide, axis=-1, keepdims=True) + NORM_EPS)
    hat_here = lax.dynamic_slice_in_dim(x, tensor_at * SLAB, SLAB, 1).astype(F32) * in_scale
    scaled = dxn * lax.dynamic_slice_in_dim(g1, tensor_at * SLAB, SLAB, 1)
    row_sums = jnp.sum(scaled * hat_here, axis=-1).reshape(-1, LANES)
    row_mean = sum_everywhere(row_sums, ("tensor",)).reshape(-1, 1) / D
    input_grad = dres + in_scale * (scaled - hat_here * row_mean)

    wide = sum_everywhere(after(carried[2], half_summed))
    small_grad = jnp.concatenate([wide[IN_ROW], wide[MID_ROW], wide[HEAD_ROW, : DV + HEADS * DK]])
    grad_lowin = lax.dynamic_slice(wide, (LOWIN_ROW, dp_at * rows_here), (RANK, rows_here)).T
    lowout = jnp.concatenate([wide[LOWOUT_ROW:, : D // 2], wide[LOWOUT_ROW:, D // 2 :]], axis=0)
    grad_lowout = lax.dynamic_slice(
        lowout, (0, tensor_at * DK + dp_at * keys_here), (RANK, keys_here)
    ).reshape(weight_lowout.shape)

    squares = sum(jnp.sum(jnp.square(s.astype(F32))) for s in (shard_feed, shard_attn))
    square_total = sum_everywhere(jnp.broadcast_to(squares, (8, LANES)))[0, 0]
    grad_norm = jnp.sqrt(square_total + jnp.sum(wide * wide))
    clip_factor = jnp.minimum(1.0, CLIP_NORM / (grad_norm + 1e-06))
    arrays = [turn(i, group[i]) for group in (masters, firsts, seconds) for i in LARGE]
    large = update(clip_factor.reshape(1), shard_attn, shard_feed, arrays)
    small_rate = jnp.where(
        lax.broadcasted_iota(jnp.int32, weight_small.shape, 0) < 2 * D + DV, GAIN_RATE, BIAS_RATE
    )
    steps = {}
    for k, i in enumerate(LARGE):
        steps[i] = [turn(i, a) for a in large[k::5]]
    for i, grad, rate, decay in (
        (2, grad_lowin, 2.0 * D ** (-0.5), WEIGHT_DECAY),
        (3, grad_lowout, 2.0 * RANK ** (-0.5), WEIGHT_DECAY),
        (7, small_grad, small_rate, 0.0),
    ):
        steps[i] = adam_step(masters[i], grad, firsts[i], seconds[i], clip_factor, rate, decay)
    return (output, input_grad, grad_norm.reshape(1), *(steps[i][k] for k in range(3) for i in range(8)))


def solution(mesh):
    weights = (
        P(None, "dp", "tensor"),
        P(None, "dp", "tensor"),
        P("dp", None),
        P(None, "tensor", "dp"),
        P("tensor", "dp"),
        P(None, "dp", "tensor"),
        P("tensor", "dp"),
        P(),
    )
    return jax.shard_map(
        body,
        mesh=mesh,
        in_specs=(P("dp", None), P("dp", "tensor"), P("dp", None), *weights, *weights, *weights),
        out_specs=(P("dp", "tensor"), P("dp", "tensor"), P(), *weights, *weights, *weights),
        check_vma=False,
    )
```

```python
import functools

import jax
import jax.numpy as jnp
from jax import lax
from jax.experimental import pallas as pl
from jax.experimental.pallas import tpu as pltpu
from jax.sharding import PartitionSpec as P

D = 1024
HEADS = 4
DK = 128
DV = 256
RANK = 16
FF = 2816
SPAN = 64
SEQ_LEN = 2048
STEP = 10

NORM_EPS = 1e-06
GATE_NORM = 16.0
BETA_FIRST = 0.9
BETA_SECOND = 0.95
ADAM_EPS = 1e-08
WEIGHT_DECAY = 0.1
CLIP_NORM = 1.0
GAIN_RATE = 2.5
BIAS_RATE = 4.0

F32 = jnp.float32
BF16 = jnp.bfloat16
LANES = 128
SLAB = 256
SLABS = 4
CHUNK = 2 * SPAN
BLOCK = 256
PIECES = 2
ORDER = (0, 2, 1, 3)
QKV = 512
QKVL = 640
ATTN = 896
MAIN = 768
FEED_COLS = 3 * 768
OUT_SCALE = DK**-0.5
VMEM_LIMIT = 60 * 1024 * 1024


def nn(a, b):
    return lax.dot_general(a, b, (((1,), (0,)), ((), ())), preferred_element_type=F32)


def nt(a, b):
    return lax.dot_general(a, b, (((1,), (1,)), ((), ())), preferred_element_type=F32)


def tn(a, b):
    return lax.dot_general(a, b, (((0,), (0,)), ((), ())), preferred_element_type=F32)


def doc_at(position, ends):
    number = jnp.zeros_like(position)
    for end in ends:
        number = number + jnp.where(position >= end, 1, 0)
    return number


def log_sigmoid(values):
    return jnp.minimum(values, 0.0) - jnp.log1p(jnp.exp(-jnp.abs(values)))


def prefix_sums(values, triangle):
    high = values.astype(BF16)
    low = (values - high.astype(F32)).astype(BF16)
    width = values.shape[1]
    both = nn(triangle, jnp.concatenate([high, low], axis=1))
    return both[:, :width] + both[:, width:]


def chunk_terms(queries, keys, forget, base, ends):
    row = lax.broadcasted_iota(jnp.int32, (CHUNK, CHUNK), 0)
    col = lax.broadcasted_iota(jnp.int32, (CHUNK, CHUNK), 1)
    decay = prefix_sums(forget, jnp.where(col <= row, 1.0, 0.0).astype(BF16))
    seg_row = doc_at(row + base, ends)
    same = seg_row == doc_at(col + base, ends)
    upper = row >= SPAN
    near = same & (col <= row) & (upper == (col >= SPAN))
    far = same & upper & (col < SPAN)
    before = jnp.where(base > 0, doc_at(base - 1, ends), -1)
    final = doc_at(base + CHUNK - 1, ends)
    alive = jnp.where(seg_row == before, 1.0, 0.0)
    keep = jnp.where(seg_row == final, 1.0, 0.0)
    carry = jnp.where(before == final, 1.0, 0.0)
    mid = jnp.where(upper, decay[SPAN + SPAN // 2 :][:1], decay[SPAN // 2 :][:1])
    grow = jnp.exp(decay - mid)
    shrink = jnp.exp(mid - decay)
    edge = jnp.exp(-jnp.abs(decay - decay[SPAN - 1 : SPAN]))
    from_start = jnp.exp(decay) * alive
    last = decay[CHUNK - 1 : CHUNK]
    to_end = jnp.exp(last - decay) * keep
    step = jnp.exp(last) * carry
    q_near = (queries * grow).astype(BF16)
    k_near = (keys * shrink).astype(BF16)
    q_far = (queries * edge).astype(BF16)
    k_far = (keys * edge).astype(BF16)
    q_state = (queries * from_start).astype(BF16)
    k_state = (keys * to_end).astype(BF16)
    scores = jnp.where(near, nt(q_near, k_near), jnp.where(far, nt(q_far, k_far), 0.0)).astype(BF16)
    return (
        (row, col, near, far),
        (grow, shrink, edge, from_start, to_end, step),
        (q_near, k_near, q_far, k_far, q_state, k_state),
        scores,
    )


def slab_at(meta, j):
    return pl.ds(pl.multiple_of(meta[j] * SLAB, SLAB), SLAB)


def lanes_at(start):
    return pl.ds(pl.multiple_of(start, LANES), LANES)


def one_hot(rows, shift):
    row = lax.broadcasted_iota(jnp.int32, (rows, LANES), 0)
    col = lax.broadcasted_iota(jnp.int32, (rows, LANES), 1)
    return jnp.where(col - row == shift, 1.0, 0.0).astype(BF16)


def pack_kernel(qk_ref, vg_ref, lowin_ref, lowout_ref, mixout_ref, gateup_ref, down_ref, attn_ref, feed_ref):
    units = gateup_ref.shape[1]
    width = feed_ref.shape[1] // 3
    attn_ref[:, :DK] = qk_ref[0].astype(BF16)
    attn_ref[:, DK : 2 * DK] = qk_ref[1].astype(BF16)
    attn_ref[:, 2 * DK : 2 * DK + DV] = vg_ref[0].astype(BF16)
    attn_ref[:, QKV:QKVL] = tn(lowin_ref[...].astype(BF16), one_hot(RANK, 0)).astype(BF16)
    lowout = lowout_ref[...].astype(BF16)
    attn_ref[:RANK, QKV:QKVL] += nn(lowout, one_hot(lowout.shape[1], RANK)).astype(BF16)
    attn_ref[:, QKVL:ATTN] = vg_ref[1].astype(BF16)
    attn_ref[:, ATTN:] = mixout_ref[...].T.astype(BF16)
    rows = feed_ref.shape[0]
    pad = jnp.zeros((rows, width - units), BF16)
    feed_ref[:, :units] = gateup_ref[0].T.astype(BF16)
    feed_ref[:, units:width] = pad
    feed_ref[:, width : width + units] = gateup_ref[1].T.astype(BF16)
    feed_ref[:, width + units : 2 * width] = pad
    feed_ref[:, 2 * width : 2 * width + units] = down_ref[...].T.astype(BF16)
    feed_ref[:, 2 * width + units :] = pad


def assemble_kernel(place, *refs):
    pieces = refs[: 2 * SLABS]
    w_ref, wo_ref, wb_ref = refs[2 * SLABS :]
    rows = pieces[0].shape[0]
    keys = DK // (2 * SLABS)
    wb_ref[...] = jnp.zeros_like(wb_ref)
    for i, piece in enumerate(pieces):
        block = place[i]
        at = pl.ds(pl.multiple_of(block * rows, rows), rows)
        w_ref[at, :] = piece[:, :ATTN]
        wo_ref[at, :] = piece[:, ATTN:]
        row = lax.broadcasted_iota(jnp.int32, (LANES, DK), 0)
        col = lax.broadcasted_iota(jnp.int32, (LANES, DK), 1)
        inside = (row >= RANK) & (row < RANK + keys)
        move = jnp.where(inside & (col - row == block * keys - RANK), 1.0, 0.0).astype(BF16)
        wb_ref[:RANK, :] += nn(piece[:RANK, QKV:QKVL], move).astype(BF16)


def attend_kernel(first_block, n_saved, meta, *refs):
    x_ref, w_ref, wo_ref, wb_ref, g1_ref, go_ref, c_ref, state_ref = refs[:8]
    refs = refs[8 + n_saved :]
    part_ref, state_out_ref = refs[:2]
    xn_ref, qkv_ref, gout_ref, lowr_ref, zeta_ref, mixed_ref, z_ref, states_ref = refs[2:]
    step = pl.program_id(0)

    @pl.when(step == 0)
    def _():
        state_out_ref[...] = state_ref[...]

    ends = [meta[META_ENDS + i] for i in range(meta.shape[0] - META_ENDS)]
    x = x_ref[...].astype(F32)
    scale = lax.rsqrt(jnp.mean(x * x, axis=-1, keepdims=True) + NORM_EPS)
    normed = (x * scale * g1_ref[...]).astype(BF16)
    xn_ref[...] = normed
    proj = nn(normed, w_ref[...])
    qkv = proj[:, :QKV].astype(BF16)
    qkv_ref[...] = qkv
    gout = proj[:, QKVL:]
    gout_ref[...] = gout
    lowr = proj[:, QKV:QKVL].astype(BF16)
    lowr_ref[...] = lowr
    zeta = nn(lowr, wb_ref[...]) + c_ref[...]
    zeta_ref[...] = zeta
    forget = log_sigmoid(zeta) * (1.0 / GATE_NORM)
    base = (first_block + step) * BLOCK
    state = state_out_ref[...]
    for i in range(BLOCK // CHUNK):
        rows = slice(i * CHUNK, (i + 1) * CHUNK)
        queries = qkv[rows, :DK].astype(F32)
        keys = qkv[rows, DK : 2 * DK].astype(F32)
        values = qkv[rows, 2 * DK :]
        start = base + i * CHUNK
        _, factors, terms, scores = chunk_terms(queries, keys, forget[rows], start, ends)
        q_state, k_state = terms[4:]
        state_low = state.astype(BF16)
        states_ref[i * DV : (i + 1) * DV, :] = state_low
        mixed = (nn(scores, values) + nt(q_state, state_low)) * OUT_SCALE
        mixed_ref[rows, :] = mixed
        state = state * factors[5] + tn(values, k_state)
        where = lax.broadcasted_iota(jnp.int32, (CHUNK, DV), 0) + start
        valid = jnp.where(where < ends[-1], 1.0, 0.0)
        head_scale = lax.rsqrt(jnp.mean(mixed * mixed, axis=-1, keepdims=True) + NORM_EPS)
        gate = gout[rows]
        z = mixed * head_scale * go_ref[...] * (gate * jax.nn.sigmoid(gate)) * valid
        z_ref[rows, :] = z.astype(BF16)
    state_out_ref[...] = state
    z = z_ref[...]
    for j in range(SLABS):
        part_ref[:, j * SLAB : (j + 1) * SLAB] = nt(z, wo_ref[slab_at(meta, j), :]).astype(BF16)


def summed(j, mine, core, *beyond):
    other = (j + 2) % SLABS
    total = mine[:, j * SLAB : (j + 1) * SLAB].astype(F32)
    total = total + core[:, other * SLAB : (other + 1) * SLAB].astype(F32)
    k = 1 - j % 2
    if len(beyond) == 2:
        far = beyond[j // 2][:, k * SLAB : (k + 1) * SLAB]
    else:
        far = beyond[2 * (j // 2) + k][...]
    return total + far.astype(F32)


def feed_kernel(n_terms, n_saved, meta, *refs):
    x_ref, terms, refs = refs[0], refs[1 : 1 + n_terms], refs[1 + n_terms :]
    dys, wf_ref, g2_ref = refs[:SLABS], refs[SLABS], refs[SLABS + 1]
    refs = refs[SLABS + 2 + n_saved :]
    part_ref = refs[0]
    feed_keep_ref, feed_send_ref, hn_ref, dy_ref, hidden_ref, dgu_ref, rhat_ref, rs_ref, resid_ref = refs[1:]
    width = hidden_ref.shape[1]
    resid = []
    total = 0.0
    for j in range(SLABS):
        part = x_ref[:, slab_at(meta, j)].astype(F32) + summed(j, *terms)
        resid.append(part)
        total = total + jnp.sum(part * part, axis=-1, keepdims=True)
    resid_ref[...] = resid[0]
    scale = lax.rsqrt(total / D + NORM_EPS)
    rs_ref[...] = jnp.broadcast_to(scale, rs_ref.shape)
    units = 0.0
    dhid = 0.0
    for j in range(SLABS):
        at = slab_at(meta, j)
        rhat = resid[j] * scale
        rhat_ref[:, j * SLAB : (j + 1) * SLAB] = rhat.astype(BF16)
        hn = (rhat * g2_ref[:, at]).astype(BF16)
        hn_ref[:, at] = hn
        dy = dys[j][...]
        dy_ref[:, at] = dy
        units = units + nn(hn, wf_ref[at, : 2 * width])
        dhid = dhid + nn(dy, wf_ref[at, 2 * width :])
    gate = units[:, :width]
    up = units[:, width:]
    sig = jax.nn.sigmoid(gate)
    act = gate * sig
    hidden = (act * up).astype(BF16)
    hidden_ref[...] = hidden
    dgate = (dhid * up * (sig * (1.0 + gate * (1.0 - sig)))).astype(BF16)
    dup = (dhid * act).astype(BF16)
    dgu_ref[:, :width] = dgate
    dgu_ref[:, width:] = dup
    for j in range(SLABS):
        at = slab_at(meta, j)
        part = nt(dgate, wf_ref[at, :width]) + nt(dup, wf_ref[at, width : 2 * width])
        part_ref[:, j * SLAB : (j + 1) * SLAB] = part.astype(BF16)
        fed = nt(hidden, wf_ref[at, 2 * width :]).astype(BF16)
        target = feed_keep_ref if j < 2 else feed_send_ref
        target[:, (j % 2) * SLAB : (j % 2 + 1) * SLAB] = fed


META_TOKENS = SLABS
META_ENDS = SLABS + 1

LOWIN_ROW = 0
IN_ROW = 16
MID_ROW = 17
HEAD_ROW = 18
LOWOUT_ROW = 24
SUM_ROWS = 32


def turn_kernel(first_block, n_saved, meta, *refs):
    terms = refs[:4]
    dy_ref, rhat_ref, rs_ref, gout_ref, mixed_ref = refs[4:9]
    wo_ref, g2_ref, go_ref, sums_ref = refs[9:13]
    refs = refs[13 + n_saved :]
    sums_out_ref, dres16_ref, dres_ref, dgout_ref, dmix_ref = refs
    step = pl.program_id(0)

    @pl.when(step == 0)
    def _():
        sums_out_ref[...] = sums_ref[...]

    base = (first_block + step) * BLOCK
    scaled = []
    dot = 0.0
    for j in range(SLABS):
        dhn = summed(j, *terms)
        rhat = rhat_ref[:, j * SLAB : (j + 1) * SLAB].astype(F32)
        if j == 0:
            sums_out_ref[MID_ROW : MID_ROW + 1, slab_at(meta, 0)] += jnp.sum(
                dhn * rhat, axis=0, keepdims=True
            )
        part = dhn * g2_ref[:, slab_at(meta, j)]
        scaled.append(part)
        dot = dot + jnp.sum(part * rhat, axis=-1, keepdims=True)
    scale = rs_ref[:, :1]
    mean = dot / D
    dz = 0.0
    for j in range(SLABS):
        at = slab_at(meta, j)
        rhat = rhat_ref[:, j * SLAB : (j + 1) * SLAB].astype(F32)
        dres = dy_ref[:, at].astype(F32) + scale * (scaled[j] - rhat * mean)
        if j == 0:
            dres_ref[...] = dres
        low = dres.astype(BF16)
        dres16_ref[:, at] = low
        dz = dz + nn(low, wo_ref[at, :])
    where = lax.broadcasted_iota(jnp.int32, (BLOCK, DV), 0) + base
    u = jnp.where(where < meta[META_TOKENS], dz, 0.0)
    mixed = mixed_ref[...]
    head_scale = lax.rsqrt(jnp.mean(mixed * mixed, axis=-1, keepdims=True) + NORM_EPS)
    hat = mixed * head_scale
    gate = gout_ref[...]
    sig = jax.nn.sigmoid(gate)
    act = gate * sig
    uhat = u * hat
    go = go_ref[...]
    sums_out_ref[HEAD_ROW : HEAD_ROW + 1, :DV] += jnp.sum(uhat * act, axis=0, keepdims=True)
    dgout_ref[...] = (uhat * go * (sig * (1.0 + gate * (1.0 - sig)))).astype(BF16)
    dhat = u * go * act
    dmix = head_scale * (dhat - hat * jnp.mean(dhat * hat, axis=-1, keepdims=True))
    dmix_ref[...] = (dmix * OUT_SCALE).astype(BF16)


def back_kernel(last_block, n_saved, meta, *refs):
    dmix_ref, dgout_ref, x_ref, xn_ref = refs[:4]
    qkv_ref, lowr_ref, zeta_ref, states_ref = refs[4:8]
    w_ref, wb_ref = refs[8:10]
    dstate_ref, next_ref, sums_ref = refs[10:13]
    refs = refs[13 + n_saved :]
    keep_ref, send_ref, dstate_out_ref, next_out_ref, sums_out_ref, dall_ref = refs
    step = pl.program_id(0)

    @pl.when(step == 0)
    def _():
        dstate_out_ref[...] = dstate_ref[...]
        next_out_ref[...] = next_ref[...]
        sums_out_ref[...] = sums_ref[...]

    ends = [meta[META_ENDS + i] for i in range(meta.shape[0] - META_ENDS)]
    base = (last_block - step) * BLOCK
    zeta = zeta_ref[...]
    forget = log_sigmoid(zeta) * (1.0 / GATE_NORM)
    slope = jax.nn.sigmoid(-zeta) * (1.0 / GATE_NORM)
    dstate = dstate_out_ref[...]
    after_state = next_out_ref[...]
    head_at = meta[0] * DK
    for i in reversed(range(BLOCK // CHUNK)):
        rows = slice(i * CHUNK, (i + 1) * CHUNK)
        queries = qkv_ref[rows, :DK].astype(F32)
        keys = qkv_ref[rows, DK : 2 * DK].astype(F32)
        values = qkv_ref[rows, 2 * DK :]
        masks, factors, parts, scores = chunk_terms(
            queries, keys, forget[rows], base + i * CHUNK, ends
        )
        row, col, near, far = masks
        grow, shrink, edge, from_start, to_end, decay_step = factors
        q_near, k_near, q_far, k_far, q_state, k_state = parts
        state = states_ref[i * DV : (i + 1) * DV, :]
        do = dmix_ref[rows, :]
        dstate_low = dstate.astype(BF16)
        dscores = nt(do, values)
        dnear = jnp.where(near, dscores, 0.0).astype(BF16)
        dfar = jnp.where(far, dscores, 0.0).astype(BF16)
        dv = tn(scores, do) + nt(k_state, dstate_low)
        dq = nn(do, state) * from_start + nn(dnear, k_near) * grow
        dq = dq + jnp.where(row >= SPAN, nn(dfar, k_far) * edge, 0.0)
        dk = nn(values, dstate_low) * to_end + tn(dnear, q_near) * shrink
        dk = dk + jnp.where(row < SPAN, tn(dfar, q_far) * edge, 0.0)
        dall_ref[rows, :DK] = dq.astype(BF16)
        dall_ref[rows, DK : 2 * DK] = dk.astype(BF16)
        dall_ref[rows, 2 * DK : QKV] = dv.astype(BF16)
        at_end = jnp.sum(dstate * after_state.astype(F32), axis=0, keepdims=True)
        ddecay = queries * dq - keys * dk
        dforget = prefix_sums(ddecay, jnp.where(col >= row, 1.0, 0.0).astype(BF16)) + at_end
        dzeta = (dforget * slope[rows]).astype(BF16)
        sums_out_ref[HEAD_ROW : HEAD_ROW + 1, lanes_at(DV + head_at)] += jnp.sum(
            dzeta.astype(F32), axis=0, keepdims=True
        )
        dlowout = tn(lowr_ref[rows, :], dzeta)
        for k in range(2):
            sums_out_ref[LOWOUT_ROW:, lanes_at(k * (D // 2) + head_at)] += dlowout[k * 8 : (k + 1) * 8]
        dall_ref[rows, QKV:] = nt(dzeta, wb_ref[...]).astype(BF16)
        dstate = dstate * decay_step + tn(do, q_state)
        after_state = state
    dstate_out_ref[...] = dstate
    next_out_ref[...] = after_state
    dall = jnp.concatenate([dall_ref[...], dgout_ref[...]], axis=1)
    sums_out_ref[LOWIN_ROW : LOWIN_ROW + RANK, :] += tn(dall[:, QKV:QKVL], xn_ref[...])[:RANK]
    x = x_ref[...].astype(F32)
    in_scale = lax.rsqrt(jnp.mean(x * x, axis=-1, keepdims=True) + NORM_EPS)
    for j in range(SLABS):
        at = slab_at(meta, j)
        part = nt(dall, w_ref[at, :])
        sums_out_ref[IN_ROW : IN_ROW + 1, at] += jnp.sum(
            part * (x_ref[:, at].astype(F32) * in_scale), axis=0, keepdims=True
        )
        target = keep_ref if j < 2 else send_ref
        target[:, (j % 2) * SLAB : (j % 2 + 1) * SLAB] = part.astype(BF16)


def feed_grad_kernel(first_ref, second_ref, *refs):
    refs[-1][...] = tn(first_ref[...], second_ref[...]).astype(BF16)


def attn_grad_kernel(row_ref, *refs):
    here_ref, away_ref, both_ref = refs[-3:]
    start = 0
    for first_ref, second_ref in zip(refs[:-3:2], refs[1:-3:2]):
        stop = start + min(second_ref.shape[1], QKV)
        both_ref[:, start:stop] = tn(first_ref[...], second_ref[:, : stop - start])
        start = stop
    rows = here_ref.shape[1]
    row = row_ref[0]
    here_ref[0] = both_ref[pl.ds(pl.multiple_of(row * rows, rows), rows), :].astype(BF16)
    away_ref[0] = both_ref[pl.ds(pl.multiple_of((1 - row) * rows, rows), rows), :].astype(BF16)


def squares_kernel(*refs):
    feed_ref, attn_ref, squares_ref = refs[-3:]
    feed = feed_ref[...].astype(F32)
    total = jnp.sum(jnp.sum(feed * feed, axis=1, keepdims=True), axis=0, keepdims=True)
    start = 0
    for kept_ref, came_ref in zip(refs[:-3:2], refs[1:-3:2]):
        attn = kept_ref[...] + came_ref[...].astype(F32)
        attn_ref[:, start : start + attn.shape[1]] = attn
        start += attn.shape[1]
        total = total + jnp.sum(jnp.sum(attn * attn, axis=1, keepdims=True), axis=0, keepdims=True)
    squares_ref[...] = jnp.broadcast_to(total, squares_ref.shape)


def update_kernel(clip_ref, attn_ref, feed_ref, *refs):
    masters, firsts, seconds = refs[:5], refs[5:10], refs[10:15]
    outs, turned, turned_attn = refs[15:30], refs[30], refs[31]
    step = pl.program_id(0)
    width = feed_ref.shape[1] // 3

    @pl.when(step == 0)
    def _():
        turned[...] = feed_ref[...].astype(F32).T
        turned_attn[...] = attn_ref[:, MAIN:].T

    clip = clip_ref[0]

    def rows(count):
        if count == attn_ref.shape[0]:
            return slice(None)
        return pl.ds(pl.multiple_of(step * count, 8), count)

    def units(k):
        count = masters[4].shape[0]
        return turned[pl.ds(pl.multiple_of(k * width + step * count, 8), count), :]

    attn = attn_ref[rows(masters[0].shape[1]), :]
    across = masters[2].shape[0]
    grads = (
        (attn[:, :DK], attn[:, DK : 2 * DK]),
        (attn[:, 2 * DK : QKV], attn[:, QKV:MAIN]),
        (turned_attn[pl.ds(pl.multiple_of(step * across, 8), across), :],),
        (units(0), units(1)),
        (units(2),),
    )
    rates = (D, D, HEADS * DV, D, FF)
    for i in range(5):
        for k, grad in enumerate(grads[i]):
            at = k if len(grads[i]) > 1 else Ellipsis
            results = adam_step(
                masters[i][at], grad, firsts[i][at], seconds[i][at], clip, 2.0 * rates[i] ** (-0.5), WEIGHT_DECAY
            )
            for n in range(3):
                outs[n * 5 + i][at] = results[n]


def whole(array):
    zeros = (0,) * array.ndim
    return pl.BlockSpec(array.shape, lambda i, meta: zeros, pipeline_mode=pl.Buffered(1))


def fixed(shape):
    return pl.BlockSpec(shape, lambda i, meta: (0,) * len(shape))


def rows_at(rows, width, place):
    return pl.BlockSpec((rows, width), lambda i, meta: (place(i), 0))


def like(shape, dtype):
    return jax.ShapeDtypeStruct(shape, dtype)


def params():
    return pltpu.CompilerParams(vmem_limit_bytes=VMEM_LIMIT)


def run_kernel(body, meta, steps, ins, in_specs, saved, outs, out_specs, saved_like, saved_specs, name, flops):
    given = [] if saved is None else list(saved)
    aliases = {1 + len(ins) + i: len(outs) + i for i in range(len(given))}
    result = pl.pallas_call(
        functools.partial(body, len(given)),
        grid_spec=pltpu.PrefetchScalarGridSpec(
            num_scalar_prefetch=1,
            grid=(steps,),
            in_specs=list(in_specs) + [pl.BlockSpec(memory_space=pl.ANY)] * len(given),
            out_specs=list(out_specs) + list(saved_specs),
        ),
        out_shape=list(outs) + list(saved_like),
        input_output_aliases=aliases,
        compiler_params=params(),
        cost_estimate=pl.CostEstimate(flops=flops, bytes_accessed=1024, transcendentals=0),
        name=name,
    )(meta, *ins, *given)
    return list(result[: len(outs)]), list(result[len(outs) :])


def attend(piece, meta, x, w, wo, wb, g1, go, c, state, saved):
    tokens = x.shape[0]
    size = tokens // PIECES
    steps = size // BLOCK
    first = piece * steps
    here = lambda i: first + i
    ins = [x, w, wo, wb, g1, go, c, state]
    in_specs = [rows_at(BLOCK, D, here)] + [whole(a) for a in ins[1:]]
    outs = [like((size, D), BF16), like(state.shape, F32)]
    out_specs = [rows_at(BLOCK, D, lambda i: i), fixed(state.shape)]
    widths = [
        (D, BF16),
        (2 * DK + DV, BF16),
        (DV, F32),
        (LANES, BF16),
        (DK, F32),
        (DV, F32),
        (DV, BF16),
    ]
    saved_like = [like((tokens, n), d) for n, d in widths]
    saved_specs = [rows_at(BLOCK, n, here) for n, _ in widths]
    saved_like.append(like((tokens // CHUNK * DV, DK), BF16))
    saved_specs.append(rows_at(BLOCK // CHUNK * DV, DK, here))
    return run_kernel(
        functools.partial(attend_kernel, first),
        meta, steps, ins, in_specs, saved, outs, out_specs, saved_like, saved_specs,
        "attend", size * 8 * D * 1024,
    )


def feed(piece, meta, x, terms, dys, wf, g2, saved):
    tokens = x.shape[0]
    size = tokens // PIECES
    steps = size // BLOCK
    first = piece * steps
    here = lambda i: first + i
    width = wf.shape[1] // 3
    ins = [x, *terms, *dys, wf, g2]
    in_specs = (
        [rows_at(BLOCK, D, here)]
        + [rows_at(BLOCK, a.shape[1], lambda i: i) for a in terms]
        + [rows_at(BLOCK, SLAB, here), rows_at(BLOCK, SLAB, lambda i: i)] * 2
        + [whole(wf), whole(g2)]
    )
    outs = [like((size, D), BF16)]
    out_specs = [rows_at(BLOCK, D, lambda i: i)]
    widths = [
        (2 * SLAB, BF16),
        (2 * SLAB, BF16),
        (D, BF16),
        (D, BF16),
        (width, BF16),
        (2 * width, BF16),
        (D, BF16),
        (LANES, F32),
        (SLAB, F32),
    ]
    saved_like = [like((tokens, n), d) for n, d in widths]
    saved_specs = [rows_at(BLOCK, n, here) for n, _ in widths]
    return run_kernel(
        functools.partial(feed_kernel, len(terms)),
        meta, steps, ins, in_specs, saved, outs, out_specs, saved_like, saved_specs,
        "feed", size * 2 * D * width * 6,
    )


def turn_back(piece, meta, terms, rows_in, wo, g2, go, sums, saved):
    tokens = rows_in[0].shape[0]
    size = tokens // PIECES
    steps = size // BLOCK
    first = piece * steps
    here = lambda i: first + i
    ins = [*terms, *rows_in, wo, g2, go, sums]
    in_specs = (
        [rows_at(BLOCK, a.shape[1], lambda i: i) for a in terms]
        + [rows_at(BLOCK, a.shape[1], here) for a in rows_in]
        + [whole(a) for a in (wo, g2, go, sums)]
    )
    widths = [(D, BF16), (SLAB, F32), (DV, BF16), (DV, BF16)]
    return run_kernel(
        functools.partial(turn_kernel, first),
        meta, steps, ins, in_specs, saved, [like(sums.shape, F32)], [fixed(sums.shape)],
        [like((tokens, n), d) for n, d in widths], [rows_at(BLOCK, n, here) for n, _ in widths],
        "turn", int(0.01 * size * 4 * D * 1024),
    )


def back(piece, meta, rows_in, states, w, wb, carried, saved):
    tokens = rows_in[0].shape[0]
    size = tokens // PIECES
    steps = size // BLOCK
    last = (piece + 1) * steps - 1
    here = lambda i: last - i
    local = lambda i: steps - 1 - i
    ins = [*rows_in, states, w, wb, *carried]
    in_specs = (
        [rows_at(BLOCK, a.shape[1], here) for a in rows_in]
        + [rows_at(BLOCK // CHUNK * DV, DK, here)]
        + [whole(a) for a in (w, wb, *carried)]
    )
    outs = [like((size, 2 * SLAB), BF16)] * 2 + [like(a.shape, a.dtype) for a in carried]
    out_specs = [rows_at(BLOCK, 2 * SLAB, local)] * 2 + [fixed(a.shape) for a in carried]
    return run_kernel(
        functools.partial(back_kernel, last),
        meta, steps, ins, in_specs, saved, outs, out_specs,
        [like((tokens, QKVL), BF16)], [rows_at(BLOCK, QKVL, here)],
        "back", int(0.7 * size * 12 * D * 1024),
    )


def feed_grad(first, second, column, full):
    tokens, width = second.shape
    ins = [first, second] + ([] if full is None else [full])
    return pl.pallas_call(
        feed_grad_kernel,
        grid=(D // SLAB,),
        in_specs=[
            pl.BlockSpec((tokens, SLAB), lambda i: (0, i)),
            pl.BlockSpec((tokens, width), lambda i: (0, 0), pipeline_mode=pl.Buffered(1)),
        ]
        + [pl.BlockSpec(memory_space=pl.ANY)] * (len(ins) - 2),
        out_specs=pl.BlockSpec((SLAB, width), lambda i: (i, column)),
        out_shape=like((D, FEED_COLS), BF16),
        input_output_aliases={2: 0} if len(ins) > 2 else {},
        compiler_params=params(),
        cost_estimate=pl.CostEstimate(
            flops=int(1 * 4 * D * tokens * width), bytes_accessed=1024, transcendentals=0
        ),
        name="feed_grad",
    )(*ins)


def attn_grad(row, *pairs):
    tokens = pairs[0].shape[0]
    half = SLAB // 2
    width = sum(min(a.shape[1], QKV) for a in pairs[1::2])
    specs = [
        whole(a) if i % 2 else pl.BlockSpec((tokens, SLAB), lambda i, row: (0, i)) for i, a in enumerate(pairs)
    ]
    return pl.pallas_call(
        attn_grad_kernel,
        grid_spec=pltpu.PrefetchScalarGridSpec(
            num_scalar_prefetch=1,
            grid=(SLABS,),
            in_specs=specs,
            out_specs=[pl.BlockSpec((1, half, width), lambda i, row: (i, 0, 0))] * 2,
            scratch_shapes=[pltpu.VMEM((SLAB, width), F32)],
        ),
        out_shape=[like((SLABS, half, width), BF16)] * 2,
        compiler_params=params(),
        cost_estimate=pl.CostEstimate(
            flops=int(0.5 * 4 * D * tokens * width), bytes_accessed=1024, transcendentals=0
        ),
        name="attn_grad",
    )(row, *pairs)


def shard_squares(*parts):
    rows = parts[0].shape[0]
    return pl.pallas_call(
        squares_kernel,
        out_shape=(like((rows, D), F32), like((8, LANES), F32)),
        compiler_params=params(),
        name="squares",
    )(*parts)


def update(clip, attn, feed, arrays):
    rows = attn.shape[0]
    steps = 4 if rows % 32 == 0 else 1
    masters = arrays[:5]

    def cut(array):
        shape = list(array.shape)
        shape[-2] //= steps
        zeros = (0,) * (len(shape) - 2)
        return pl.BlockSpec(tuple(shape), lambda i: (*zeros, i, 0))

    return pl.pallas_call(
        update_kernel,
        grid=(steps,),
        in_specs=[pl.BlockSpec(memory_space=pltpu.SMEM)]
        + [pl.BlockSpec(a.shape, lambda i: (0, 0), pipeline_mode=pl.Buffered(1)) for a in (attn, feed)]
        + [cut(a) for a in arrays],
        out_specs=[cut(a) for a in masters] * 3,
        out_shape=[like(a.shape, F32) for a in masters] * 3,
        scratch_shapes=[pltpu.VMEM((FEED_COLS, rows), F32), pltpu.VMEM((DV, rows), F32)],
        compiler_params=params(),
        name="update",
    )(clip, attn, feed, *arrays)


def after(array, *others):
    return lax.optimization_barrier((array, *others))[0]


def swap(array, axis, bit):
    return lax.ppermute(array, axis, [(i, i ^ bit) for i in range(lax.axis_size(axis))])


def swap_core(array):
    return swap(array, "tensor", 1)


def swap_far(array):
    return swap(array, "tensor", 2)


def swap_row(array):
    return swap(array, "dp", 1)


def shift_layer(array, by):
    count = lax.axis_size("dp")
    return lax.ppermute(array, "dp", [(i, (i + 2 * by) % count) for i in range(count)])


def gather_attn(own, earlier):
    dp_at = lax.axis_index("dp")
    found = {(0, 0): own, (1, 0): shift_layer(own, 1), (3, 0): shift_layer(own, 3), (0, 1): swap_row(own)}
    first = list(found.values())[1:]
    found[2, 0] = shift_layer(after(own, *first), 2)
    for k in (1, 3):
        found[k, 1] = swap_row(after(found[k, 0], *first))
    second = [found[2, 0], found[1, 1], found[3, 1]]
    found[2, 1] = swap_row(after(*second, earlier))
    places = [((dp_at - 2 * k) % (2 * SLABS)) ^ h for k, h in found]
    pieces = list(found.values())
    rows = D
    return first, pl.pallas_call(
        assemble_kernel,
        in_specs=[pl.BlockSpec(memory_space=pltpu.SMEM)]
        + [pl.BlockSpec(memory_space=pltpu.VMEM)] * (2 * SLABS),
        out_shape=(like((rows, ATTN), BF16), like((rows, DV), BF16), like((LANES, DK), BF16)),
        compiler_params=params(),
        name="assemble",
    )(jnp.stack(places).astype(jnp.int32), *pieces)


def gather_plain(own, earlier):
    count, rows = lax.axis_size("dp"), own.shape[0]
    full = lax.all_gather(own, "dp", axis=0, tiled=True)
    keys = DK // count
    blocks = full.reshape(count, rows, -1)[:, :RANK, QKV + RANK : QKV + RANK + keys]
    wb = jnp.pad(blocks.transpose(1, 0, 2).reshape(RANK, DK), ((0, LANES - RANK), (0, 0)))
    return [own], (full[:, :ATTN], full[:, ATTN:], wb)


def pick(array, axis, index):
    return lax.dynamic_index_in_dim(array, index, axis, keepdims=False)


def scatter_rows(here, away, *earlier):
    came = after(swap_row(away), *earlier)
    return (here.astype(F32) + came.astype(F32)).reshape(2, 2, *here.shape[1:])


def scatter_near(total, low, *earlier):
    away = pick(total, 1, 1 - low).astype(BF16)
    return pick(total, 1, low) + after(swap(away, "dp", 2), *earlier).astype(F32)


def scatter_far(total, high, *earlier):
    away = pick(total, 0, 1 - high).astype(BF16)
    return pick(total, 0, high), after(swap(away, "dp", 4), *earlier)


def sum_terms(part, earlier, beside=(), before=(), halves=False):
    core = after(swap_core(after(part, *earlier)), *beside)
    own = []
    for start, stop in ((0, SLAB), (SLAB, 2 * SLAB)) if halves else ((0, 2 * SLAB),):
        beside = core[:, 2 * SLAB + start : 2 * SLAB + stop].astype(F32)
        own.append((part[:, start:stop].astype(F32) + beside).astype(BF16))
    far = [swap_far(after(own[0], *before))]
    if halves:
        far.append(swap_far(after(own[1], far[0])))
    return own, part, core, far


def slab_sum(keep, send, earlier):
    own = keep.astype(F32) + swap_core(send).astype(F32)
    far = swap_far(after(own[:, SLAB:].astype(BF16), earlier))
    return own[:, :SLAB] + far.astype(F32), far


def sum_everywhere(array, axes=("tensor", "dp")):
    for axis in axes:
        size = lax.axis_size(axis)
        bit = 1
        while bit < size:
            array = array + swap(array, axis, bit)
            bit *= 2
    return array


def add_rounded(array, axis, bit, *earlier):
    low = after(array.astype(BF16), *earlier)
    return low.astype(F32) + swap(low, axis, bit).astype(F32)


def adam_step(weight, gradient, first_moment, second_moment, clip_factor, learn_rate, weight_decay):
    clipped = gradient * clip_factor
    momentum = BETA_FIRST * first_moment + (1.0 - BETA_FIRST) * clipped
    variance = BETA_SECOND * second_moment + (1.0 - BETA_SECOND) * clipped * clipped
    step_size = (
        momentum
        / (1.0 - BETA_FIRST**STEP)
        / (jnp.sqrt(variance / (1.0 - BETA_SECOND**STEP)) + ADAM_EPS)
    )
    updated = weight * (1.0 - learn_rate * weight_decay) - learn_rate * step_size
    return (momentum, variance, updated)


LARGE = (0, 1, 4, 5, 6)


def body(*args):
    inputs, cotangent, doc_lengths = args[:3]
    masters, firsts, seconds = args[3:11], args[11:19], args[19:27]
    weight_qk, weight_vg, weight_lowin, weight_lowout, weight_mixout, weight_gateup, weight_down = masters[:7]
    weight_small = masters[7]
    tensor_at = lax.axis_index("tensor")
    dp_at = lax.axis_index("dp")
    layered = lax.axis_size("dp") == 2 * SLABS
    rows_here = weight_qk.shape[1]
    ranks, _, keys_here = weight_lowout.shape
    turn = lambda i, a: jnp.swapaxes(a, 1, 2) if i == 5 else a
    size = cotangent.shape[0] // PIECES
    far_cots = [swap_far(cotangent[i * size : (i + 1) * size]) for i in range(PIECES)]

    attn_pack, feed_pack = pl.pallas_call(
        pack_kernel,
        out_shape=(like((rows_here, ATTN + DV), BF16), like((rows_here, FEED_COLS), BF16)),
        compiler_params=params(),
        name="pack",
    )(
        weight_qk, weight_vg, weight_lowin.T, weight_lowout[:, 0, :], weight_mixout,
        turn(5, weight_gateup), weight_down,
    )
    arrived, (w, wo, wb) = (gather_attn if layered else gather_plain)(attn_pack, far_cots[0])
    wf = lax.all_gather(after(feed_pack, *arrived), "dp", axis=0, tiled=True)
    doc_ends = jnp.cumsum(doc_lengths[0])
    slots = jnp.stack([tensor_at ^ o for o in ORDER])
    meta = jnp.concatenate([slots.astype(jnp.int32), doc_ends[-1:].astype(jnp.int32), doc_ends.astype(jnp.int32)])

    g1, g2 = weight_small[:D].reshape(1, D), weight_small[D : 2 * D].reshape(1, D)
    go = weight_small[2 * D : 2 * D + DV].reshape(1, DV)
    gate_bias = lax.dynamic_slice_in_dim(weight_small, 2 * D + DV + tensor_at * DK, DK).reshape(1, DK)
    x = inputs
    x_wide = x.astype(F32)
    in_scale = lax.rsqrt(jnp.mean(x_wide * x_wide, axis=-1, keepdims=True) + NORM_EPS)
    meta, _, in_scale = lax.optimization_barrier((meta, far_cots[-1], in_scale))
    core_cot = swap_core(after(cotangent, w))
    dys = [(cotangent, far, core_cot, swap_core(after(far, w))) for far in far_cots]

    state = jnp.zeros((DV, DK), F32)
    saved = None
    terms = []
    earlier = before = []
    for piece in range(PIECES):
        (part, state), saved = attend(piece, meta, x, w, wo, wb, g1, go, gate_bias, state, saved)
        own, part, core, far = sum_terms(part, earlier, before=before, halves=piece < PIECES - 1)
        terms.append((part, core, far))
        earlier = far[:1]
        before = far[-1:]
        state = after(state, *own)
    xn, *kept = saved
    z = kept.pop(5)
    terms = [(part, core, *far, *(swap_core(after(f, *own)) for f in far)) for part, core, far in terms]

    fed = None
    back_terms = []
    order = after(meta, *own)
    for piece in range(PIECES):
        (part,), fed = feed(piece, order, x, terms[piece], dys[piece], wf, g2, fed)
        beside = []
        if piece == PIECES - 1:
            feed_keep, feed_send, hn, dy, hidden, dgu, rhat, rs, resid = fed
            grad_feed = feed_grad(dy, hidden, 2, None)
            beside = [grad_feed]
        own, part, core, far = sum_terms(part, earlier, beside)
        (own,), (far,) = own, far
        earlier = [far]
        order = after(meta, own)
        if piece < PIECES - 1:
            back_terms.append((part, core, far, swap_core(far)))
    grad_feed = feed_grad(after(hn, own), dgu, 0, grad_feed)
    fed_own = (feed_keep.astype(F32) + swap_core(after(feed_send, own)).astype(F32)).astype(BF16)
    shard_feed = lax.psum_scatter(grad_feed, "dp", scatter_dimension=0, tiled=True)

    qkv, gout, lowr, zeta, mixed, states = kept
    turned = None
    sums = jnp.zeros((SUM_ROWS, D), F32)
    order = after(meta, grad_feed, fed_own)
    for piece in range(PIECES):
        if piece == PIECES - 1:
            back_terms.append((part, core, far, swap_core(after(far, sums))))
        (sums,), turned = turn_back(
            piece, order, back_terms[piece], (dy, rhat, rs, gout, mixed), wo, g2, go, sums, turned
        )
    dres16, dres, dgout, dmix = turned
    fed_far = swap_far(after(fed_own[:, SLAB:], far))
    row_at = (dp_at % 2 if layered else jnp.zeros_like(dp_at)).astype(jnp.int32).reshape(1)
    high, low = dp_at // 4, (dp_at // 2) % 2
    here, away = attn_grad(row_at, xn, dgout, dres16, z)
    if layered:
        early = scatter_rows(here, away)
        early_layer = scatter_near(early, low)
        early_parts = scatter_far(early_layer, high)

    carried = [jnp.zeros((DV, DK), F32), jnp.zeros((DV, DK), BF16), sums]
    backed = None
    dxn = []
    order = after(meta, away)
    for piece in reversed(range(PIECES)):
        (keep, send, *carried), backed = back(
            piece, order, (dmix, dgout, x, xn, qkv, lowr, zeta), states, w, wb, carried, backed
        )
        if layered:
            order = after(meta, early)
        dxn.insert(0, (keep, send))
    (dall,) = backed
    late_here, late_away = attn_grad(after(row_at, early_layer, fed_far) if layered else row_at, xn, dall)
    dxn_far = [fed_far]
    for piece in reversed(range(PIECES)):
        keep, send = dxn[piece]
        dxn[piece], far = slab_sum(keep, after(send, late_here), dxn_far[-1])
        dxn_far.append(far)
    if layered:
        late = scatter_rows(late_here, late_away, early_parts[1], *dxn_far[1:-1])
    else:
        late = late_here
    fed_sum = fed_own[:, :SLAB].astype(F32) + after(fed_far, late).astype(F32)
    output = (resid + fed_sum).astype(BF16)
    if layered:
        late_layer = scatter_near(late, low, output)
        parts = *scatter_far(late_layer, high, dxn_far[-1]), *early_parts
    else:
        late_layer = late_here
        grads = [jnp.stack(g, axis=1).reshape(D, -1) for g in ((late_here, late_away), (here, away))]
        kept = lax.psum_scatter(
            jnp.concatenate(grads, axis=1), "dp", scatter_dimension=0, tiled=True
        ).astype(F32)
        parts = kept, jnp.zeros(kept.shape, BF16)

    dxn = jnp.concatenate(dxn, axis=0)
    hat_here = lax.dynamic_slice_in_dim(x, tensor_at * SLAB, SLAB, 1).astype(F32) * in_scale
    scaled = dxn * lax.dynamic_slice_in_dim(g1, tensor_at * SLAB, SLAB, 1)
    row_sums = jnp.sum(scaled * hat_here, axis=-1).reshape(-1, LANES)
    row_mean = sum_everywhere(row_sums, ("tensor",)).reshape(-1, 1) / D
    input_grad = dres + in_scale * (scaled - hat_here * row_mean)

    wide = add_rounded(carried[2], "tensor", 1, late_here)
    wide = add_rounded(wide, "tensor", 2)
    for bit in (1 << i for i in range(lax.axis_size("dp").bit_length() - 1)):
        wide = add_rounded(wide, "dp", bit, late if bit == 1 else late_layer)
    small_grad = jnp.concatenate([wide[IN_ROW], wide[MID_ROW], wide[HEAD_ROW, : DV + HEADS * DK]])
    grad_lowin = lax.dynamic_slice(wide, (LOWIN_ROW, dp_at * rows_here), (RANK, rows_here)).T
    lowout = jnp.concatenate([wide[LOWOUT_ROW:, : D // 2], wide[LOWOUT_ROW:, D // 2 :]], axis=0)
    grad_lowout = lax.dynamic_slice(
        lowout, (0, tensor_at * DK + dp_at * keys_here), (RANK, keys_here)
    ).reshape(weight_lowout.shape)

    shard_attn, squares = shard_squares(*parts, shard_feed)
    square_total = sum_everywhere(squares)[0, 0]
    grad_norm = jnp.sqrt(square_total + jnp.sum(wide * wide))
    clip_factor = jnp.minimum(1.0, CLIP_NORM / (grad_norm + 1e-06))
    arrays = [turn(i, group[i]) for group in (masters, firsts, seconds) for i in LARGE]
    large = update(clip_factor.reshape(1), shard_attn, shard_feed, arrays)
    small_rate = jnp.where(
        lax.broadcasted_iota(jnp.int32, weight_small.shape, 0) < 2 * D + DV, GAIN_RATE, BIAS_RATE
    )
    steps = {}
    for k, i in enumerate(LARGE):
        steps[i] = [turn(i, a) for a in large[k::5]]
    for i, grad, rate, decay in (
        (2, grad_lowin, 2.0 * D ** (-0.5), WEIGHT_DECAY),
        (3, grad_lowout, 2.0 * RANK ** (-0.5), WEIGHT_DECAY),
        (7, small_grad, small_rate, 0.0),
    ):
        steps[i] = adam_step(masters[i], grad, firsts[i], seconds[i], clip_factor, rate, decay)
    return (output, input_grad, grad_norm.reshape(1), *(steps[i][k] for k in range(3) for i in range(8)))


def solution(mesh):
    weights = (
        P(None, "dp", "tensor"),
        P(None, "dp", "tensor"),
        P("dp", None),
        P(None, "tensor", "dp"),
        P("tensor", "dp"),
        P(None, "dp", "tensor"),
        P("tensor", "dp"),
        P(),
    )
    return jax.shard_map(
        body,
        mesh=mesh,
        in_specs=(P("dp", None), P("dp", "tensor"), P("dp", None), *weights, *weights, *weights),
        out_specs=(P("dp", "tensor"), P("dp", "tensor"), P(), *weights, *weights, *weights),
        check_vma=False,
    )
```

```python
import functools

import jax
import jax.numpy as jnp
from jax import lax
from jax.experimental import pallas as pl
from jax.experimental.pallas import tpu as pltpu
from jax.sharding import PartitionSpec as P

D = 1024
HEADS = 4
DK = 128
DV = 256
RANK = 16
FF = 2816
SPAN = 64
SEQ_LEN = 2048
STEP = 10

NORM_EPS = 1e-06
GATE_NORM = 16.0
BETA_FIRST = 0.9
BETA_SECOND = 0.95
ADAM_EPS = 1e-08
WEIGHT_DECAY = 0.1
CLIP_NORM = 1.0
GAIN_RATE = 2.5
BIAS_RATE = 4.0

F32 = jnp.float32
BF16 = jnp.bfloat16
LANES = 128
SLAB = 256
SLABS = 4
CHUNK = 2 * SPAN
BLOCK = 256
PIECES = 2
ORDER = (0, 2, 1, 3)
QKV = 512
QKVL = 640
ATTN = 896
MAIN = 768
FEED_COLS = 3 * 768
OUT_SCALE = DK**-0.5
VMEM_LIMIT = 60 * 1024 * 1024


def nn(a, b):
    return lax.dot_general(a, b, (((1,), (0,)), ((), ())), preferred_element_type=F32)


def nt(a, b):
    return lax.dot_general(a, b, (((1,), (1,)), ((), ())), preferred_element_type=F32)


def tn(a, b):
    return lax.dot_general(a, b, (((0,), (0,)), ((), ())), preferred_element_type=F32)


def doc_at(position, ends):
    number = jnp.zeros_like(position)
    for end in ends:
        number = number + jnp.where(position >= end, 1, 0)
    return number


def log_sigmoid(values):
    return jnp.minimum(values, 0.0) - jnp.log1p(jnp.exp(-jnp.abs(values)))


def prefix_sums(values, triangle):
    high = values.astype(BF16)
    low = (values - high.astype(F32)).astype(BF16)
    width = values.shape[1]
    both = nn(triangle, jnp.concatenate([high, low], axis=1))
    return both[:, :width] + both[:, width:]


def chunk_terms(queries, keys, forget, base, ends):
    row = lax.broadcasted_iota(jnp.int32, (CHUNK, CHUNK), 0)
    col = lax.broadcasted_iota(jnp.int32, (CHUNK, CHUNK), 1)
    decay = prefix_sums(forget, jnp.where(col <= row, 1.0, 0.0).astype(BF16))
    seg_row = doc_at(row + base, ends)
    same = seg_row == doc_at(col + base, ends)
    upper = row >= SPAN
    near = same & (col <= row) & (upper == (col >= SPAN))
    far = same & upper & (col < SPAN)
    before = jnp.where(base > 0, doc_at(base - 1, ends), -1)
    final = doc_at(base + CHUNK - 1, ends)
    alive = jnp.where(seg_row == before, 1.0, 0.0)
    keep = jnp.where(seg_row == final, 1.0, 0.0)
    carry = jnp.where(before == final, 1.0, 0.0)
    mid = jnp.where(upper, decay[SPAN + SPAN // 2 :][:1], decay[SPAN // 2 :][:1])
    grow = jnp.exp(decay - mid)
    shrink = jnp.exp(mid - decay)
    edge = jnp.exp(-jnp.abs(decay - decay[SPAN - 1 : SPAN]))
    from_start = jnp.exp(decay) * alive
    last = decay[CHUNK - 1 : CHUNK]
    to_end = jnp.exp(last - decay) * keep
    step = jnp.exp(last) * carry
    q_near = (queries * grow).astype(BF16)
    k_near = (keys * shrink).astype(BF16)
    q_far = (queries * edge).astype(BF16)
    k_far = (keys * edge).astype(BF16)
    q_state = (queries * from_start).astype(BF16)
    k_state = (keys * to_end).astype(BF16)
    scores = jnp.where(near, nt(q_near, k_near), jnp.where(far, nt(q_far, k_far), 0.0)).astype(BF16)
    return (
        (row, col, near, far),
        (grow, shrink, edge, from_start, to_end, step),
        (q_near, k_near, q_far, k_far, q_state, k_state),
        scores,
    )


def slab_at(meta, j):
    return pl.ds(pl.multiple_of(meta[j] * SLAB, SLAB), SLAB)


def lanes_at(start):
    return pl.ds(pl.multiple_of(start, LANES), LANES)


def one_hot(rows, shift):
    row = lax.broadcasted_iota(jnp.int32, (rows, LANES), 0)
    col = lax.broadcasted_iota(jnp.int32, (rows, LANES), 1)
    return jnp.where(col - row == shift, 1.0, 0.0).astype(BF16)


def pack_kernel(qk_ref, vg_ref, lowin_ref, lowout_ref, mixout_ref, gateup_ref, down_ref, attn_ref, feed_ref):
    units = gateup_ref.shape[1]
    width = feed_ref.shape[1] // 3
    attn_ref[:, :DK] = qk_ref[0].astype(BF16)
    attn_ref[:, DK : 2 * DK] = qk_ref[1].astype(BF16)
    attn_ref[:, 2 * DK : 2 * DK + DV] = vg_ref[0].astype(BF16)
    attn_ref[:, QKV:QKVL] = tn(lowin_ref[...].astype(BF16), one_hot(RANK, 0)).astype(BF16)
    lowout = lowout_ref[...].astype(BF16)
    attn_ref[:RANK, QKV:QKVL] += nn(lowout, one_hot(lowout.shape[1], RANK)).astype(BF16)
    attn_ref[:, QKVL:ATTN] = vg_ref[1].astype(BF16)
    attn_ref[:, ATTN:] = mixout_ref[...].T.astype(BF16)
    rows = feed_ref.shape[0]
    pad = jnp.zeros((rows, width - units), BF16)
    feed_ref[:, :units] = gateup_ref[0].T.astype(BF16)
    feed_ref[:, units:width] = pad
    feed_ref[:, width : width + units] = gateup_ref[1].T.astype(BF16)
    feed_ref[:, width + units : 2 * width] = pad
    feed_ref[:, 2 * width : 2 * width + units] = down_ref[...].T.astype(BF16)
    feed_ref[:, 2 * width + units :] = pad


def assemble_kernel(place, *refs):
    pieces = refs[: 2 * SLABS]
    w_ref, wo_ref, wb_ref = refs[2 * SLABS :]
    rows = pieces[0].shape[0]
    keys = DK // (2 * SLABS)
    wb_ref[...] = jnp.zeros_like(wb_ref)
    for i, piece in enumerate(pieces):
        block = place[i]
        at = pl.ds(pl.multiple_of(block * rows, rows), rows)
        w_ref[at, :] = piece[:, :ATTN]
        wo_ref[at, :] = piece[:, ATTN:]
        row = lax.broadcasted_iota(jnp.int32, (LANES, DK), 0)
        col = lax.broadcasted_iota(jnp.int32, (LANES, DK), 1)
        inside = (row >= RANK) & (row < RANK + keys)
        move = jnp.where(inside & (col - row == block * keys - RANK), 1.0, 0.0).astype(BF16)
        wb_ref[:RANK, :] += nn(piece[:RANK, QKV:QKVL], move).astype(BF16)


def attend_kernel(first_block, n_saved, meta, *refs):
    xn_ref, w_ref, wo_ref, wb_ref, go_ref, c_ref, state_ref = refs[:7]
    refs = refs[7 + n_saved :]
    part_ref, state_out_ref = refs[:2]
    qkv_ref, gout_ref, lowr_ref, zeta_ref, mixed_ref, z_ref, states_ref = refs[2:]
    step = pl.program_id(0)

    @pl.when(step == 0)
    def _():
        state_out_ref[...] = state_ref[...]

    ends = [meta[META_ENDS + i] for i in range(meta.shape[0] - META_ENDS)]
    proj = nn(xn_ref[...], w_ref[...])
    qkv = proj[:, :QKV].astype(BF16)
    qkv_ref[...] = qkv
    gout = proj[:, QKVL:]
    gout_ref[...] = gout
    lowr = proj[:, QKV:QKVL].astype(BF16)
    lowr_ref[...] = lowr
    zeta = nn(lowr, wb_ref[...]) + c_ref[...]
    zeta_ref[...] = zeta
    forget = log_sigmoid(zeta) * (1.0 / GATE_NORM)
    base = (first_block + step) * BLOCK
    state = state_out_ref[...]
    for i in range(BLOCK // CHUNK):
        rows = slice(i * CHUNK, (i + 1) * CHUNK)
        queries = qkv[rows, :DK].astype(F32)
        keys = qkv[rows, DK : 2 * DK].astype(F32)
        values = qkv[rows, 2 * DK :]
        start = base + i * CHUNK
        _, factors, terms, scores = chunk_terms(queries, keys, forget[rows], start, ends)
        q_state, k_state = terms[4:]
        state_low = state.astype(BF16)
        states_ref[i * DV : (i + 1) * DV, :] = state_low
        mixed = (nn(scores, values) + nt(q_state, state_low)) * OUT_SCALE
        mixed_ref[rows, :] = mixed
        state = state * factors[5] + tn(values, k_state)
        where = lax.broadcasted_iota(jnp.int32, (CHUNK, DV), 0) + start
        valid = jnp.where(where < ends[-1], 1.0, 0.0)
        head_scale = lax.rsqrt(jnp.mean(mixed * mixed, axis=-1, keepdims=True) + NORM_EPS)
        gate = gout[rows]
        z = mixed * head_scale * go_ref[...] * (gate * jax.nn.sigmoid(gate)) * valid
        z_ref[rows, :] = z.astype(BF16)
    state_out_ref[...] = state
    z = z_ref[...]
    for j in range(SLABS):
        part_ref[:, j * SLAB : (j + 1) * SLAB] = nt(z, wo_ref[slab_at(meta, j), :]).astype(BF16)


def summed(j, mine, core, *beyond):
    other = (j + 2) % SLABS
    total = mine[:, j * SLAB : (j + 1) * SLAB].astype(F32)
    total = total + core[:, other * SLAB : (other + 1) * SLAB].astype(F32)
    k = 1 - j % 2
    if len(beyond) == 2:
        far = beyond[j // 2][:, k * SLAB : (k + 1) * SLAB]
    else:
        far = beyond[2 * (j // 2) + k][...]
    return total + far.astype(F32)


def feed_kernel(n_terms, n_saved, meta, *refs):
    x_ref, terms, refs = refs[0], refs[1 : 1 + n_terms], refs[1 + n_terms :]
    dys, wf_ref, g2_ref = refs[:SLABS], refs[SLABS], refs[SLABS + 1]
    refs = refs[SLABS + 2 + n_saved :]
    part_ref = refs[0]
    feed_keep_ref, feed_send_ref, hn_ref, dy_ref, hidden_ref, dgu_ref, rhat_ref, rs_ref, resid_ref = refs[1:]
    width = hidden_ref.shape[1]
    resid = []
    total = 0.0
    for j in range(SLABS):
        part = x_ref[:, slab_at(meta, j)].astype(F32) + summed(j, *terms)
        resid.append(part)
        total = total + jnp.sum(part * part, axis=-1, keepdims=True)
    resid_ref[...] = resid[0]
    scale = lax.rsqrt(total / D + NORM_EPS)
    rs_ref[...] = jnp.broadcast_to(scale, rs_ref.shape)
    for j in range(SLABS):
        at = slab_at(meta, j)
        rhat = resid[j] * scale
        rhat_ref[:, j * SLAB : (j + 1) * SLAB] = rhat.astype(BF16)
        hn = (rhat * g2_ref[:, at]).astype(BF16)
        hn_ref[:, at] = hn
        dy = dys[j][...]
        dy_ref[:, at] = dy
    units = nn(hn_ref[...], wf_ref[:, : 2 * width])
    dhid = nn(dy_ref[...], wf_ref[:, 2 * width :])
    gate = units[:, :width]
    up = units[:, width:]
    sig = jax.nn.sigmoid(gate)
    act = gate * sig
    hidden = (act * up).astype(BF16)
    hidden_ref[...] = hidden
    dgate = (dhid * up * (sig * (1.0 + gate * (1.0 - sig)))).astype(BF16)
    dup = (dhid * act).astype(BF16)
    dgu_ref[:, :width] = dgate
    dgu_ref[:, width:] = dup
    for j in range(SLABS):
        at = slab_at(meta, j)
        part = nt(dgu_ref[...], wf_ref[at, : 2 * width])
        part_ref[:, j * SLAB : (j + 1) * SLAB] = part.astype(BF16)
        fed = nt(hidden, wf_ref[at, 2 * width :]).astype(BF16)
        target = feed_keep_ref if j < 2 else feed_send_ref
        target[:, (j % 2) * SLAB : (j % 2 + 1) * SLAB] = fed


META_TOKENS = SLABS
META_ENDS = SLABS + 1

LOWIN_ROW = 0
IN_ROW = 16
MID_ROW = 17
HEAD_ROW = 18
LOWOUT_ROW = 24
SUM_ROWS = 32


def turn_kernel(first_block, n_saved, meta, *refs):
    terms = refs[:4]
    dy_ref, rhat_ref, rs_ref, gout_ref, mixed_ref = refs[4:9]
    wo_ref, g2_ref, go_ref, sums_ref = refs[9:13]
    refs = refs[13 + n_saved :]
    sums_out_ref, dres16_ref, dres_ref, dgout_ref, dmix_ref = refs
    step = pl.program_id(0)

    @pl.when(step == 0)
    def _():
        sums_out_ref[...] = sums_ref[...]

    base = (first_block + step) * BLOCK
    scaled = []
    dot = 0.0
    for j in range(SLABS):
        dhn = summed(j, *terms)
        rhat = rhat_ref[:, j * SLAB : (j + 1) * SLAB].astype(F32)
        if j == 0:
            sums_out_ref[MID_ROW : MID_ROW + 1, slab_at(meta, 0)] += jnp.sum(
                dhn * rhat, axis=0, keepdims=True
            )
        part = dhn * g2_ref[:, slab_at(meta, j)]
        scaled.append(part)
        dot = dot + jnp.sum(part * rhat, axis=-1, keepdims=True)
    scale = rs_ref[:, :1]
    mean = dot / D
    dz = 0.0
    for j in range(SLABS):
        at = slab_at(meta, j)
        rhat = rhat_ref[:, j * SLAB : (j + 1) * SLAB].astype(F32)
        dres = dy_ref[:, at].astype(F32) + scale * (scaled[j] - rhat * mean)
        if j == 0:
            dres_ref[...] = dres
        low = dres.astype(BF16)
        dres16_ref[:, at] = low
        dz = dz + nn(low, wo_ref[at, :])
    where = lax.broadcasted_iota(jnp.int32, (BLOCK, DV), 0) + base
    u = jnp.where(where < meta[META_TOKENS], dz, 0.0)
    mixed = mixed_ref[...]
    head_scale = lax.rsqrt(jnp.mean(mixed * mixed, axis=-1, keepdims=True) + NORM_EPS)
    hat = mixed * head_scale
    gate = gout_ref[...]
    sig = jax.nn.sigmoid(gate)
    act = gate * sig
    uhat = u * hat
    go = go_ref[...]
    sums_out_ref[HEAD_ROW : HEAD_ROW + 1, :DV] += jnp.sum(uhat * act, axis=0, keepdims=True)
    dgout_ref[...] = (uhat * go * (sig * (1.0 + gate * (1.0 - sig)))).astype(BF16)
    dhat = u * go * act
    dmix = head_scale * (dhat - hat * jnp.mean(dhat * hat, axis=-1, keepdims=True))
    dmix_ref[...] = (dmix * OUT_SCALE).astype(BF16)


def back_kernel(last_block, n_saved, meta, *refs):
    dmix_ref, dgout_ref, x_ref, xn_ref = refs[:4]
    qkv_ref, lowr_ref, zeta_ref, states_ref = refs[4:8]
    w_ref, wb_ref = refs[8:10]
    dstate_ref, next_ref, sums_ref = refs[10:13]
    refs = refs[13 + n_saved :]
    keep_ref, send_ref, dstate_out_ref, next_out_ref, sums_out_ref, dall_ref = refs
    step = pl.program_id(0)

    @pl.when(step == 0)
    def _():
        dstate_out_ref[...] = dstate_ref[...]
        next_out_ref[...] = next_ref[...]
        sums_out_ref[...] = sums_ref[...]

    ends = [meta[META_ENDS + i] for i in range(meta.shape[0] - META_ENDS)]
    base = (last_block - step) * BLOCK
    zeta = zeta_ref[...]
    forget = log_sigmoid(zeta) * (1.0 / GATE_NORM)
    slope = jax.nn.sigmoid(-zeta) * (1.0 / GATE_NORM)
    dstate = dstate_out_ref[...]
    after_state = next_out_ref[...]
    head_at = meta[0] * DK
    for i in reversed(range(BLOCK // CHUNK)):
        rows = slice(i * CHUNK, (i + 1) * CHUNK)
        queries = qkv_ref[rows, :DK].astype(F32)
        keys = qkv_ref[rows, DK : 2 * DK].astype(F32)
        values = qkv_ref[rows, 2 * DK :]
        masks, factors, parts, scores = chunk_terms(
            queries, keys, forget[rows], base + i * CHUNK, ends
        )
        row, col, near, far = masks
        grow, shrink, edge, from_start, to_end, decay_step = factors
        q_near, k_near, q_far, k_far, q_state, k_state = parts
        state = states_ref[i * DV : (i + 1) * DV, :]
        do = dmix_ref[rows, :]
        dstate_low = dstate.astype(BF16)
        dscores = nt(do, values)
        dnear = jnp.where(near, dscores, 0.0).astype(BF16)
        dfar = jnp.where(far, dscores, 0.0).astype(BF16)
        dv = tn(scores, do) + nt(k_state, dstate_low)
        dq = nn(do, state) * from_start + nn(dnear, k_near) * grow
        dq = dq + jnp.where(row >= SPAN, nn(dfar, k_far) * edge, 0.0)
        dk = nn(values, dstate_low) * to_end + tn(dnear, q_near) * shrink
        dk = dk + jnp.where(row < SPAN, tn(dfar, q_far) * edge, 0.0)
        dall_ref[rows, :DK] = dq.astype(BF16)
        dall_ref[rows, DK : 2 * DK] = dk.astype(BF16)
        dall_ref[rows, 2 * DK : QKV] = dv.astype(BF16)
        at_end = jnp.sum(dstate * after_state.astype(F32), axis=0, keepdims=True)
        ddecay = queries * dq - keys * dk
        dforget = prefix_sums(ddecay, jnp.where(col >= row, 1.0, 0.0).astype(BF16)) + at_end
        dzeta = (dforget * slope[rows]).astype(BF16)
        sums_out_ref[HEAD_ROW : HEAD_ROW + 1, lanes_at(DV + head_at)] += jnp.sum(
            dzeta.astype(F32), axis=0, keepdims=True
        )
        dlowout = tn(lowr_ref[rows, :], dzeta)
        for k in range(2):
            sums_out_ref[LOWOUT_ROW:, lanes_at(k * (D // 2) + head_at)] += dlowout[k * 8 : (k + 1) * 8]
        dall_ref[rows, QKV:] = nt(dzeta, wb_ref[...]).astype(BF16)
        dstate = dstate * decay_step + tn(do, q_state)
        after_state = state
    dstate_out_ref[...] = dstate
    next_out_ref[...] = after_state
    dall = jnp.concatenate([dall_ref[...], dgout_ref[...]], axis=1)
    sums_out_ref[LOWIN_ROW : LOWIN_ROW + RANK, :] += tn(dall[:, QKV:QKVL], xn_ref[...])[:RANK]
    x = x_ref[...].astype(F32)
    in_scale = lax.rsqrt(jnp.mean(x * x, axis=-1, keepdims=True) + NORM_EPS)
    for j in range(SLABS):
        at = slab_at(meta, j)
        part = nt(dall, w_ref[at, :])
        sums_out_ref[IN_ROW : IN_ROW + 1, at] += jnp.sum(
            part * (x_ref[:, at].astype(F32) * in_scale), axis=0, keepdims=True
        )
        target = keep_ref if j < 2 else send_ref
        target[:, (j % 2) * SLAB : (j % 2 + 1) * SLAB] = part.astype(BF16)


def feed_grad_kernel(first_ref, second_ref, *refs):
    refs[-1][...] = tn(first_ref[...], second_ref[...]).astype(BF16)


def attn_grad_kernel(row_ref, *refs):
    here_ref, away_ref, both_ref = refs[-3:]
    start = 0
    for first_ref, second_ref in zip(refs[:-3:2], refs[1:-3:2]):
        stop = start + min(second_ref.shape[1], QKV)
        both_ref[:, start:stop] = tn(first_ref[...], second_ref[:, : stop - start])
        start = stop
    rows = here_ref.shape[1]
    row = row_ref[0]
    here_ref[0] = both_ref[pl.ds(pl.multiple_of(row * rows, rows), rows), :].astype(BF16)
    away_ref[0] = both_ref[pl.ds(pl.multiple_of((1 - row) * rows, rows), rows), :].astype(BF16)


def squares_kernel(*refs):
    feed_ref, attn_ref, squares_ref = refs[-3:]
    feed = feed_ref[...].astype(F32)
    total = jnp.sum(jnp.sum(feed * feed, axis=1, keepdims=True), axis=0, keepdims=True)
    start = 0
    for kept_ref, came_ref in zip(refs[:-3:2], refs[1:-3:2]):
        attn = kept_ref[...] + came_ref[...].astype(F32)
        attn_ref[:, start : start + attn.shape[1]] = attn
        start += attn.shape[1]
        total = total + jnp.sum(jnp.sum(attn * attn, axis=1, keepdims=True), axis=0, keepdims=True)
    squares_ref[...] = jnp.broadcast_to(total, squares_ref.shape)


def update_kernel(clip_ref, attn_ref, feed_ref, *refs):
    masters, firsts, seconds = refs[:5], refs[5:10], refs[10:15]
    outs, turned, turned_attn = refs[15:30], refs[30], refs[31]
    step = pl.program_id(0)
    width = feed_ref.shape[1] // 3

    @pl.when(step == 0)
    def _():
        turned[...] = feed_ref[...].astype(F32).T
        turned_attn[...] = attn_ref[:, MAIN:].T

    clip = clip_ref[0]

    def rows(count):
        if count == attn_ref.shape[0]:
            return slice(None)
        return pl.ds(pl.multiple_of(step * count, 8), count)

    def units(k):
        count = masters[4].shape[0]
        return turned[pl.ds(pl.multiple_of(k * width + step * count, 8), count), :]

    attn = attn_ref[rows(masters[0].shape[1]), :]
    across = masters[2].shape[0]
    grads = (
        (attn[:, :DK], attn[:, DK : 2 * DK]),
        (attn[:, 2 * DK : QKV], attn[:, QKV:MAIN]),
        (turned_attn[pl.ds(pl.multiple_of(step * across, 8), across), :],),
        (units(0), units(1)),
        (units(2),),
    )
    rates = (D, D, HEADS * DV, D, FF)
    for i in range(5):
        for k, grad in enumerate(grads[i]):
            at = k if len(grads[i]) > 1 else Ellipsis
            results = adam_step(
                masters[i][at], grad, firsts[i][at], seconds[i][at], clip, 2.0 * rates[i] ** (-0.5), WEIGHT_DECAY
            )
            for n in range(3):
                outs[n * 5 + i][at] = results[n]


def whole(array):
    zeros = (0,) * array.ndim
    return pl.BlockSpec(array.shape, lambda i, meta: zeros, pipeline_mode=pl.Buffered(1))


def fixed(shape):
    return pl.BlockSpec(shape, lambda i, meta: (0,) * len(shape))


def rows_at(rows, width, place):
    return pl.BlockSpec((rows, width), lambda i, meta: (place(i), 0))


def like(shape, dtype):
    return jax.ShapeDtypeStruct(shape, dtype)


def params():
    return pltpu.CompilerParams(vmem_limit_bytes=VMEM_LIMIT)


def run_kernel(body, meta, steps, ins, in_specs, saved, outs, out_specs, saved_like, saved_specs, name, flops):
    given = [] if saved is None else list(saved)
    aliases = {1 + len(ins) + i: len(outs) + i for i in range(len(given))}
    result = pl.pallas_call(
        functools.partial(body, len(given)),
        grid_spec=pltpu.PrefetchScalarGridSpec(
            num_scalar_prefetch=1,
            grid=(steps,),
            in_specs=list(in_specs) + [pl.BlockSpec(memory_space=pl.ANY)] * len(given),
            out_specs=list(out_specs) + list(saved_specs),
        ),
        out_shape=list(outs) + list(saved_like),
        input_output_aliases=aliases,
        compiler_params=params(),
        cost_estimate=pl.CostEstimate(flops=flops, bytes_accessed=1024, transcendentals=0),
        name=name,
    )(meta, *ins, *given)
    return list(result[: len(outs)]), list(result[len(outs) :])


def attend(piece, meta, xn, w, wo, wb, go, c, state, saved):
    tokens = xn.shape[0]
    size = tokens // PIECES
    steps = size // BLOCK
    first = piece * steps
    here = lambda i: first + i
    ins = [xn, w, wo, wb, go, c, state]
    in_specs = [rows_at(BLOCK, D, here)] + [whole(a) for a in ins[1:]]
    outs = [like((size, D), BF16), like(state.shape, F32)]
    out_specs = [rows_at(BLOCK, D, lambda i: i), fixed(state.shape)]
    widths = [
        (2 * DK + DV, BF16),
        (DV, F32),
        (LANES, BF16),
        (DK, F32),
        (DV, F32),
        (DV, BF16),
    ]
    saved_like = [like((tokens, n), d) for n, d in widths]
    saved_specs = [rows_at(BLOCK, n, here) for n, _ in widths]
    saved_like.append(like((tokens // CHUNK * DV, DK), BF16))
    saved_specs.append(rows_at(BLOCK // CHUNK * DV, DK, here))
    return run_kernel(
        functools.partial(attend_kernel, first),
        meta, steps, ins, in_specs, saved, outs, out_specs, saved_like, saved_specs,
        "attend", size * 8 * D * 1024,
    )


def feed(piece, meta, x, terms, dys, wf, g2, saved):
    tokens = x.shape[0]
    size = tokens // PIECES
    steps = size // BLOCK
    first = piece * steps
    here = lambda i: first + i
    width = wf.shape[1] // 3
    ins = [x, *terms, *dys, wf, g2]
    in_specs = (
        [rows_at(BLOCK, D, here)]
        + [rows_at(BLOCK, a.shape[1], lambda i: i) for a in terms]
        + [rows_at(BLOCK, SLAB, here), rows_at(BLOCK, SLAB, lambda i: i)] * 2
        + [whole(wf), whole(g2)]
    )
    outs = [like((size, D), BF16)]
    out_specs = [rows_at(BLOCK, D, lambda i: i)]
    widths = [
        (2 * SLAB, BF16),
        (2 * SLAB, BF16),
        (D, BF16),
        (D, BF16),
        (width, BF16),
        (2 * width, BF16),
        (D, BF16),
        (LANES, F32),
        (SLAB, F32),
    ]
    saved_like = [like((tokens, n), d) for n, d in widths]
    saved_specs = [rows_at(BLOCK, n, here) for n, _ in widths]
    return run_kernel(
        functools.partial(feed_kernel, len(terms)),
        meta, steps, ins, in_specs, saved, outs, out_specs, saved_like, saved_specs,
        "feed", size * 2 * D * width * 6,
    )


def turn_back(piece, meta, terms, rows_in, wo, g2, go, sums, saved):
    tokens = rows_in[0].shape[0]
    size = tokens // PIECES
    steps = size // BLOCK
    first = piece * steps
    here = lambda i: first + i
    ins = [*terms, *rows_in, wo, g2, go, sums]
    in_specs = (
        [rows_at(BLOCK, a.shape[1], lambda i: i) for a in terms]
        + [rows_at(BLOCK, a.shape[1], here) for a in rows_in]
        + [whole(a) for a in (wo, g2, go, sums)]
    )
    widths = [(D, BF16), (SLAB, F32), (DV, BF16), (DV, BF16)]
    return run_kernel(
        functools.partial(turn_kernel, first),
        meta, steps, ins, in_specs, saved, [like(sums.shape, F32)], [fixed(sums.shape)],
        [like((tokens, n), d) for n, d in widths], [rows_at(BLOCK, n, here) for n, _ in widths],
        "turn", int(0.01 * size * 4 * D * 1024),
    )


def back(piece, meta, rows_in, states, w, wb, carried, saved):
    tokens = rows_in[0].shape[0]
    size = tokens // PIECES
    steps = size // BLOCK
    last = (piece + 1) * steps - 1
    here = lambda i: last - i
    local = lambda i: steps - 1 - i
    ins = [*rows_in, states, w, wb, *carried]
    in_specs = (
        [rows_at(BLOCK, a.shape[1], here) for a in rows_in]
        + [rows_at(BLOCK // CHUNK * DV, DK, here)]
        + [whole(a) for a in (w, wb, *carried)]
    )
    outs = [like((size, 2 * SLAB), BF16)] * 2 + [like(a.shape, a.dtype) for a in carried]
    out_specs = [rows_at(BLOCK, 2 * SLAB, local)] * 2 + [fixed(a.shape) for a in carried]
    return run_kernel(
        functools.partial(back_kernel, last),
        meta, steps, ins, in_specs, saved, outs, out_specs,
        [like((tokens, QKVL), BF16)], [rows_at(BLOCK, QKVL, here)],
        "back", int(0.7 * size * 12 * D * 1024),
    )


def feed_grad(first, second, column, full):
    tokens, width = second.shape
    ins = [first, second] + ([] if full is None else [full])
    return pl.pallas_call(
        feed_grad_kernel,
        grid=(D // SLAB,),
        in_specs=[
            pl.BlockSpec((tokens, SLAB), lambda i: (0, i)),
            pl.BlockSpec((tokens, width), lambda i: (0, 0), pipeline_mode=pl.Buffered(1)),
        ]
        + [pl.BlockSpec(memory_space=pl.ANY)] * (len(ins) - 2),
        out_specs=pl.BlockSpec((SLAB, width), lambda i: (i, column)),
        out_shape=like((D, FEED_COLS), BF16),
        input_output_aliases={2: 0} if len(ins) > 2 else {},
        compiler_params=params(),
        cost_estimate=pl.CostEstimate(
            flops=int(1 * 4 * D * tokens * width), bytes_accessed=1024, transcendentals=0
        ),
        name="feed_grad",
    )(*ins)


def attn_grad(row, *pairs):
    tokens = pairs[0].shape[0]
    half = SLAB // 2
    width = sum(min(a.shape[1], QKV) for a in pairs[1::2])
    specs = [
        whole(a) if i % 2 else pl.BlockSpec((tokens, SLAB), lambda i, row: (0, i)) for i, a in enumerate(pairs)
    ]
    return pl.pallas_call(
        attn_grad_kernel,
        grid_spec=pltpu.PrefetchScalarGridSpec(
            num_scalar_prefetch=1,
            grid=(SLABS,),
            in_specs=specs,
            out_specs=[pl.BlockSpec((1, half, width), lambda i, row: (i, 0, 0))] * 2,
            scratch_shapes=[pltpu.VMEM((SLAB, width), F32)],
        ),
        out_shape=[like((SLABS, half, width), BF16)] * 2,
        compiler_params=params(),
        cost_estimate=pl.CostEstimate(
            flops=int(0.5 * 4 * D * tokens * width), bytes_accessed=1024, transcendentals=0
        ),
        name="attn_grad",
    )(row, *pairs)


def shard_squares(*parts):
    rows = parts[0].shape[0]
    return pl.pallas_call(
        squares_kernel,
        out_shape=(like((rows, D), F32), like((8, LANES), F32)),
        compiler_params=params(),
        name="squares",
    )(*parts)


def update(clip, attn, feed, arrays):
    rows = attn.shape[0]
    steps = 4 if rows % 32 == 0 else 1
    masters = arrays[:5]

    def cut(array):
        shape = list(array.shape)
        shape[-2] //= steps
        zeros = (0,) * (len(shape) - 2)
        return pl.BlockSpec(tuple(shape), lambda i: (*zeros, i, 0))

    return pl.pallas_call(
        update_kernel,
        grid=(steps,),
        in_specs=[pl.BlockSpec(memory_space=pltpu.SMEM)]
        + [pl.BlockSpec(a.shape, lambda i: (0, 0), pipeline_mode=pl.Buffered(1)) for a in (attn, feed)]
        + [cut(a) for a in arrays],
        out_specs=[cut(a) for a in masters] * 3,
        out_shape=[like(a.shape, F32) for a in masters] * 3,
        scratch_shapes=[pltpu.VMEM((FEED_COLS, rows), F32), pltpu.VMEM((DV, rows), F32)],
        compiler_params=params(),
        name="update",
    )(clip, attn, feed, *arrays)


def after(array, *others):
    return lax.optimization_barrier((array, *others))[0]


def swap(array, axis, bit):
    return lax.ppermute(array, axis, [(i, i ^ bit) for i in range(lax.axis_size(axis))])


def swap_core(array):
    return swap(array, "tensor", 1)


def swap_far(array):
    return swap(array, "tensor", 2)


def swap_row(array):
    return swap(array, "dp", 1)


def shift_layer(array, by):
    count = lax.axis_size("dp")
    return lax.ppermute(array, "dp", [(i, (i + 2 * by) % count) for i in range(count)])


def gather_attn(own, soon, later):
    dp_at = lax.axis_index("dp")
    found = {(0, 0): own, (1, 0): shift_layer(own, 1), (3, 0): shift_layer(own, 3), (0, 1): swap_row(own)}
    first = list(found.values())[1:]
    found[2, 0] = shift_layer(after(own, *first, *soon), 2)
    for k in (1, 3):
        found[k, 1] = swap_row(after(found[k, 0], *first))
    second = [found[2, 0], found[1, 1], found[3, 1]]
    places = jnp.stack([((dp_at - 2 * k) % (2 * SLABS)) ^ h for k, h in [*found, (2, 1)]]).astype(jnp.int32)
    sent, places, *_ = lax.optimization_barrier((found[2, 0], places, *second[1:], *later))
    found[2, 1] = swap_row(sent)
    pieces = list(found.values())
    rows = D
    return first, pl.pallas_call(
        assemble_kernel,
        in_specs=[pl.BlockSpec(memory_space=pltpu.SMEM)]
        + [pl.BlockSpec(memory_space=pltpu.VMEM)] * (2 * SLABS),
        out_shape=(like((rows, ATTN), BF16), like((rows, DV), BF16), like((LANES, DK), BF16)),
        compiler_params=params(),
        name="assemble",
    )(places, *pieces)


def gather_plain(own, soon, later):
    count, rows = lax.axis_size("dp"), own.shape[0]
    full = lax.all_gather(own, "dp", axis=0, tiled=True)
    keys = DK // count
    blocks = full.reshape(count, rows, -1)[:, :RANK, QKV + RANK : QKV + RANK + keys]
    wb = jnp.pad(blocks.transpose(1, 0, 2).reshape(RANK, DK), ((0, LANES - RANK), (0, 0)))
    return [own], (full[:, :ATTN], full[:, ATTN:], wb)


def pick(array, axis, index):
    return lax.dynamic_index_in_dim(array, index, axis, keepdims=False)


def scatter_rows(here, away, *earlier):
    came = after(swap_row(away), *earlier)
    return (here.astype(F32) + came.astype(F32)).reshape(2, 2, *here.shape[1:])


def scatter_near(total, low, *earlier):
    away = pick(total, 1, 1 - low).astype(BF16)
    return pick(total, 1, low) + after(swap(away, "dp", 2), *earlier).astype(F32)


def scatter_far(total, high, *earlier):
    away = pick(total, 0, 1 - high).astype(BF16)
    return pick(total, 0, high), after(swap(away, "dp", 4), *earlier)


def sum_terms(part, earlier, beside=(), before=(), halves=False):
    core = after(swap_core(after(part, *earlier)), *beside)
    own = []
    for start, stop in ((0, SLAB), (SLAB, 2 * SLAB)) if halves else ((0, 2 * SLAB),):
        beside = core[:, 2 * SLAB + start : 2 * SLAB + stop].astype(F32)
        own.append((part[:, start:stop].astype(F32) + beside).astype(BF16))
    far = [swap_far(after(own[0], *before))]
    if halves:
        far.append(swap_far(after(own[1], far[0])))
    return own, part, core, far


def slab_sum(keep, send, earlier):
    own = keep.astype(F32) + swap_core(send).astype(F32)
    far = swap_far(after(own[:, SLAB:].astype(BF16), earlier))
    return own[:, :SLAB] + far.astype(F32), far


def sum_everywhere(array, axes=("tensor", "dp")):
    for axis in axes:
        size = lax.axis_size(axis)
        bit = 1
        while bit < size:
            array = array + swap(array, axis, bit)
            bit *= 2
    return array


def add_rounded(array, axis, bit, *earlier):
    low = after(array.astype(BF16), *earlier)
    return low.astype(F32) + swap(low, axis, bit).astype(F32)


def adam_step(weight, gradient, first_moment, second_moment, clip_factor, learn_rate, weight_decay):
    clipped = gradient * clip_factor
    momentum = BETA_FIRST * first_moment + (1.0 - BETA_FIRST) * clipped
    variance = BETA_SECOND * second_moment + (1.0 - BETA_SECOND) * clipped * clipped
    step_size = (
        momentum
        / (1.0 - BETA_FIRST**STEP)
        / (jnp.sqrt(variance / (1.0 - BETA_SECOND**STEP)) + ADAM_EPS)
    )
    updated = weight * (1.0 - learn_rate * weight_decay) - learn_rate * step_size
    return (momentum, variance, updated)


LARGE = (0, 1, 4, 5, 6)


def body(*args):
    inputs, cotangent, doc_lengths = args[:3]
    masters, firsts, seconds = args[3:11], args[11:19], args[19:27]
    weight_qk, weight_vg, weight_lowin, weight_lowout, weight_mixout, weight_gateup, weight_down = masters[:7]
    weight_small = masters[7]
    tensor_at = lax.axis_index("tensor")
    dp_at = lax.axis_index("dp")
    layered = lax.axis_size("dp") == 2 * SLABS
    rows_here = weight_qk.shape[1]
    ranks, _, keys_here = weight_lowout.shape
    turn = lambda i, a: jnp.swapaxes(a, 1, 2) if i == 5 else a
    size = cotangent.shape[0] // PIECES
    far_cots = [swap_far(cotangent[i * size : (i + 1) * size]) for i in range(PIECES)]

    attn_pack, feed_pack = pl.pallas_call(
        pack_kernel,
        out_shape=(like((rows_here, ATTN + DV), BF16), like((rows_here, FEED_COLS), BF16)),
        compiler_params=params(),
        name="pack",
    )(
        weight_qk, weight_vg, weight_lowin.T, weight_lowout[:, 0, :], weight_mixout,
        turn(5, weight_gateup), weight_down,
    )
    doc_ends = jnp.cumsum(doc_lengths[0])
    slots = jnp.stack([tensor_at ^ o for o in ORDER])
    meta = jnp.concatenate([slots.astype(jnp.int32), doc_ends[-1:].astype(jnp.int32), doc_ends.astype(jnp.int32)])

    g1, g2 = weight_small[:D].reshape(1, D), weight_small[D : 2 * D].reshape(1, D)
    go = weight_small[2 * D : 2 * D + DV].reshape(1, DV)
    gate_bias = lax.dynamic_slice_in_dim(weight_small, 2 * D + DV + tensor_at * DK, DK).reshape(1, DK)
    x = inputs
    x_wide = x.astype(F32)
    in_scale = lax.rsqrt(jnp.mean(x_wide * x_wide, axis=-1, keepdims=True) + NORM_EPS)
    in_scale = lax.optimization_barrier(in_scale)
    xn = lax.optimization_barrier((x_wide * in_scale * g1).astype(BF16))
    arrived, (w, wo, wb) = (gather_attn if layered else gather_plain)(
        attn_pack, [in_scale], [far_cots[0], xn, meta, gate_bias]
    )
    wf = lax.all_gather(after(feed_pack, *arrived), "dp", axis=0, tiled=True)
    meta = after(meta, far_cots[-1])
    core_cot = swap_core(after(cotangent, w))
    dys = [(cotangent, far, core_cot, swap_core(after(far, w))) for far in far_cots]

    state = jnp.zeros((DV, DK), F32)
    saved = None
    terms = []
    earlier = before = []
    for piece in range(PIECES):
        (part, state), saved = attend(piece, meta, xn, w, wo, wb, go, gate_bias, state, saved)
        own, part, core, far = sum_terms(part, earlier, before=before, halves=piece < PIECES - 1)
        terms.append((part, core, far))
        earlier = far[:1]
        before = far[-1:]
        state = after(state, *own)
    kept = list(saved)
    z = kept.pop(5)
    terms = [(part, core, *far, *(swap_core(after(f, *own)) for f in far)) for part, core, far in terms]

    fed = None
    back_terms = []
    order = after(meta, *own)
    for piece in range(PIECES):
        (part,), fed = feed(piece, order, x, terms[piece], dys[piece], wf, g2, fed)
        beside = []
        if piece == PIECES - 1:
            feed_keep, feed_send, hn, dy, hidden, dgu, rhat, rs, resid = fed
            grad_feed = feed_grad(dy, hidden, 2, None)
            beside = [grad_feed]
        own, part, core, far = sum_terms(part, earlier, beside)
        (own,), (far,) = own, far
        earlier = [far]
        order = after(meta, own)
        if piece < PIECES - 1:
            back_terms.append((part, core, far, swap_core(far)))
    grad_feed = feed_grad(after(hn, own), dgu, 0, grad_feed)
    fed_own = (feed_keep.astype(F32) + swap_core(after(feed_send, own)).astype(F32)).astype(BF16)
    shard_feed = lax.psum_scatter(grad_feed, "dp", scatter_dimension=0, tiled=True)

    qkv, gout, lowr, zeta, mixed, states = kept
    turned = None
    sums = jnp.zeros((SUM_ROWS, D), F32)
    order = after(meta, grad_feed, fed_own)
    for piece in range(PIECES):
        if piece == PIECES - 1:
            back_terms.append((part, core, far, swap_core(after(far, sums))))
        (sums,), turned = turn_back(
            piece, order, back_terms[piece], (dy, rhat, rs, gout, mixed), wo, g2, go, sums, turned
        )
    dres16, dres, dgout, dmix = turned
    fed_far = swap_far(after(fed_own[:, SLAB:], far))
    row_at = (dp_at % 2 if layered else jnp.zeros_like(dp_at)).astype(jnp.int32).reshape(1)
    high, low = dp_at // 4, (dp_at // 2) % 2
    here, away = attn_grad(row_at, xn, dgout, dres16, z)
    if layered:
        early = scatter_rows(here, away)
        early_layer = scatter_near(early, low)
        early_parts = scatter_far(early_layer, high)

    carried = [jnp.zeros((DV, DK), F32), jnp.zeros((DV, DK), BF16), sums]
    backed = None
    dxn = []
    order = after(meta, away)
    for piece in reversed(range(PIECES)):
        (keep, send, *carried), backed = back(
            piece, order, (dmix, dgout, x, xn, qkv, lowr, zeta), states, w, wb, carried, backed
        )
        if layered:
            order = after(meta, early)
        dxn.insert(0, (keep, send))
    (dall,) = backed
    late_here, late_away = attn_grad(after(row_at, early_layer, fed_far) if layered else row_at, xn, dall)
    dxn_far = [fed_far]
    for piece in reversed(range(PIECES)):
        keep, send = dxn[piece]
        dxn[piece], far = slab_sum(keep, after(send, late_here), dxn_far[-1])
        dxn_far.append(far)
    if layered:
        late = scatter_rows(late_here, late_away, early_parts[1], *dxn_far[1:-1])
    else:
        late = late_here
    fed_sum = fed_own[:, :SLAB].astype(F32) + after(fed_far, late).astype(F32)
    output = (resid + fed_sum).astype(BF16)
    if layered:
        late_layer = scatter_near(late, low, output)
        parts = *scatter_far(late_layer, high, dxn_far[-1]), *early_parts
    else:
        late_layer = late_here
        grads = [jnp.stack(g, axis=1).reshape(D, -1) for g in ((late_here, late_away), (here, away))]
        kept = lax.psum_scatter(
            jnp.concatenate(grads, axis=1), "dp", scatter_dimension=0, tiled=True
        ).astype(F32)
        parts = kept, jnp.zeros(kept.shape, BF16)

    dxn = jnp.concatenate(dxn, axis=0)
    hat_here = lax.dynamic_slice_in_dim(x, tensor_at * SLAB, SLAB, 1).astype(F32) * in_scale
    scaled = dxn * lax.dynamic_slice_in_dim(g1, tensor_at * SLAB, SLAB, 1)
    row_sums = jnp.sum(scaled * hat_here, axis=-1).reshape(-1, LANES)
    row_mean = sum_everywhere(row_sums, ("tensor",)).reshape(-1, 1) / D
    input_grad = dres + in_scale * (scaled - hat_here * row_mean)

    wide = add_rounded(carried[2], "tensor", 1, late_here)
    wide = add_rounded(wide, "tensor", 2)
    for bit in (1 << i for i in range(lax.axis_size("dp").bit_length() - 1)):
        wide = add_rounded(wide, "dp", bit, late if bit == 1 else late_layer)
    small_grad = jnp.concatenate([wide[IN_ROW], wide[MID_ROW], wide[HEAD_ROW, : DV + HEADS * DK]])
    grad_lowin = lax.dynamic_slice(wide, (LOWIN_ROW, dp_at * rows_here), (RANK, rows_here)).T
    lowout = jnp.concatenate([wide[LOWOUT_ROW:, : D // 2], wide[LOWOUT_ROW:, D // 2 :]], axis=0)
    grad_lowout = lax.dynamic_slice(
        lowout, (0, tensor_at * DK + dp_at * keys_here), (RANK, keys_here)
    ).reshape(weight_lowout.shape)

    shard_attn, squares = shard_squares(*parts, shard_feed)
    square_total = sum_everywhere(squares)[0, 0]
    grad_norm = jnp.sqrt(square_total + jnp.sum(wide * wide))
    clip_factor = jnp.minimum(1.0, CLIP_NORM / (grad_norm + 1e-06))
    arrays = [turn(i, group[i]) for group in (masters, firsts, seconds) for i in LARGE]
    large = update(clip_factor.reshape(1), shard_attn, shard_feed, arrays)
    small_rate = jnp.where(
        lax.broadcasted_iota(jnp.int32, weight_small.shape, 0) < 2 * D + DV, GAIN_RATE, BIAS_RATE
    )
    steps = {}
    for k, i in enumerate(LARGE):
        steps[i] = [turn(i, a) for a in large[k::5]]
    for i, grad, rate, decay in (
        (2, grad_lowin, 2.0 * D ** (-0.5), WEIGHT_DECAY),
        (3, grad_lowout, 2.0 * RANK ** (-0.5), WEIGHT_DECAY),
        (7, small_grad, small_rate, 0.0),
    ):
        steps[i] = adam_step(masters[i], grad, firsts[i], seconds[i], clip_factor, rate, decay)
    return (output, input_grad, grad_norm.reshape(1), *(steps[i][k] for k in range(3) for i in range(8)))


def solution(mesh):
    weights = (
        P(None, "dp", "tensor"),
        P(None, "dp", "tensor"),
        P("dp", None),
        P(None, "tensor", "dp"),
        P("tensor", "dp"),
        P(None, "dp", "tensor"),
        P("tensor", "dp"),
        P(),
    )
    return jax.shard_map(
        body,
        mesh=mesh,
        in_specs=(P("dp", None), P("dp", "tensor"), P("dp", None), *weights, *weights, *weights),
        out_specs=(P("dp", "tensor"), P("dp", "tensor"), P(), *weights, *weights, *weights),
        check_vma=False,
    )
```
